32 devices in a mesh: groups: 2 (over x), seq: 16 (over z, y, core).
Axes of the slice: x: 2, y: 2, z: 4, core: 2. Of those that a mesh axis runs over, the one named last changes fastest.
Arguments:
- query_seq: bfloat16 [8192, 6144], P(('groups', 'seq')), parts along dimension 0, may hold values from -15 to 15
- key_seq: bfloat16 [8192, 6144], P(('groups', 'seq')), parts along dimension 0, may hold values from -15 to 15
- value_seq: bfloat16 [8192, 6144], P(('groups', 'seq')), parts along dimension 0, may hold values from -288 to 288
- conv_kernel: bfloat16 [3, 4, 6144], replicated, may hold values from -3 to 3
- feature_map: bfloat16 [128, 128], replicated, may hold values from -1.5 to 1.5
- norm_gain: float32 [6144], replicated, may hold values from 0.25 to 1.75
Outputs:
- attended: bfloat16 [8192, 6144], P(('groups', 'seq')), parts along dimension 0
The draws below stay inside these ranges and needn't reach their ends.
There are 2 independent parts, one for each index of `groups`. The reference program is written for one: setup_inputs(seed, part) draws one part's arguments, and reference() takes and returns one part's arrays. A program takes and returns all parts, laid end to end along the dimension named above; an argument that names none is the same for every part. Nothing has to cross between parts.
All inputs are finite; a program needn't handle non-finite values.
Results may differ from the reference program's by a relative error of at most 0.012.
The reference program's roundings to bfloat16 on the way count: a program that leaves them out, or rounds other values in their place, can miss the bound.
Values may be sent and summed in bfloat16 or wider, within the bound.
No kernel may reach another device: no remote copies, remote signals or barrier semaphores. Data moves between devices by JAX's collectives and lax.ppermute only.
A program may use at most 128 MiB of HBM per device.

```python
import math
import jax
import jax.numpy as jnp
from jax import lax

H = 48
DH = 128
D = 6144
SPAN = 256
KCONV = 4
TOKENS = 4096


def draw_value_seq(key, part):
    key_noise = jax.random.fold_in(key, 11)
    key_column = jax.random.fold_in(key, 12)
    key_row = jax.random.fold_in(key, 14)
    noise = jnp.clip(jax.random.normal(key_noise, (TOKENS, D), jnp.float32), -4.0, 4.0)
    column = jnp.exp(jax.random.uniform(key_column, (1, D), jnp.float32) * math.log(10.0))
    row_scale = jnp.exp(jax.random.uniform(key_row, (TOKENS, 1), jnp.float32) * math.log(4.0))
    base = noise * column * row_scale
    earlier = jnp.concatenate([jnp.zeros((1, D), jnp.float32), base[:-1]], axis=0)
    return (base - 0.8 * earlier).astype(jnp.bfloat16)


def draw_feature_map(key, part):
    key_sign = jax.random.fold_in(key, 21)
    key_off = jax.random.fold_in(key, 22)
    signs = (jax.random.randint(key_sign, (DH,), 0, 2) * 2 - 1).astype(jnp.float32)
    off_diag = jnp.clip(jax.random.normal(key_off, (DH, DH), jnp.float32), -4.0, 4.0) * (0.45 / math.sqrt(DH - 1))
    eye = jnp.eye(DH, dtype=jnp.float32)
    return (eye * (1.5 * signs)[None, :] + (1.0 - eye) * off_diag).astype(jnp.bfloat16)


def steps_of(own_key, shape, split, least, high):
    def one(position, blocks):
        draws = jax.random.uniform(jax.random.fold_in(jax.random.fold_in(own_key, 6), position), (blocks,), jnp.float32, least / len(split), high / len(split))
        return jnp.repeat(jnp.exp(draws), shape[position] // blocks).reshape((-1,) + (1,) * (len(shape) - position - 1))

    gain = one(*split[0])
    for cut in split[1:]:
        gain = gain * one(*cut)
    return gain


def gaussian(own_key, dims, width, most, cuts=(), kind=jnp.bfloat16):
    entries = width * jax.random.normal(own_key, dims, jnp.float32)
    if cuts:
        entries = entries * steps_of(own_key, dims, cuts, -0.22, 0.18)
    return jnp.clip(entries, -most, most).astype(kind)


def setup_inputs(seed: int = 0, part: int = 0) -> dict:
    splits = jax.random.split(jax.random.key(seed), 7)
    own_keys = jax.random.split(jax.random.fold_in(splits[6], part), 7)
    query_seq = gaussian(own_keys[0], (TOKENS, D), 3.0, 15.0, ((0, 16),))
    key_seq = gaussian(own_keys[1], (TOKENS, D), 3.0, 15.0, ((0, 16),))
    value_seq = draw_value_seq(jax.random.fold_in(jax.random.fold_in(splits[6], part), 71), part)
    conv_kernel = gaussian(splits[3], (3, KCONV, D), KCONV ** -0.5, 3.0)
    feature_map = draw_feature_map(jax.random.fold_in(splits[6], 71), part)
    norm_gain = jnp.clip(1.0 + 0.15 * jax.random.normal(splits[5], (D,), jnp.float32), 0.25, 1.75)
    return {"query_seq": query_seq, "key_seq": key_seq, "value_seq": value_seq, "conv_kernel": conv_kernel, "feature_map": feature_map, "norm_gain": norm_gain}


def short_conv(seq_rows, kernel):
    tap_count = kernel.shape[0]
    length = seq_rows.shape[0]
    padded = jnp.concatenate([jnp.zeros((tap_count - 1, seq_rows.shape[1]), seq_rows.dtype), seq_rows], axis=0)
    summed = jnp.zeros(seq_rows.shape, jnp.float32)
    for offset in range(tap_count):
        window = padded[tap_count - 1 - offset:tap_count - 1 - offset + length]
        summed = summed + kernel[offset].astype(jnp.float32) * window.astype(jnp.float32)
    return summed.astype(jnp.bfloat16)

def feature_rows(conv_rows, feature_map):
    head_rows = conv_rows.reshape(conv_rows.shape[0], H, DH).astype(jnp.float32)
    projected = jnp.einsum('thd,de->the', head_rows, feature_map.astype(jnp.float32))
    return (jax.nn.elu(projected) + 1.0).astype(jnp.bfloat16)

def reference(query_seq, key_seq, value_seq, conv_kernel, feature_map, norm_gain):
    query_conv = short_conv(query_seq, conv_kernel[0])
    key_conv = short_conv(key_seq, conv_kernel[1])
    value_conv = short_conv(value_seq, conv_kernel[2])
    block_count = TOKENS // SPAN
    query_feat = feature_rows(query_conv, feature_map).reshape(block_count, SPAN, H, DH)
    key_feat = feature_rows(key_conv, feature_map).reshape(block_count, SPAN, H, DH)
    value_heads = value_conv.reshape(block_count, SPAN, H, DH)
    causal = jnp.arange(SPAN)[:, None] >= jnp.arange(SPAN)[None, :]

    def advance(prefix, blocks):
        query_blk, key_blk, value_blk = blocks
        query_wide = query_blk.astype(jnp.float32)
        key_wide = key_blk.astype(jnp.float32)
        value_wide = value_blk.astype(jnp.float32)
        scores = jnp.einsum('ihd,jhd->hij', query_wide, key_wide)
        weights = lax.optimization_barrier(jnp.where(causal[None], scores, 0.0).astype(jnp.bfloat16))
        mixed_rows = jnp.einsum('hij,jhd->ihd', weights.astype(jnp.float32), value_wide)
        prefix_bf = lax.optimization_barrier(prefix.astype(jnp.bfloat16))
        mixed_rows = mixed_rows + jnp.einsum('ihd,hde->ihe', query_wide, prefix_bf.astype(jnp.float32))
        kv_state = jnp.einsum('jhd,jhe->hde', key_wide, value_wide)
        return (prefix + kv_state, mixed_rows)
    start_state = jnp.zeros((H, DH, DH), jnp.float32)
    _, mixed_all = lax.scan(advance, start_state, (query_feat, key_feat, value_heads))
    mixed_all = mixed_all.reshape(TOKENS, H, DH)
    inverse_rms = lax.rsqrt(lax.optimization_barrier(jnp.mean(mixed_all * mixed_all, axis=-1, keepdims=True)) + 1e-06)
    normed = (mixed_all * inverse_rms).reshape(TOKENS, D) * norm_gain
    return normed.astype(jnp.bfloat16)
```

```python
import functools

import jax
import jax.numpy as jnp
from jax import lax
from jax.experimental import pallas as pl
from jax.experimental.pallas import tpu as pltpu
from jax.sharding import PartitionSpec as P

SPAN = 256
GROUPS = 1
RIM = 16
TILE = 8
VMEM_BYTES = 40 * 1024 * 1024


def pack_kernel(tap_count, query_ref, key_ref, value_ref, rim_ref):
    taps = tap_count - 1
    row = lax.broadcasted_iota(jnp.int32, (TILE, query_ref.shape[1]), 0)
    key_tail = key_ref[...].astype(jnp.float32)[-TILE:]
    value_tail = value_ref[...].astype(jnp.float32)[-TILE:]
    query_tail = query_ref[...].astype(jnp.float32)[-TILE:]
    key_rows = pltpu.roll(key_tail, taps, 0)
    value_rows = pltpu.roll(value_tail, 2 * taps, 0)
    first = jnp.where(row < taps, key_rows, value_rows)
    rim_ref[...] = jnp.concatenate([first, query_tail], axis=0).astype(jnp.bfloat16)


def pack_rims(query_seq, key_seq, value_seq, tap_count):
    tok_count, width = query_seq.shape
    tail = pl.BlockSpec((RIM, width), lambda i: (tok_count // RIM - 1, 0))
    return pl.pallas_call(
        functools.partial(pack_kernel, tap_count),
        grid=(1,),
        in_specs=[tail] * 3,
        out_specs=pl.BlockSpec((RIM, width), lambda i: (0, 0)),
        out_shape=jax.ShapeDtypeStruct((RIM, width), jnp.bfloat16),
        name="pack_rims",
    )(query_seq, key_seq, value_seq)


def convolved(rows, taps, rim=None, rim_end=0):
    total = taps[0:1] * rows
    row = lax.broadcasted_iota(jnp.int32, (TILE, rows.shape[1]), 0)
    for offset in range(1, taps.shape[0]):
        moved = pltpu.roll(rows, offset, 0)
        before = 0.0 if rim is None else pltpu.roll(rim, (offset - rim_end) % TILE, 0)
        first = jnp.where(row < offset, before, moved[:TILE])
        moved = jnp.concatenate([first, moved[TILE:]], axis=0)
        total = total + taps[offset : offset + 1] * moved
    return total.astype(jnp.bfloat16)


def features(conv_rows, feature_map):
    projected = jnp.dot(conv_rows, feature_map, preferred_element_type=jnp.float32)
    return jnp.where(projected > 0, projected + 1.0, jnp.exp(projected)).astype(jnp.bfloat16)


def query_kernel(query_ref, taps_ref, map_ref, feat_ref):
    head_dim = map_ref.shape[0]
    for start in range(0, query_ref.shape[1], head_dim):
        cols = slice(start, start + head_dim)
        conv = convolved(query_ref[:, cols].astype(jnp.float32), taps_ref[0, :, cols].astype(jnp.float32))
        feat_ref[:, cols] = features(conv, map_ref[...])


def query_features(query_seq, conv_kernel, feature_map, step):
    tok_count, width = query_seq.shape
    tap_count = conv_kernel.shape[1]
    block = pl.BlockSpec((tok_count, step), lambda i: (0, i))
    return pl.pallas_call(
        query_kernel,
        grid=(width // step,),
        in_specs=[
            block,
            pl.BlockSpec((1, tap_count, step), lambda i: (0, 0, i)),
            pl.BlockSpec(feature_map.shape, lambda i: (0, 0)),
        ],
        out_specs=block,
        out_shape=jax.ShapeDtypeStruct(query_seq.shape, jnp.bfloat16),
        compiler_params=pltpu.CompilerParams(vmem_limit_bytes=VMEM_BYTES),
        cost_estimate=pl.CostEstimate(
            flops=2 * query_seq.size * feature_map.shape[0],
            bytes_accessed=4 * query_seq.size,
            transcendentals=query_seq.size,
        ),
        name="query_features",
    )(query_seq, conv_kernel, feature_map)


def state_kernel(places, key_ref, value_ref, rim_ref, taps_ref, map_ref, feat_ref, conv_ref, state_ref):
    head_dim = map_ref.shape[0]
    back = taps_ref.shape[1] - 1
    for head in range(key_ref.shape[1] // head_dim):
        cols = slice(head * head_dim, (head + 1) * head_dim)
        rim = rim_ref[:, cols].astype(jnp.float32)[:TILE]
        rim = jnp.where(places[0] > 0, rim, 0.0)
        taps = taps_ref[:, :, cols].astype(jnp.float32)
        key_conv = convolved(key_ref[:, cols].astype(jnp.float32), taps[1], rim, back)
        key_feat = features(key_conv, map_ref[...])
        feat_ref[:, cols] = key_feat
        value_conv = convolved(value_ref[:, cols].astype(jnp.float32), taps[2], rim, 2 * back)
        conv_ref[:, cols] = value_conv
        state = lax.dot_general(
            key_feat, value_conv, (((0,), (0,)), ((), ())), preferred_element_type=jnp.float32
        )
        state_ref[head * head_dim : (head + 1) * head_dim] = state.astype(state_ref.dtype)


def key_states(places, key_seq, value_seq, rims, conv_kernel, feature_map, group, first, state_type):
    tok_count, width = key_seq.shape
    tap_count = conv_kernel.shape[1]
    head_dim = feature_map.shape[0]
    step = width // (4 * GROUPS)

    def natural(i, places):
        return places[1 + first + i] * GROUPS + group

    block = pl.BlockSpec((tok_count, step), lambda i, places: (0, natural(i, places)))
    local = pl.BlockSpec((tok_count, step), lambda i, places: (0, i))
    return pl.pallas_call(
        state_kernel,
        grid_spec=pltpu.PrefetchScalarGridSpec(
            num_scalar_prefetch=1,
            grid=(2,),
            in_specs=[
                block,
                block,
                pl.BlockSpec((RIM, step), lambda i, places: (0, natural(i, places))),
                pl.BlockSpec((3, tap_count, step), lambda i, places: (0, 0, natural(i, places))),
                pl.BlockSpec(feature_map.shape, lambda i, places: (0, 0)),
            ],
            out_specs=[local, local, pl.BlockSpec((step, head_dim), lambda i, places: (i, 0))],
        ),
        out_shape=[
            jax.ShapeDtypeStruct((tok_count, 2 * step), jnp.bfloat16),
            jax.ShapeDtypeStruct((tok_count, 2 * step), jnp.bfloat16),
            jax.ShapeDtypeStruct((2 * step, head_dim), state_type),
        ],
        compiler_params=pltpu.CompilerParams(vmem_limit_bytes=VMEM_BYTES),
        cost_estimate=pl.CostEstimate(
            flops=8 * tok_count * step * head_dim,
            bytes_accessed=16 * tok_count * step,
            transcendentals=2 * tok_count * step,
        ),
        name="key_states",
    )(places, key_seq, value_seq, rims, conv_kernel, feature_map)


def within_kernel(
    places, query_ref, feat_ref, rim_ref, taps_ref, map_ref, key_ref, value_ref, fixed_ref, mixed_ref
):
    head_dim = map_ref.shape[0]
    tok_count = feat_ref.shape[0]
    half = tok_count // 2
    causal = lax.broadcasted_iota(jnp.int32, (half, half), 0) >= lax.broadcasted_iota(
        jnp.int32, (half, half), 1
    )
    for start in range(0, feat_ref.shape[1], head_dim):
        cols = slice(start, start + head_dim)
        rim = rim_ref[:, cols].astype(jnp.float32)[TILE:]
        rim = jnp.where(places[0] > 0, rim, 0.0)
        first = convolved(
            query_ref[:, cols].astype(jnp.float32), taps_ref[0, :, cols].astype(jnp.float32), rim, TILE
        )
        first = features(first, map_ref[...])
        feat = jnp.concatenate([first, feat_ref[RIM:, cols]], axis=0)
        fixed_ref[:, cols] = feat
        key, value = key_ref[:, cols], value_ref[:, cols]
        for at in (0, half):
            scores = lax.dot_general(
                feat[at : at + half],
                key[: at + half],
                (((1,), (1,)), ((), ())),
                preferred_element_type=jnp.float32,
            )
            masked = jnp.where(causal, scores[:, at:], 0.0).astype(jnp.bfloat16)
            if at:
                masked = jnp.concatenate([scores[:, :at].astype(jnp.bfloat16), masked], axis=1)
            mixed_ref[at : at + half, cols] = jnp.dot(
                masked, value[: at + half], preferred_element_type=jnp.float32
            )


def within_block(places, query_seq, query_feat, rims, conv_kernel, feature_map, key_feat, value_conv, group, first):
    tok_count, width = query_seq.shape
    tap_count = conv_kernel.shape[1]
    head_dim = feature_map.shape[0]
    step = width // (4 * GROUPS)

    def natural(i, places):
        return places[1 + first + i] * GROUPS + group

    local = pl.BlockSpec((tok_count, step), lambda i, places: (0, i))
    return pl.pallas_call(
        within_kernel,
        grid_spec=pltpu.PrefetchScalarGridSpec(
            num_scalar_prefetch=1,
            grid=(2,),
            in_specs=[
                pl.BlockSpec((RIM, step), lambda i, places: (0, natural(i, places))),
                pl.BlockSpec((tok_count, step), lambda i, places: (0, natural(i, places))),
                pl.BlockSpec((RIM, step), lambda i, places: (0, natural(i, places))),
                pl.BlockSpec((1, tap_count, step), lambda i, places: (0, 0, natural(i, places))),
                pl.BlockSpec(feature_map.shape, lambda i, places: (0, 0)),
                local,
                local,
            ],
            out_specs=[local, local],
        ),
        out_shape=[
            jax.ShapeDtypeStruct((tok_count, 2 * step), jnp.bfloat16),
            jax.ShapeDtypeStruct((tok_count, 2 * step), jnp.float32),
        ],
        compiler_params=pltpu.CompilerParams(vmem_limit_bytes=VMEM_BYTES),
        cost_estimate=pl.CostEstimate(
            flops=8 * tok_count * tok_count * step,
            bytes_accessed=24 * tok_count * step,
            transcendentals=0,
        ),
        name="within_block",
    )(places, query_seq, query_feat, rims, conv_kernel, feature_map, key_feat, value_conv)


def finish_kernel(places, feat_ref, mixed_ref, prefix_ref, gain_ref, *rest):
    out_ref = rest[-1]
    head_dim = prefix_ref.shape[1]
    for start in range(0, feat_ref.shape[1], head_dim):
        cols = slice(start, start + head_dim)
        mixed = mixed_ref[:, cols] + jnp.dot(
            feat_ref[:, cols], prefix_ref[cols], preferred_element_type=jnp.float32
        )
        inverse_rms = lax.rsqrt(jnp.mean(mixed * mixed, axis=-1, keepdims=True) + 1e-06)
        out_ref[:, cols] = (mixed * inverse_rms * gain_ref[:, cols]).astype(jnp.bfloat16)


def finish(places, fixed_feat, mixed, prefix, norm_gain, before, group, first, position):
    tok_count = mixed.shape[0]
    width = norm_gain.shape[1]
    step = width // (4 * GROUPS)
    head_dim = prefix.shape[1]

    def natural(i, places):
        return places[1 + position] * GROUPS + group

    local = pl.BlockSpec((tok_count, step), lambda i, places: (0, position - first))
    in_specs = [
        local,
        local,
        pl.BlockSpec((step, head_dim), lambda i, places: (0, 0)),
        pl.BlockSpec((1, step), lambda i, places: (0, natural(i, places))),
    ]
    operands = [places, fixed_feat, mixed, prefix, norm_gain]
    aliases = {}
    if before is not None:
        in_specs.append(pl.BlockSpec(memory_space=pl.ANY))
        operands.append(before)
        aliases = {5: 0}
    return pl.pallas_call(
        finish_kernel,
        grid_spec=pltpu.PrefetchScalarGridSpec(
            num_scalar_prefetch=1,
            grid=(1,),
            in_specs=in_specs,
            out_specs=pl.BlockSpec((tok_count, step), lambda i, places: (0, natural(i, places))),
        ),
        out_shape=jax.ShapeDtypeStruct((tok_count, width), jnp.bfloat16),
        input_output_aliases=aliases,
        compiler_params=pltpu.CompilerParams(vmem_limit_bytes=VMEM_BYTES),
        cost_estimate=pl.CostEstimate(
            flops=2 * tok_count * step * head_dim,
            bytes_accessed=8 * tok_count * step,
            transcendentals=tok_count * step // head_dim,
        ),
        name="finish",
    )(*operands)


def swapped(block, axis, distance):
    return lax.ppermute(block, axis, [(i, i ^ distance) for i in range(lax.axis_size(axis))])


def rotated(block, axis, distance):
    count = lax.axis_size(axis)
    return lax.ppermute(block, axis, [(i, (i + distance) % count) for i in range(count)])


def on_device(query_seq, key_seq, value_seq, conv_kernel, feature_map, norm_gain):
    tok_count, width = query_seq.shape
    tap_count = conv_kernel.shape[1]
    head_dim = feature_map.shape[0]
    step = width // (4 * GROUPS)
    assert tok_count == SPAN and step % head_dim == 0
    device_count = lax.axis_size("seq")
    device = lax.axis_index("seq")
    core, pair = device % 2, device // 2 % 2
    places = jnp.stack(
        [
            device,
            2 * (1 - core) + 1 - pair,
            2 * (1 - core) + pair,
            2 * core + 1 - pair,
            2 * core + pair,
        ]
    ).astype(jnp.int32)
    gain = norm_gain.reshape(1, width)
    f32, bf16 = jnp.float32, jnp.bfloat16

    rims = rotated(pack_rims(query_seq, key_seq, value_seq, tap_count), "seq", 1)
    query_feat = query_features(query_seq, conv_kernel, feature_map, step)

    out = None
    for group in range(GROUPS):
        states = functools.partial(
            key_states, places, key_seq, value_seq, rims, conv_kernel, feature_map, group
        )
        key_a, value_a, state_a = states(0, bf16)
        from_core = swapped(state_a, "seq", 1).astype(f32)
        key_b, value_b, state_b = states(2, f32)
        chip = state_b + from_core
        from_pair = swapped(chip[:step].astype(bf16), "seq", 2).astype(f32)
        total = chip[step:] + from_pair
        earlier = jnp.zeros_like(total)
        running = total
        distance = 4
        while distance < device_count:
            arrived = rotated(running.astype(bf16), "seq", distance).astype(f32)
            arrived = jnp.where(device >= distance, arrived, 0.0)
            earlier = earlier + arrived
            running = running + arrived
            distance *= 2
        own = earlier + jnp.where(pair == 1, from_pair, 0.0)
        others = earlier + jnp.where(pair == 0, chip[step:], 0.0)
        back = swapped(others.astype(bf16), "seq", 2).astype(f32)
        prefix_3 = (own + jnp.where(core == 1, from_core[step:], 0.0)).astype(bf16)
        give_3 = (own + jnp.where(core == 0, state_b[step:], 0.0)).astype(bf16)
        prefix_1 = swapped(give_3, "seq", 1)
        prefix_2 = (back + jnp.where(core == 1, from_core[:step], 0.0)).astype(bf16)
        give_2 = (back + jnp.where(core == 0, state_b[:step], 0.0)).astype(bf16)
        prefix_0 = swapped(give_2, "seq", 1)
        within = functools.partial(
            within_block, places, query_seq, query_feat, rims, conv_kernel, feature_map
        )
        feat_a, mixed_a = within(key_a, value_a, group, 0)
        feat_b, mixed_b = within(key_b, value_b, group, 2)
        for position, prefix in ((3, prefix_3), (1, prefix_1), (2, prefix_2), (0, prefix_0)):
            feat, mixed = (feat_a, mixed_a) if position < 2 else (feat_b, mixed_b)
            first = 0 if position < 2 else 2
            out = finish(places, feat, mixed, prefix, gain, out, group, first, position)
    return out


def solution(mesh):
    return jax.shard_map(
        on_device,
        mesh=mesh,
        in_specs=(
            P(("groups", "seq"), None),
            P(("groups", "seq"), None),
            P(("groups", "seq"), None),
            P(),
            P(),
            P(),
        ),
        out_specs=P(("groups", "seq"), None),
        check_vma=False,
    )
```

```python
import functools

import jax
import jax.numpy as jnp
from jax import lax
from jax.experimental import pallas as pl
from jax.experimental.pallas import tpu as pltpu
from jax.sharding import PartitionSpec as P

SPAN = 256
GROUPS = 1
RIM = 16
TILE = 8
VMEM_BYTES = 16 * 1024 * 1024


def in_hbm(array):
    return pltpu.with_memory_space_constraint(array, pltpu.HBM)


def pack_kernel(tap_count, query_ref, key_ref, value_ref, rim_ref):
    taps = tap_count - 1
    row = lax.broadcasted_iota(jnp.int32, (TILE, query_ref.shape[1]), 0)
    key_tail = key_ref[...].astype(jnp.float32)[-TILE:]
    value_tail = value_ref[...].astype(jnp.float32)[-TILE:]
    query_tail = query_ref[...].astype(jnp.float32)[-TILE:]
    key_rows = pltpu.roll(key_tail, taps, 0)
    value_rows = pltpu.roll(value_tail, 2 * taps, 0)
    first = jnp.where(row < taps, key_rows, value_rows)
    rim_ref[...] = jnp.concatenate([first, query_tail], axis=0).astype(jnp.bfloat16)


def pack_rims(query_seq, key_seq, value_seq, tap_count):
    tok_count, width = query_seq.shape
    tail = pl.BlockSpec((RIM, width), lambda i: (tok_count // RIM - 1, 0))
    return pl.pallas_call(
        functools.partial(pack_kernel, tap_count),
        grid=(1,),
        in_specs=[tail] * 3,
        out_specs=pl.BlockSpec((RIM, width), lambda i: (0, 0)),
        out_shape=jax.ShapeDtypeStruct((RIM, width), jnp.bfloat16),
        name="pack_rims",
    )(in_hbm(query_seq), in_hbm(key_seq), in_hbm(value_seq))


def convolved(rows, taps, rim=None, rim_end=0):
    total = taps[0:1] * rows
    row = lax.broadcasted_iota(jnp.int32, (TILE, rows.shape[1]), 0)
    for offset in range(1, taps.shape[0]):
        moved = pltpu.roll(rows, offset, 0)
        before = 0.0 if rim is None else pltpu.roll(rim, (offset - rim_end) % TILE, 0)
        first = jnp.where(row < offset, before, moved[:TILE])
        moved = jnp.concatenate([first, moved[TILE:]], axis=0)
        total = total + taps[offset : offset + 1] * moved
    return total.astype(jnp.bfloat16)


def convolved_by(scratch, rows, taps, rim=None, rim_end=0):
    length = rows.shape[0]
    if rim is None:
        scratch[:TILE] = jnp.zeros((TILE, rows.shape[1]), jnp.float32)
    else:
        scratch[:TILE] = pltpu.roll(rim, (-rim_end) % TILE, 0)
    scratch[TILE : TILE + length] = rows
    total = taps[0:1] * rows
    for offset in range(1, taps.shape[0]):
        total = total + taps[offset : offset + 1] * scratch[TILE - offset : TILE - offset + length]
    return total.astype(jnp.bfloat16)


def features(conv_rows, feature_map):
    projected = jnp.dot(conv_rows, feature_map, preferred_element_type=jnp.float32)
    return jnp.where(projected > 0, projected + 1.0, jnp.exp(projected)).astype(jnp.bfloat16)


def query_kernel(query_ref, taps_ref, map_ref, feat_ref, scratch):
    head_dim = map_ref.shape[0]
    for start in range(0, query_ref.shape[1], head_dim):
        cols = slice(start, start + head_dim)
        conv = convolved_by(
            scratch.at[start // head_dim], query_ref[:, cols].astype(jnp.float32), taps_ref[0, :, cols].astype(jnp.float32)
        )
        feat_ref[:, cols] = features(conv, map_ref[...])


def query_features(query_seq, conv_kernel, feature_map, step):
    tok_count, width = query_seq.shape
    tap_count = conv_kernel.shape[1]
    block = pl.BlockSpec((tok_count, step), lambda i: (0, i))
    return pl.pallas_call(
        query_kernel,
        grid=(width // step,),
        in_specs=[
            block,
            pl.BlockSpec((1, tap_count, step), lambda i: (0, 0, i)),
            pl.BlockSpec(feature_map.shape, lambda i: (0, 0)),
        ],
        out_specs=block,
        scratch_shapes=[pltpu.VMEM((step // feature_map.shape[0], TILE + tok_count, feature_map.shape[0]), jnp.float32)],
        out_shape=jax.ShapeDtypeStruct(query_seq.shape, jnp.bfloat16),
        compiler_params=pltpu.CompilerParams(vmem_limit_bytes=VMEM_BYTES),
        cost_estimate=pl.CostEstimate(
            flops=2 * query_seq.size * feature_map.shape[0],
            bytes_accessed=4 * query_seq.size,
            transcendentals=query_seq.size,
        ),
        name="query_features",
    )(in_hbm(query_seq), conv_kernel, feature_map)


def state_kernel(places, key_ref, value_ref, rim_ref, taps_ref, map_ref, feat_ref, conv_ref, state_ref, scratch):
    head_dim = map_ref.shape[0]
    back = taps_ref.shape[1] - 1
    for head in range(key_ref.shape[1] // head_dim):
        cols = slice(head * head_dim, (head + 1) * head_dim)
        rim = rim_ref[:, cols].astype(jnp.float32)[:TILE]
        rim = jnp.where(places[0] > 0, rim, 0.0)
        taps = taps_ref[:, :, cols].astype(jnp.float32)
        key_conv = convolved_by(scratch.at[0, head], key_ref[:, cols].astype(jnp.float32), taps[1], rim, back)
        key_feat = features(key_conv, map_ref[...])
        feat_ref[:, cols] = key_feat
        value_conv = convolved_by(scratch.at[1, head], value_ref[:, cols].astype(jnp.float32), taps[2], rim, 2 * back)
        conv_ref[:, cols] = value_conv
        state = lax.dot_general(
            key_feat, value_conv, (((0,), (0,)), ((), ())), preferred_element_type=jnp.float32
        )
        state_ref[head * head_dim : (head + 1) * head_dim] = state.astype(state_ref.dtype)


def key_states(places, key_seq, value_seq, rims, conv_kernel, feature_map, group, first, state_type):
    tok_count, width = key_seq.shape
    tap_count = conv_kernel.shape[1]
    head_dim = feature_map.shape[0]
    step = width // (4 * GROUPS)

    def natural(i, places):
        return places[1 + first + i] * GROUPS + group

    block = pl.BlockSpec((tok_count, step), lambda i, places: (0, natural(i, places)))
    local = pl.BlockSpec((tok_count, step), lambda i, places: (0, i))
    return pl.pallas_call(
        state_kernel,
        grid_spec=pltpu.PrefetchScalarGridSpec(
            num_scalar_prefetch=1,
            grid=(2,),
            in_specs=[
                block,
                block,
                pl.BlockSpec((RIM, step), lambda i, places: (0, natural(i, places))),
                pl.BlockSpec((3, tap_count, step), lambda i, places: (0, 0, natural(i, places))),
                pl.BlockSpec(feature_map.shape, lambda i, places: (0, 0)),
            ],
            out_specs=[local, local, pl.BlockSpec((step, head_dim), lambda i, places: (i, 0))],
            scratch_shapes=[pltpu.VMEM((2, step // head_dim, TILE + tok_count, head_dim), jnp.float32)],
        ),
        out_shape=[
            jax.ShapeDtypeStruct((tok_count, 2 * step), jnp.bfloat16),
            jax.ShapeDtypeStruct((tok_count, 2 * step), jnp.bfloat16),
            jax.ShapeDtypeStruct((2 * step, head_dim), state_type),
        ],
        compiler_params=pltpu.CompilerParams(vmem_limit_bytes=VMEM_BYTES),
        cost_estimate=pl.CostEstimate(
            flops=8 * tok_count * step * head_dim,
            bytes_accessed=16 * tok_count * step,
            transcendentals=2 * tok_count * step,
        ),
        name="key_states",
    )(places, in_hbm(key_seq), in_hbm(value_seq), rims, conv_kernel, feature_map)


def within_kernel(
    places, query_ref, feat_ref, rim_ref, taps_ref, map_ref, key_ref, value_ref, fixed_ref, mixed_ref
):
    head_dim = map_ref.shape[0]
    tok_count = feat_ref.shape[0]
    causal = lax.broadcasted_iota(jnp.int32, (tok_count, tok_count), 0) >= lax.broadcasted_iota(
        jnp.int32, (tok_count, tok_count), 1
    )
    for start in range(0, feat_ref.shape[1], head_dim):
        cols = slice(start, start + head_dim)
        rim = rim_ref[:, cols].astype(jnp.float32)[TILE:]
        rim = jnp.where(places[0] > 0, rim, 0.0)
        first = convolved(
            query_ref[:, cols].astype(jnp.float32), taps_ref[0, :, cols].astype(jnp.float32), rim, TILE
        )
        first = features(first, map_ref[...])
        feat = jnp.concatenate([first, feat_ref[RIM:, cols]], axis=0)
        fixed_ref[:, cols] = feat
        scores = lax.dot_general(
            feat, key_ref[:, cols], (((1,), (1,)), ((), ())), preferred_element_type=jnp.float32
        )
        weights = jnp.where(causal, scores, 0.0).astype(jnp.bfloat16)
        mixed_ref[:, cols] = jnp.dot(weights, value_ref[:, cols], preferred_element_type=jnp.float32)


def within_block(places, query_seq, query_feat, rims, conv_kernel, feature_map, key_feat, value_conv, group, first):
    tok_count, width = query_seq.shape
    tap_count = conv_kernel.shape[1]
    head_dim = feature_map.shape[0]
    step = width // (4 * GROUPS)

    def natural(i, places):
        return places[1 + first + i] * GROUPS + group

    local = pl.BlockSpec((tok_count, step), lambda i, places: (0, i))
    return pl.pallas_call(
        within_kernel,
        grid_spec=pltpu.PrefetchScalarGridSpec(
            num_scalar_prefetch=1,
            grid=(2,),
            in_specs=[
                pl.BlockSpec((RIM, step), lambda i, places: (0, natural(i, places))),
                pl.BlockSpec((tok_count, step), lambda i, places: (0, natural(i, places))),
                pl.BlockSpec((RIM, step), lambda i, places: (0, natural(i, places))),
                pl.BlockSpec((1, tap_count, step), lambda i, places: (0, 0, natural(i, places))),
                pl.BlockSpec(feature_map.shape, lambda i, places: (0, 0)),
                local,
                local,
            ],
            out_specs=[local, local],
        ),
        out_shape=[
            jax.ShapeDtypeStruct((tok_count, 2 * step), jnp.bfloat16),
            jax.ShapeDtypeStruct((tok_count, 2 * step), jnp.float32),
        ],
        compiler_params=pltpu.CompilerParams(vmem_limit_bytes=VMEM_BYTES),
        cost_estimate=pl.CostEstimate(
            flops=8 * tok_count * tok_count * step,
            bytes_accessed=24 * tok_count * step,
            transcendentals=0,
        ),
        name="within_block",
    )(places, in_hbm(query_seq), query_feat, rims, conv_kernel, feature_map, key_feat, value_conv)


def finish_kernel(places, feat_ref, mixed_ref, prefix_ref, gain_ref, *rest):
    out_ref = rest[-1]
    head_dim = prefix_ref.shape[1]
    for start in range(0, feat_ref.shape[1], head_dim):
        cols = slice(start, start + head_dim)
        mixed = mixed_ref[:, cols] + jnp.dot(
            feat_ref[:, cols], prefix_ref[cols], preferred_element_type=jnp.float32
        )
        inverse_rms = lax.rsqrt(jnp.mean(mixed * mixed, axis=-1, keepdims=True) + 1e-06)
        out_ref[:, cols] = (mixed * inverse_rms * gain_ref[:, cols]).astype(jnp.bfloat16)


def finish(places, fixed_feat, mixed, prefix, norm_gain, before, group, first, position):
    tok_count = mixed.shape[0]
    width = norm_gain.shape[1]
    step = width // (4 * GROUPS)
    head_dim = prefix.shape[1]

    def natural(i, places):
        return places[1 + position] * GROUPS + group

    local = pl.BlockSpec((tok_count, step), lambda i, places: (0, position - first))
    in_specs = [
        local,
        local,
        pl.BlockSpec((step, head_dim), lambda i, places: (0, 0)),
        pl.BlockSpec((1, step), lambda i, places: (0, natural(i, places))),
    ]
    operands = [places, fixed_feat, mixed, prefix, norm_gain]
    aliases = {}
    if before is not None:
        in_specs.append(pl.BlockSpec(memory_space=pl.ANY))
        operands.append(before)
        aliases = {5: 0}
    return pl.pallas_call(
        finish_kernel,
        grid_spec=pltpu.PrefetchScalarGridSpec(
            num_scalar_prefetch=1,
            grid=(1,),
            in_specs=in_specs,
            out_specs=pl.BlockSpec((tok_count, step), lambda i, places: (0, natural(i, places))),
        ),
        out_shape=jax.ShapeDtypeStruct((tok_count, width), jnp.bfloat16),
        input_output_aliases=aliases,
        compiler_params=pltpu.CompilerParams(vmem_limit_bytes=VMEM_BYTES),
        cost_estimate=pl.CostEstimate(
            flops=2 * tok_count * step * head_dim,
            bytes_accessed=8 * tok_count * step,
            transcendentals=tok_count * step // head_dim,
        ),
        name="finish",
    )(*operands)


def swapped(block, distance):
    return lax.ppermute(block, "seq", [(i, i ^ distance) for i in range(lax.axis_size("seq"))])


def rotated(block):
    count = lax.axis_size("seq")
    return lax.ppermute(block, "seq", [(i, (i + 1) % count) for i in range(count)])


def tied(*arrays):
    return lax.optimization_barrier(arrays)


def on_device(query_seq, key_seq, value_seq, conv_kernel, feature_map, norm_gain):
    tok_count, width = query_seq.shape
    tap_count = conv_kernel.shape[1]
    head_dim = feature_map.shape[0]
    step = width // (4 * GROUPS)
    device_count = lax.axis_size("seq")
    assert tok_count == SPAN and step % head_dim == 0 and device_count & (device_count - 1) == 0
    device = lax.axis_index("seq")
    core, pair = device & 1, (device >> 1) & 1
    places = jnp.stack(
        [
            device,
            2 * (1 - core) + 1 - pair,
            2 * (1 - core) + pair,
            2 * core + 1 - pair,
            2 * core + pair,
        ]
    ).astype(jnp.int32)
    gain = norm_gain.reshape(1, width)
    f32, bf16 = jnp.float32, jnp.bfloat16

    packed, query_seq = tied(pack_rims(query_seq, key_seq, value_seq, tap_count), query_seq)
    rims = rotated(packed)
    query_feat = query_features(query_seq, conv_kernel, feature_map, step)
    rims, query_feat = tied(rims, query_feat)

    def within(key_feat, value_conv, first):
        return within_block(
            places, query_seq, query_feat, rims, conv_kernel, feature_map, key_feat, value_conv, 0, first
        )

    states = functools.partial(key_states, places, key_seq, value_seq, rims, conv_kernel, feature_map, 0)
    key_a, value_a, state_a = states(0, bf16)
    from_core = swapped(state_a, 1)
    key_b, value_b, state_b = states(2, f32)
    from_core, key_b, value_b, state_b = tied(from_core, key_b, value_b, state_b)
    from_core = from_core.astype(f32)
    chip = state_b + from_core
    give, key_a, value_a = tied(chip[:step].astype(bf16), key_a, value_a)
    from_pair = swapped(give, 2)
    feat_a, mixed_a = within(key_a, value_a, 0)
    from_pair, feat_a, mixed_a = tied(from_pair, feat_a, mixed_a)
    from_pair = from_pair.astype(f32)
    running = chip[step:] + from_pair
    earlier = jnp.zeros_like(running)
    distance = 4
    while distance < device_count:
        upper = (device & distance) != 0
        give = running.astype(bf16)
        if distance == 4:
            give, key_b, value_b = tied(give, key_b, value_b)
            arrived = swapped(give, distance)
            feat_b, mixed_b = within(key_b, value_b, 2)
            arrived, feat_b, mixed_b = tied(arrived, feat_b, mixed_b)
        else:
            half = step // 2
            odd = (device & (distance // 2)) != 0
            mine = swapped(jnp.where(odd, give[half:], give[:half]), distance)
            other = swapped(mine, distance // 2)
            arrived = jnp.concatenate([jnp.where(odd, other, mine), jnp.where(odd, mine, other)], axis=0)
        arrived = arrived.astype(f32)
        earlier = earlier + jnp.where(upper, arrived, 0.0)
        running = running + arrived
        distance *= 2
    own = earlier + jnp.where(pair == 1, from_pair, 0.0)
    others = earlier + jnp.where(pair == 0, chip[step:], 0.0)
    back = swapped(others.astype(bf16), 2).astype(f32)
    prefix_3 = (own + jnp.where(core == 1, from_core[step:], 0.0)).astype(bf16)
    give_3 = (own + jnp.where(core == 0, state_b[step:], 0.0)).astype(bf16)
    prefix_1 = swapped(give_3, 1)
    out = None
    out = finish(places, feat_b, mixed_b, prefix_3, gain, out, 0, 2, 3)
    out = finish(places, feat_a, mixed_a, prefix_1, gain, out, 0, 0, 1)
    back, out = tied(back, out)
    prefix_2 = (back + jnp.where(core == 1, from_core[:step], 0.0)).astype(bf16)
    give_2 = (back + jnp.where(core == 0, state_b[:step], 0.0)).astype(bf16)
    prefix_0 = swapped(give_2, 1)
    out = finish(places, feat_b, mixed_b, prefix_2, gain, out, 0, 2, 2)
    prefix_0, out = tied(prefix_0, out)
    return finish(places, feat_a, mixed_a, prefix_0, gain, out, 0, 0, 0)


def solution(mesh):
    return jax.shard_map(
        on_device,
        mesh=mesh,
        in_specs=(
            P(("groups", "seq"), None),
            P(("groups", "seq"), None),
            P(("groups", "seq"), None),
            P(),
            P(),
            P(),
        ),
        out_specs=P(("groups", "seq"), None),
        check_vma=False,
    )
```

```python
import functools

import jax
import jax.numpy as jnp
from jax import lax
from jax.experimental import pallas as pl
from jax.experimental.pallas import tpu as pltpu
from jax.sharding import PartitionSpec as P

SPAN = 256
GROUPS = 2
BLOCK_HEADS = 6
RIM = 16
TILE = 8
VMEM_BYTES = 16 * 1024 * 1024
f32, bf16 = jnp.float32, jnp.bfloat16
IN_VMEM = pl.BlockSpec(memory_space=pltpu.VMEM)
IN_PLACE = pl.BlockSpec(memory_space=pl.ANY)
LIGHT = pl.CostEstimate(flops=1024, bytes_accessed=1024, transcendentals=0)


def in_hbm(array):
    return pltpu.with_memory_space_constraint(array, pltpu.HBM)


def kernel_call(body, name, in_specs, out_specs, out_shape, scratch=(), aliases=None):
    return pl.pallas_call(
        body,
        in_specs=in_specs,
        out_specs=out_specs,
        out_shape=out_shape,
        scratch_shapes=list(scratch),
        input_output_aliases=aliases or {},
        compiler_params=pltpu.CompilerParams(vmem_limit_bytes=VMEM_BYTES),
        cost_estimate=LIGHT,
        name=name,
    )


def shape(dims, kind):
    return jax.ShapeDtypeStruct(dims, kind)


def quarter_start(quarter, width):
    device = lax.axis_index("seq")
    core = (device & 1) ^ int(quarter < 2)
    pair = ((device >> 1) & 1) ^ int(quarter % 2 == 0)
    return (2 * core + pair) * (width // 4)


def columns(start, size):
    return pl.ds(pl.multiple_of(start, 128), size)


def block_heads(heads):
    return max(n for n in range(1, BLOCK_HEADS + 1) if heads % n == 0)


def pack_kernel(tap_count, query_ref, key_ref, value_ref, rim_ref, tails, sems):
    taps = tap_count - 1
    rows = pl.ds(query_ref.shape[0] - RIM, RIM)
    copies = [
        pltpu.make_async_copy(ref.at[rows], tails.at[i], sems.at[i])
        for i, ref in enumerate((key_ref, value_ref, query_ref))
    ]
    for copy in copies:
        copy.start()
    for copy in copies:
        copy.wait()
    key_tail, value_tail, query_tail = (tails[i].astype(f32)[-TILE:] for i in range(3))
    row = lax.broadcasted_iota(jnp.int32, key_tail.shape, 0)
    first = jnp.where(row < taps, pltpu.roll(key_tail, taps, 0), pltpu.roll(value_tail, 2 * taps, 0))
    rim_ref[...] = jnp.concatenate([first, query_tail], axis=0).astype(bf16)


def pack_rims(query_seq, key_seq, value_seq, tap_count):
    width = query_seq.shape[1]
    return kernel_call(
        functools.partial(pack_kernel, tap_count),
        "pack_rims",
        [IN_PLACE] * 3,
        IN_VMEM,
        shape((RIM, width), bf16),
        [pltpu.VMEM((3, RIM, width), bf16), pltpu.SemaphoreType.DMA((3,))],
    )(in_hbm(query_seq), in_hbm(key_seq), in_hbm(value_seq))


def convolved(scratch, rows, taps, rim=None, rim_end=0):
    length = rows.shape[0]
    if rim is None:
        scratch[:TILE] = jnp.zeros((TILE, rows.shape[1]), f32)
    else:
        scratch[:TILE] = pltpu.roll(rim, (-rim_end) % TILE, 0)
    scratch[TILE : TILE + length] = rows
    total = taps[0:1] * rows
    for offset in range(1, taps.shape[0]):
        total = total + taps[offset : offset + 1] * scratch[TILE - offset : TILE - offset + length]
    return total.astype(bf16)


def features(conv_rows, feature_map):
    projected = jnp.dot(conv_rows, feature_map, preferred_element_type=f32)
    return jnp.where(projected > 0, projected + 1.0, jnp.exp(projected)).astype(bf16)


def state_of(key_feat, value_conv):
    return lax.dot_general(
        key_feat, value_conv, (((0,), (0,)), ((), ())), preferred_element_type=f32
    )


def rim_rows(rim_ref, cols, start):
    rim = rim_ref[:, cols].astype(f32)[start : start + TILE]
    return jnp.where(lax.axis_index("seq") > 0, rim, 0.0)


def head_states(key, value, taps_ref, map_ref, rim_ref, natural, local, feat_ref, conv_ref, state_ref, scratch):
    head_dim = map_ref.shape[0]
    back = taps_ref.shape[1] - 1
    rim = None if rim_ref is None else rim_rows(rim_ref, natural, 0)
    key_conv = convolved(scratch.at[0], key.astype(f32), taps_ref[1, :, natural].astype(f32), rim, back)
    key_feat = features(key_conv, map_ref[...])
    feat_ref[:, local] = key_feat
    value_conv = convolved(scratch.at[1], value.astype(f32), taps_ref[2, :, natural].astype(f32), rim, 2 * back)
    conv_ref[:, local] = value_conv
    if rim is None:
        row = lax.broadcasted_iota(jnp.int32, (RIM, head_dim), 0)
        later = jnp.where(row < back, 0.0, key_feat[:RIM].astype(f32)).astype(bf16)
        key_feat = jnp.concatenate([later, key_feat[RIM:]], axis=0)
    state_ref[local] = state_of(key_feat, value_conv).astype(state_ref.dtype)


def near_states_kernel(
    key_ref, value_ref, taps_ref, map_ref,
    feat_ref, conv_ref, state_ref, key_first, value_first, key_other, value_other, key_rows, value_rows, scratch, sems,
):
    head_dim = map_ref.shape[0]
    width = key_ref.shape[1]
    quarter = width // 4
    heads = quarter // head_dim
    size = block_heads(heads) * head_dim
    count = quarter // size

    def copies(i, quarter_of, key_to, value_to):
        cols = columns(quarter_start(quarter_of + i // count, width) + i % count * size, size)
        local = pl.ds(i * size, size)
        slot = 2 * (quarter_of // 2)
        return (
            pltpu.make_async_copy(key_ref.at[:, cols], key_to.at[:, local], sems.at[slot, i]),
            pltpu.make_async_copy(value_ref.at[:, cols], value_to.at[:, local], sems.at[slot + 1, i]),
        )

    near = [copies(i, 2, key_rows, value_rows) for i in range(2 * count)]
    other = [copies(i, 0, key_other, value_other) for i in range(2 * count)]
    for pair in near + other:
        for copy in pair:
            copy.start()
    for i in range(2 * count):
        for copy in near[i]:
            copy.wait()
        natural = quarter_start(2 + i // count, width) + i % count * size
        for head in range(size // head_dim):
            start = i * size + head * head_dim
            local = slice(start, start + head_dim)
            head_states(
                key_rows[:, local], value_rows[:, local], taps_ref, map_ref, None,
                columns(natural + head * head_dim, head_dim), local,
                feat_ref, conv_ref, state_ref, scratch.at[head],
            )
    key_first[...] = key_rows[:RIM]
    value_first[...] = value_rows[:RIM]
    for pair in other:
        for copy in pair:
            copy.wait()


def near_states(key_seq, value_seq, conv_kernel, feature_map):
    tok_count, width = key_seq.shape
    head_dim = feature_map.shape[0]
    half = width // 2
    size = block_heads(half // 2 // head_dim)
    count = half // (size * head_dim)
    rows = shape((tok_count, half), bf16)
    return kernel_call(
        near_states_kernel,
        "near_states",
        [IN_PLACE, IN_PLACE, IN_VMEM, IN_VMEM],
        [IN_VMEM] * 7,
        [rows, rows, shape((half, head_dim), f32), shape((RIM, half), bf16), shape((RIM, half), bf16), rows, rows],
        [
            pltpu.VMEM((tok_count, half), bf16),
            pltpu.VMEM((tok_count, half), bf16),
            pltpu.VMEM((size, 2, TILE + tok_count, head_dim), f32),
            pltpu.SemaphoreType.DMA((4, count)),
        ],
    )(in_hbm(key_seq), in_hbm(value_seq), conv_kernel, feature_map)


def other_states_kernel(key_ref, value_ref, taps_ref, map_ref, rim_ref, feat_ref, conv_ref, state_ref, scratch):
    head_dim = map_ref.shape[0]
    half = key_ref.shape[1]
    for head in range(half // head_dim):
        local = slice(head * head_dim, (head + 1) * head_dim)
        natural = quarter_start(local.start // (half // 2), 2 * half) + local.start % (half // 2)
        head_states(
            key_ref[:, local], value_ref[:, local], taps_ref, map_ref, rim_ref,
            columns(natural, head_dim), local, feat_ref, conv_ref, state_ref, scratch.at[head % scratch.shape[0]],
        )


def other_states(key_rows, value_rows, conv_kernel, feature_map, rims):
    tok_count, half = key_rows.shape
    head_dim = feature_map.shape[0]
    rows = shape((tok_count, half), bf16)
    return kernel_call(
        other_states_kernel,
        "other_states",
        [IN_VMEM] * 5,
        [IN_VMEM] * 3,
        [rows, rows, shape((half, head_dim), bf16)],
        [pltpu.VMEM((BLOCK_HEADS, 2, TILE + tok_count, head_dim), f32)],
    )(key_rows, value_rows, conv_kernel, feature_map, rims)


def first_rows_kernel(
    key_ref, value_ref, taps_ref, map_ref, rim_ref, state_ref, feat_ref, conv_ref, sum_ref, scratch
):
    head_dim = map_ref.shape[0]
    half = key_ref.shape[1]
    back = taps_ref.shape[1] - 1
    row = lax.broadcasted_iota(jnp.int32, (RIM, head_dim), 0)
    size = block_heads(half // 2 // head_dim) * head_dim
    for start in range(0, half, size):
        local = slice(start, start + size)
        natural = columns(quarter_start(2 + start // (half // 2), 2 * half) + start % (half // 2), size)
        rim = rim_rows(rim_ref, natural, 0)
        conv = convolved(scratch.at[0], key_ref[:, local].astype(f32), taps_ref[1, :, natural].astype(f32), rim, back)
        value_conv = convolved(
            scratch.at[1], value_ref[:, local].astype(f32), taps_ref[2, :, natural].astype(f32), rim, 2 * back
        )
        conv_ref[:, local] = value_conv
        parts = [slice(at, at + head_dim) for at in range(0, size, head_dim)]
        feats = [features(conv[:, part], map_ref[...]) for part in parts]
        feat_ref[:, local] = jnp.concatenate(feats, axis=1)
        firsts = [jnp.where(row < back, feat.astype(f32), 0.0).astype(bf16) for feat in feats]
        for part, first in zip(parts, firsts):
            at = slice(start + part.start, start + part.stop)
            sum_ref[at] = state_ref[at] + state_of(first, value_conv[:, part])


def first_rows(key_first, value_first, conv_kernel, feature_map, rims, state):
    half = key_first.shape[1]
    head_dim = feature_map.shape[0]
    size = block_heads(half // 2 // head_dim) * head_dim
    rows = shape((RIM, half), bf16)
    return kernel_call(
        first_rows_kernel,
        "first_rows",
        [IN_VMEM] * 6,
        [IN_VMEM] * 3,
        [rows, rows, shape(state.shape, f32)],
        [pltpu.VMEM((2, TILE + RIM, size), f32)],
    )(key_first, value_first, conv_kernel, feature_map, rims, state)


def within_kernel(quarter, query_ref, taps_ref, map_ref, rim_ref, key_ref, value_ref, *rest):
    (*firsts, feat_ref, mixed_ref, scratch) = rest
    head_dim = map_ref.shape[0]
    tok_count, width = query_ref.shape
    causal = lax.broadcasted_iota(jnp.int32, (tok_count, tok_count), 0) >= lax.broadcasted_iota(
        jnp.int32, (tok_count, tok_count), 1
    )
    for head in range(width // 4 // head_dim):
        natural = columns(quarter_start(quarter, width) + head * head_dim, head_dim)
        local = slice(head * head_dim, (head + 1) * head_dim)
        at = quarter % 2 * (width // 4) + head * head_dim
        at = slice(at, at + head_dim)
        key, value = key_ref[:, at], value_ref[:, at]
        if firsts:
            key = jnp.concatenate([firsts[0][:, at], key[RIM:]], axis=0)
            value = jnp.concatenate([firsts[1][:, at], value[RIM:]], axis=0)
        rim = rim_rows(rim_ref, natural, TILE)
        taps = taps_ref[0, :, natural].astype(f32)
        conv = convolved(scratch.at[head % scratch.shape[0]], query_ref[:, natural].astype(f32), taps, rim, TILE)
        feat = features(conv, map_ref[...])
        feat_ref[:, local] = feat
        scores = lax.dot_general(feat, key, (((1,), (1,)), ((), ())), preferred_element_type=f32)
        weights = jnp.where(causal, scores, 0.0).astype(bf16)
        mixed_ref[:, local] = jnp.dot(weights, value, preferred_element_type=f32)


def within_block(quarter, query_seq, conv_kernel, feature_map, rims, key_feat, value_conv, firsts):
    tok_count, width = query_seq.shape
    head_dim = feature_map.shape[0]
    operands = (query_seq, conv_kernel, feature_map, rims, key_feat, value_conv, *firsts)
    return kernel_call(
        functools.partial(within_kernel, quarter),
        "within_block",
        [IN_VMEM] * len(operands),
        [IN_VMEM] * 2,
        [shape((tok_count, width // 4), bf16), shape((tok_count, width // 4), f32)],
        [pltpu.VMEM((BLOCK_HEADS, TILE + tok_count, head_dim), f32)],
    )(*operands)


def finish_kernel(pieces, gain_ref, *rest):
    count = len(pieces)
    feats, mixes, prefixes = rest[:count], rest[count : 2 * count], rest[2 * count : 3 * count]
    out_ref, rows, sems = rest[-3:]
    head_dim = prefixes[0].shape[1]
    width = out_ref.shape[1]
    copies = []
    for i, (quarter, group) in enumerate(pieces):
        size = prefixes[i].shape[0]
        natural = quarter_start(quarter, width) + group * size
        for start in range(0, size, head_dim):
            cols = slice(group * size + start, group * size + start + head_dim)
            mixed = mixes[i][:, cols] + jnp.dot(
                feats[i][:, cols], prefixes[i][start : start + head_dim], preferred_element_type=f32
            )
            inverse_rms = lax.rsqrt(jnp.mean(mixed * mixed, axis=-1, keepdims=True) + 1e-06)
            gain = gain_ref[:, columns(natural + start, head_dim)]
            rows[i, :, start : start + head_dim] = (mixed * inverse_rms * gain).astype(bf16)
        copies.append(pltpu.make_async_copy(rows.at[i], out_ref.at[:, columns(natural, size)], sems.at[i]))
        copies[-1].start()
    for copy in copies:
        copy.wait()


def finish(pieces, mixed, prefixes, norm_gain, before):
    width = norm_gain.shape[1]
    count = len(pieces)
    tok_count = mixed[pieces[0][0]][0].shape[0]
    operands = [norm_gain, *(mixed[q][0] for q, _ in pieces), *(mixed[q][1] for q, _ in pieces), *prefixes]
    in_specs = [IN_VMEM] * len(operands)
    aliases = {}
    if before is not None:
        aliases = {len(operands): 0}
        operands.append(in_hbm(before))
        in_specs.append(IN_PLACE)
    return kernel_call(
        functools.partial(finish_kernel, pieces),
        "finish",
        in_specs,
        IN_PLACE,
        pltpu.HBM((tok_count, width), bf16),
        [pltpu.VMEM((count, tok_count, prefixes[0].shape[0]), bf16), pltpu.SemaphoreType.DMA((count,))],
        aliases,
    )(*operands)


def swapped(block, distance):
    return lax.ppermute(block, "seq", [(i, i ^ distance) for i in range(lax.axis_size("seq"))])


def rotated(block):
    count = lax.axis_size("seq")
    return lax.ppermute(block, "seq", [(i, (i + 1) % count) for i in range(count)])


def tied(*arrays):
    return lax.optimization_barrier(arrays)


def mapped(name, function, outputs, *arrays):
    def body(*refs):
        values = [ref[...] for ref in refs[: len(arrays)]]
        for ref, value in zip(refs[len(arrays) :], function(lax.axis_index("seq"), *values)):
            ref[...] = value.astype(ref.dtype)

    columns = arrays[0].shape[1]
    return kernel_call(
        body,
        name,
        [IN_VMEM] * len(arrays),
        [IN_VMEM] * len(outputs),
        [shape((rows, columns), kind) for rows, kind in outputs],
    )(*arrays)


def on_device(query_seq, key_seq, value_seq, conv_kernel, feature_map, norm_gain):
    tok_count, width = query_seq.shape
    tap_count = conv_kernel.shape[1]
    head_dim = feature_map.shape[0]
    device_count = lax.axis_size("seq")
    assert tok_count == SPAN and width % (4 * GROUPS * head_dim) == 0
    assert device_count >= 4 and device_count & (device_count - 1) == 0
    groups = range(GROUPS)
    rows = width // (4 * GROUPS)
    gain = norm_gain.reshape(1, width)

    def of_core(device):
        return (device & 1) != 0

    def of_pair(device):
        return (device & 2) != 0

    packed, key_seq, value_seq = tied(
        pack_rims(query_seq, key_seq, value_seq, tap_count), key_seq, value_seq
    )
    rims = rotated(packed)
    near = near_states(key_seq, value_seq, conv_kernel, feature_map)
    rims, *near = tied(rims, *near)
    feat_b, conv_b, state_b, key_first, value_first, key_other, value_other = near
    feat_a, conv_a, state_a = other_states(key_other, value_other, conv_kernel, feature_map, rims)
    state_a, key_first = tied(state_a, key_first)
    from_core = swapped(state_a, 1)
    feat_first, conv_first, state_b = first_rows(
        key_first, value_first, conv_kernel, feature_map, rims, state_b
    )
    from_core, state_b = tied(from_core, state_b)

    mixed = {}
    fill = [2, 3, 0, 1]
    turn = [rims]

    def beside(*gives):
        if fill:
            q = fill.pop(0)
            *gives, turn[0] = tied(*gives, turn[0])
            operands = (feat_b, conv_b, (feat_first, conv_first)) if q >= 2 else (feat_a, conv_a, ())
            mixed[q] = within_block(q, query_seq, conv_kernel, feature_map, turn[0], *operands)
        return gives

    def after(arrived):
        names = list(mixed)
        arrived, turn[0], *done = tied(arrived, turn[0], *(mixed[q][0] for q in names))
        for q, feat in zip(names, done):
            mixed[q] = (feat, mixed[q][1])
        return arrived

    def chip_sums(device, state, arrived):
        for g in groups:
            here = slice(g * rows, (g + 1) * rows)
            yield state[here] + arrived[here].astype(f32)
        for g in groups:
            here = slice((GROUPS + g) * rows, (GROUPS + g + 1) * rows)
            yield state[here] + arrived[here].astype(f32)

    sums = mapped(
        "chip_sums", chip_sums, [(rows, bf16)] * GROUPS + [(rows, f32)] * GROUPS, state_b, from_core
    )
    gives, chip = beside(*sums[:GROUPS]), sums[GROUPS:]
    arriving = [swapped(give, 2) for give in gives]
    running, earlier, from_pair = [None] * GROUPS, [None] * GROUPS, [None] * GROUPS

    def pair_sums(device, own, arrived):
        total = own + arrived.astype(f32)
        return total, total

    def plane_sums(distance, device, total, before, *arrived):
        upper = (device & distance) != 0
        if len(arrived) == 2:
            odd = (device & (distance // 2)) != 0
            mine, other = arrived
            arrived = (jnp.concatenate([jnp.where(odd, other, mine), jnp.where(odd, mine, other)], axis=0),)
        arrived = arrived[0].astype(f32)
        before = before + jnp.where(upper, arrived, 0.0)
        total = total + arrived
        give = total.astype(bf16)
        return total, before, jnp.where(upper, give[rows // 2 :], give[: rows // 2])

    distance = 4
    for g in groups:
        from_pair[g] = after(arriving[g])
        running[g], give = mapped("pair_sums", pair_sums, [(rows, f32), (rows, bf16)], chip[g], from_pair[g])
        earlier[g] = jnp.zeros((rows, head_dim), f32)
        if distance < device_count:
            (give,) = beside(give)
            arriving[g] = (swapped(give, distance),)
    while distance < device_count:
        for g in groups:
            arrived = [after(part) for part in arriving[g]]
            running[g], earlier[g], give = mapped(
                "plane_sums",
                functools.partial(plane_sums, distance),
                [(rows, f32), (rows, f32), (rows // 2, bf16)],
                running[g],
                earlier[g],
                *arrived,
            )
            if 2 * distance < device_count:
                (give,) = beside(give)
                arriving[g] = swapped(give, 2 * distance)
        if 2 * distance < device_count:
            mine = [after(arriving[g]) for g in groups]
            arriving = [(half, swapped(half, distance)) for half in mine]
        distance *= 2
    while fill:
        beside()

    def own_prefixes(g, device, before, own, paired, cored, state):
        own_part = before + jnp.where(of_pair(device), paired.astype(f32), 0.0)
        others = before + jnp.where(of_pair(device), 0.0, own)
        here = slice((GROUPS + g) * rows, (GROUPS + g + 1) * rows)
        return (
            others,
            own_part + jnp.where(of_core(device), cored[here].astype(f32), 0.0),
            own_part + jnp.where(of_core(device), 0.0, state[here]),
        )

    def paired_prefixes(g, device, arrived, cored, state):
        arrived = arrived.astype(f32)
        here = slice(g * rows, (g + 1) * rows)
        return (
            arrived + jnp.where(of_core(device), cored[here].astype(f32), 0.0),
            arrived + jnp.where(of_core(device), 0.0, state[here]),
        )

    back, prefix_own, prefix_core = [], [], []
    for g in groups:
        others, own, cored = mapped(
            "own_prefixes",
            functools.partial(own_prefixes, g),
            [(rows, bf16)] * 3,
            earlier[g],
            chip[g],
            from_pair[g],
            from_core,
            state_b,
        )
        back.append(others)
        prefix_own.append(own)
        prefix_core.append(cored)
    *back, gain = tied(*back, gain)
    back = [swapped(give, 2) for give in back]
    prefix_core = [swapped(give, 1) for give in prefix_core]
    pieces = [(q, g) for g in groups for q in (3, 1)]
    prefixes = [(prefix_own if q == 3 else prefix_core)[g] for q, g in pieces]
    out = finish(pieces, mixed, prefixes, gain, None)
    for g in groups:
        arrived, out = tied(back[g], out)
        prefix_2, prefix_0 = mapped(
            "paired_prefixes",
            functools.partial(paired_prefixes, g),
            [(rows, bf16)] * 2,
            arrived,
            from_core,
            state_b,
        )
        prefix_0, prefix_2 = tied(prefix_0, prefix_2)
        prefix_0 = swapped(prefix_0, 1)
        out = finish([(2, g)], mixed, [prefix_2], gain, out)
        prefix_0, out = tied(prefix_0, out)
        out = finish([(0, g)], mixed, [prefix_0], gain, out)
    return out


def solution(mesh):
    return jax.shard_map(
        on_device,
        mesh=mesh,
        in_specs=(
            P(("groups", "seq"), None),
            P(("groups", "seq"), None),
            P(("groups", "seq"), None),
            P(),
            P(),
            P(),
        ),
        out_specs=P(("groups", "seq"), None),
        check_vma=False,
    )
```

```python
import functools

import jax
import jax.numpy as jnp
from jax import lax
from jax.experimental import pallas as pl
from jax.experimental.pallas import tpu as pltpu
from jax.sharding import PartitionSpec as P

SPAN = 256
GROUPS = 2
BLOCK_HEADS = 6
RIM = 16
TILE = 8
VMEM_BYTES = 12 * 1024 * 1024
f32, bf16 = jnp.float32, jnp.bfloat16
IN_VMEM = pl.BlockSpec(memory_space=pltpu.VMEM)
IN_PLACE = pl.BlockSpec(memory_space=pl.ANY)
LIGHT = pl.CostEstimate(flops=1024, bytes_accessed=1024, transcendentals=0)


def in_hbm(array):
    return pltpu.with_memory_space_constraint(array, pltpu.HBM)


class Turn:
    last = ()


def kernel_call(body, name, in_specs, out_specs, out_shape, scratch=(), aliases=None):
    count = len(in_specs)

    def call(*operands):
        before = Turn.last

        def ordered(*refs):
            body(*refs[:count], *refs[count + len(before) :])

        results = pl.pallas_call(
            ordered,
            in_specs=[*in_specs, *[IN_PLACE] * len(before)],
            out_specs=out_specs,
            out_shape=out_shape,
            scratch_shapes=list(scratch),
            input_output_aliases=aliases or {},
            compiler_params=pltpu.CompilerParams(vmem_limit_bytes=VMEM_BYTES),
            cost_estimate=LIGHT,
            name=name,
        )(*operands, *before)
        Turn.last = (results[-1] if isinstance(results, (list, tuple)) else results,)
        return results

    return call


def shape(dims, kind):
    return jax.ShapeDtypeStruct(dims, kind)


def quarter_start(quarter, width):
    device = lax.axis_index("seq")
    core = (device & 1) ^ int(quarter < 2)
    pair = ((device >> 1) & 1) ^ int(quarter % 2 == 0)
    return (2 * core + pair) * (width // 4)


def columns(start, size):
    return pl.ds(pl.multiple_of(start, 128), size)


def block_heads(heads):
    return max(n for n in range(1, BLOCK_HEADS + 1) if heads % n == 0)


def pack_kernel(tap_count, query_ref, key_ref, value_ref, rim_ref, tails, sems):
    taps = tap_count - 1
    rows = pl.ds(query_ref.shape[0] - RIM, RIM)
    copies = [
        pltpu.make_async_copy(ref.at[rows], tails.at[i], sems.at[i])
        for i, ref in enumerate((key_ref, value_ref, query_ref))
    ]
    for copy in copies:
        copy.start()
    for copy in copies:
        copy.wait()
    key_tail, value_tail, query_tail = (tails[i].astype(f32)[-TILE:] for i in range(3))
    row = lax.broadcasted_iota(jnp.int32, key_tail.shape, 0)
    first = jnp.where(row < taps, pltpu.roll(key_tail, taps, 0), pltpu.roll(value_tail, 2 * taps, 0))
    rim_ref[...] = jnp.concatenate([first, query_tail], axis=0).astype(bf16)


def pack_rims(query_seq, key_seq, value_seq, tap_count):
    width = query_seq.shape[1]
    return kernel_call(
        functools.partial(pack_kernel, tap_count),
        "pack_rims",
        [IN_PLACE] * 3,
        IN_VMEM,
        shape((RIM, width), bf16),
        [pltpu.VMEM((3, RIM, width), bf16), pltpu.SemaphoreType.DMA((3,))],
    )(in_hbm(query_seq), in_hbm(key_seq), in_hbm(value_seq))


def convolved(scratch, rows, taps, rim=None, rim_end=0):
    length = rows.shape[0]
    if rim is None:
        scratch[:TILE] = jnp.zeros((TILE, rows.shape[1]), f32)
    else:
        scratch[:TILE] = pltpu.roll(rim, (-rim_end) % TILE, 0)
    scratch[TILE : TILE + length] = rows
    total = taps[0:1] * rows
    for offset in range(1, taps.shape[0]):
        total = total + taps[offset : offset + 1] * scratch[TILE - offset : TILE - offset + length]
    return total.astype(bf16)


def features(conv_rows, feature_map):
    projected = jnp.dot(conv_rows, feature_map, preferred_element_type=f32)
    return jnp.where(projected > 0, projected + 1.0, jnp.exp(projected)).astype(bf16)


def state_of(key_feat, value_conv):
    return lax.dot_general(
        key_feat, value_conv, (((0,), (0,)), ((), ())), preferred_element_type=f32
    )


def rim_rows(rim_ref, cols, start):
    rim = rim_ref[:, cols].astype(f32)[start : start + TILE]
    return jnp.where(lax.axis_index("seq") > 0, rim, 0.0)


def near_states_kernel(
    group, key_ref, value_ref, taps_ref, map_ref, feat_ref, conv_ref, state_ref, key_first, value_first, scratch
):
    head_dim = map_ref.shape[0]
    width = key_ref.shape[1]
    size = width // (4 * GROUPS)
    back = taps_ref.shape[1] - 1
    row = lax.broadcasted_iota(jnp.int32, (RIM, head_dim), 0)
    for quarter in range(4):
        for start in range(0, size, head_dim):
            natural = columns(quarter_start(quarter, width) + group * size + start, head_dim)
            at = quarter * size + start
            local = slice(at, at + head_dim)
            buffers = scratch.at[at // head_dim % scratch.shape[0]]
            key, value = key_ref[:, natural], value_ref[:, natural]
            key_first[:, local] = key[:RIM]
            value_first[:, local] = value[:RIM]
            key_conv = convolved(buffers.at[0], key.astype(f32), taps_ref[1, :, natural].astype(f32))
            key_feat = features(key_conv, map_ref[...])
            feat_ref[:, local] = key_feat
            value_conv = convolved(buffers.at[1], value.astype(f32), taps_ref[2, :, natural].astype(f32))
            conv_ref[:, local] = value_conv
            later = jnp.where(row < back, 0.0, key_feat[:RIM].astype(f32)).astype(bf16)
            key_feat = jnp.concatenate([later, key_feat[RIM:]], axis=0)
            state_ref[local] = state_of(key_feat, value_conv)


def near_states(group, key_seq, value_seq, conv_kernel, feature_map):
    tok_count, width = key_seq.shape
    head_dim = feature_map.shape[0]
    size = width // GROUPS
    rows, firsts = shape((tok_count, size), bf16), shape((RIM, size), bf16)
    return kernel_call(
        functools.partial(near_states_kernel, group),
        "near_states",
        [IN_VMEM] * 4,
        [IN_VMEM] * 5,
        [rows, rows, shape((size, head_dim), f32), firsts, firsts],
        [pltpu.VMEM((BLOCK_HEADS, 2, TILE + tok_count, head_dim), f32)],
    )(key_seq, value_seq, conv_kernel, feature_map)


def first_rows_kernel(
    group, quarters, key_ref, value_ref, taps_ref, map_ref, rim_ref, state_ref,
    feat_ref, conv_ref, sum_ref, scratch,
):
    head_dim = map_ref.shape[0]
    width = taps_ref.shape[2]
    back = taps_ref.shape[1] - 1
    row = lax.broadcasted_iota(jnp.int32, (RIM, head_dim), 0)
    size = width // (4 * GROUPS)
    for i, quarter in enumerate(quarters):
        there = slice(quarter * size, (quarter + 1) * size)
        natural = columns(quarter_start(quarter, width) + group * size, size)
        rim = rim_rows(rim_ref, natural, 0)
        conv = convolved(
            scratch.at[i, 0], key_ref[:, there].astype(f32), taps_ref[1, :, natural].astype(f32), rim, back
        )
        value_conv = convolved(
            scratch.at[i, 1], value_ref[:, there].astype(f32), taps_ref[2, :, natural].astype(f32), rim, 2 * back
        )
        conv_ref[:, i * size : (i + 1) * size] = value_conv
        parts = [slice(at, at + head_dim) for at in range(0, size, head_dim)]
        feats = [features(conv[:, part], map_ref[...]) for part in parts]
        feat_ref[:, i * size : (i + 1) * size] = jnp.concatenate(feats, axis=1)
        firsts = [jnp.where(row < back, feat.astype(f32), 0.0).astype(bf16) for feat in feats]
        for part, first in zip(parts, firsts):
            state = state_ref[there.start + part.start : there.start + part.stop]
            state = state + state_of(first, value_conv[:, part])
            sum_ref[i * size + part.start : i * size + part.stop] = state.astype(sum_ref.dtype)


def first_rows(group, quarters, state_type, key_first, value_first, conv_kernel, feature_map, rims, state):
    width = conv_kernel.shape[2]
    head_dim = feature_map.shape[0]
    size = width // (4 * GROUPS)
    rows = shape((RIM, len(quarters) * size), bf16)
    return kernel_call(
        functools.partial(first_rows_kernel, group, quarters),
        "first_rows",
        [IN_VMEM] * 6,
        [IN_VMEM] * 3,
        [rows, rows, shape((len(quarters) * size, head_dim), state_type)],
        [pltpu.VMEM((len(quarters), 2, TILE + RIM, size), f32)],
    )(key_first, value_first, conv_kernel, feature_map, rims, state)


def within_kernel(
    quarter, group, query_ref, taps_ref, map_ref, rim_ref, key_ref, value_ref, key_first, value_first,
    feat_ref, mixed_ref, scratch,
):
    head_dim = map_ref.shape[0]
    tok_count, width = query_ref.shape
    size = width // (4 * GROUPS)
    causal = lax.broadcasted_iota(jnp.int32, (tok_count, tok_count), 0) >= lax.broadcasted_iota(
        jnp.int32, (tok_count, tok_count), 1
    )
    for start in range(0, size, head_dim):
        natural = columns(quarter_start(quarter, width) + group * size + start, head_dim)
        local = slice(start, start + head_dim)
        at = slice(quarter * size + start, quarter * size + start + head_dim)
        first = slice(quarter % 2 * size + start, quarter % 2 * size + start + head_dim)
        key = jnp.concatenate([key_first[:, first], key_ref[RIM:, at]], axis=0)
        value = jnp.concatenate([value_first[:, first], value_ref[RIM:, at]], axis=0)
        rim = rim_rows(rim_ref, natural, TILE)
        taps = taps_ref[0, :, natural].astype(f32)
        buffer = scratch.at[start // head_dim % scratch.shape[0]]
        conv = convolved(buffer, query_ref[:, natural].astype(f32), taps, rim, TILE)
        feat = features(conv, map_ref[...])
        feat_ref[:, local] = feat
        scores = lax.dot_general(feat, key, (((1,), (1,)), ((), ())), preferred_element_type=f32)
        weights = jnp.where(causal, scores, 0.0).astype(bf16)
        mixed_ref[:, local] = jnp.dot(weights, value, preferred_element_type=f32)


def within_block(quarter, group, query_seq, conv_kernel, feature_map, rims, feat, conv, firsts):
    tok_count, width = query_seq.shape
    head_dim = feature_map.shape[0]
    size = width // (4 * GROUPS)
    operands = (query_seq, conv_kernel, feature_map, rims, feat, conv, *firsts)
    return kernel_call(
        functools.partial(within_kernel, quarter, group),
        "within_block",
        [IN_VMEM] * len(operands),
        [IN_VMEM] * 2,
        [shape((tok_count, size), bf16), shape((tok_count, size), f32)],
        [pltpu.VMEM((BLOCK_HEADS, TILE + tok_count, head_dim), f32)],
    )(*operands)


def finish_kernel(pieces, gain_ref, *rest):
    count = sum(len(part) for part in pieces)
    prefixes, rest = rest[: len(pieces)], rest[len(pieces) :]
    feats, mixes = rest[:count], rest[count : 2 * count]
    out_ref, token_ref, rows, sems = rest[-4:]
    token_ref[...] = jnp.zeros(token_ref.shape, f32)
    head_dim = prefixes[0].shape[1]
    tok_count, size = feats[0].shape
    copies = []
    for prefix_ref, part in zip(prefixes, pieces):
        for at, (quarter, group) in enumerate(part):
            i = len(copies)
            natural = quarter_start(quarter, out_ref.shape[1]) + group * size
            for start in range(0, size, head_dim):
                cols = slice(start, start + head_dim)
                prefix = prefix_ref[at * size + start : at * size + start + head_dim]
                mixed = mixes[i][:, cols] + jnp.dot(feats[i][:, cols], prefix, preferred_element_type=f32)
                inverse_rms = lax.rsqrt(jnp.mean(mixed * mixed, axis=-1, keepdims=True) + 1e-06)
                gain = gain_ref[:, columns(natural + start, head_dim)]
                rows[i, :, cols] = (mixed * inverse_rms * gain).astype(bf16)
            copies.append(pltpu.make_async_copy(rows.at[i], out_ref.at[:, columns(natural, size)], sems.at[i]))
            copies[-1].start()
    for copy in copies:
        copy.wait()


def finish(pieces, mixed, prefixes, norm_gain, before):
    width = norm_gain.shape[1]
    every = [piece for part in pieces for piece in part]
    count = len(every)
    tok_count, size = mixed[every[0]][0].shape
    operands = [norm_gain, *prefixes, *(mixed[p][0] for p in every), *(mixed[p][1] for p in every)]
    in_specs = [IN_VMEM] * len(operands)
    aliases = {}
    if before is not None:
        aliases = {len(operands): 0}
        operands.append(in_hbm(before))
        in_specs.append(IN_PLACE)
    return kernel_call(
        functools.partial(finish_kernel, pieces),
        "finish",
        in_specs,
        [IN_PLACE, IN_VMEM],
        [pltpu.HBM((tok_count, width), bf16), shape((TILE, 128), f32)],
        [pltpu.VMEM((count, tok_count, size), bf16), pltpu.SemaphoreType.DMA((count,))],
        aliases,
    )(*operands)[0]


def swapped(block, distance):
    return lax.ppermute(block, "seq", [(i, i ^ distance) for i in range(lax.axis_size("seq"))])


def rotated(block):
    count = lax.axis_size("seq")
    return lax.ppermute(block, "seq", [(i, (i + 1) % count) for i in range(count)])


def mapped(name, function, outputs, *arrays):
    def body(*refs):
        values = [ref[...] for ref in refs[: len(arrays)]]
        for ref, value in zip(refs[len(arrays) :], function(lax.axis_index("seq"), *values)):
            ref[...] = value.astype(ref.dtype)

    columns = arrays[0].shape[1]
    return kernel_call(
        body,
        name,
        [IN_VMEM] * len(arrays),
        [IN_VMEM] * len(outputs),
        [shape((rows, columns), kind) for rows, kind in outputs],
    )(*arrays)


def on_device(query_seq, key_seq, value_seq, conv_kernel, feature_map, norm_gain):
    tok_count, width = query_seq.shape
    tap_count = conv_kernel.shape[1]
    head_dim = feature_map.shape[0]
    device_count = lax.axis_size("seq")
    assert tok_count == SPAN and width % (4 * GROUPS * head_dim) == 0
    assert device_count >= 8 and device_count & (device_count - 1) == 0
    groups = range(GROUPS)
    rows = width // (4 * GROUPS)
    gain = norm_gain.reshape(1, width)

    def of_core(device):
        return (device & 1) != 0

    def of_pair(device):
        return (device & 2) != 0

    Turn.last = ()
    rims = rotated(pack_rims(query_seq, key_seq, value_seq, tap_count))
    near = [near_states(g, key_seq, value_seq, conv_kernel, feature_map) for g in groups]
    firsts, from_core = [], []
    for g in groups:
        *first, state_a = first_rows(
            g, (0, 1), bf16, *near[g][3:], conv_kernel, feature_map, rims, near[g][2]
        )
        firsts.append([first])
        from_core.append(swapped(state_a, 1))
    for g in groups:
        firsts[g].append(
            first_rows(g, (2, 3), f32, *near[g][3:], conv_kernel, feature_map, rims, near[g][2])
        )
    state_b = [first[1][2] for first in firsts]

    mixed = {}
    fill = [(q, g) for q in (3, 2, 1, 0) for g in groups]
    total = len(fill)

    def score(share):
        while fill and total - len(fill) < round(share * total):
            q, g = fill.pop(0)
            mixed[q, g] = within_block(
                q, g, query_seq, conv_kernel, feature_map, rims, *near[g][:2], firsts[g][q // 2][:2]
            )

    def chip_sums(device, state, arrived):
        return (
            state[:rows] + arrived[:rows].astype(f32),
            state[rows:] + arrived[rows:].astype(f32),
        )

    def pair_sums(device, own, arrived):
        total = own + arrived.astype(f32)
        return total, total

    def plane_sums(distance, device, total, *arrived):
        before, arrived = (0.0, arrived) if distance == 4 else (arrived[0], arrived[1:])
        upper = (device & distance) != 0
        if len(arrived) == 2:
            odd = (device & (distance // 2)) != 0
            mine, other = arrived
            arrived = (jnp.concatenate([jnp.where(odd, other, mine), jnp.where(odd, mine, other)], axis=0),)
        arrived = arrived[0].astype(f32)
        before = before + jnp.where(upper, arrived, 0.0)
        total = total + arrived
        give = total.astype(bf16)
        return total, before, jnp.where(upper, give[rows // 2 :], give[: rows // 2])

    def own_prefixes(distance, device, own, paired, cored, state, *step):
        before = plane_sums(distance, device, *step)[1] if step else jnp.zeros((rows, head_dim), f32)
        own_part = before + jnp.where(of_pair(device), paired.astype(f32), 0.0)
        others = before + jnp.where(of_pair(device), 0.0, own)
        return (
            others,
            own_part + jnp.where(of_core(device), cored[rows:].astype(f32), 0.0),
            own_part + jnp.where(of_core(device), 0.0, state[rows:]),
        )

    def paired_prefixes(device, arrived, cored, state, own):
        arrived = arrived.astype(f32)
        give = arrived + jnp.where(of_core(device), 0.0, state[:rows])
        return (
            arrived + jnp.where(of_core(device), cored[:rows].astype(f32), 0.0),
            jnp.concatenate([give.astype(bf16), own], axis=0),
        )

    chip, arriving = [None] * GROUPS, [None] * GROUPS
    for g in groups:
        give, chip[g] = mapped(
            "chip_sums", chip_sums, [(rows, bf16), (rows, f32)], state_b[g], from_core[g]
        )
        arriving[g] = swapped(give, 2)
    running, earlier, from_pair = [None] * GROUPS, [None] * GROUPS, [None] * GROUPS
    distance = 4
    score(0.375)
    for g in groups:
        from_pair[g] = arriving[g]
        if distance < device_count:
            running[g], give = mapped("pair_sums", pair_sums, [(rows, f32), (rows, bf16)], chip[g], from_pair[g])
            arriving[g] = (swapped(give, distance),)
            if g == 0:
                score(0.625)
    while 2 * distance < device_count:
        for g in groups:
            before = [] if distance == 4 else [earlier[g]]
            running[g], earlier[g], give = mapped(
                "plane_sums",
                functools.partial(plane_sums, distance),
                [(rows, f32), (rows, f32), (rows // 2, bf16)],
                running[g],
                *before,
                *arriving[g],
            )
            arriving[g] = swapped(give, 2 * distance)
            if g == 0:
                score(0.875)
        arriving = [(mine, swapped(mine, distance)) for mine in arriving]
        distance *= 2
    score(1)

    back, own_give = [None] * GROUPS, [None] * GROUPS
    out = None
    for g in groups:
        step = ()
        if distance < device_count:
            step = (running[g], *([] if distance == 4 else [earlier[g]]), *arriving[g])
        others, own, own_give[g] = mapped(
            "own_prefixes",
            functools.partial(own_prefixes, distance),
            [(rows, bf16)] * 3,
            chip[g],
            from_pair[g],
            from_core[g],
            state_b[g],
            *step,
        )
        back[g] = swapped(others, 2)
        out = finish([[(3, g)]], mixed, [own], gain, out)
    from_other = [None] * GROUPS
    for g in groups:
        prefix_2, give = mapped(
            "paired_prefixes",
            paired_prefixes,
            [(rows, bf16), (2 * rows, bf16)],
            back[g],
            from_core[g],
            state_b[g],
            own_give[g],
        )
        from_other[g] = swapped(give, 1)
        if g == 0:
            out = finish([[(2, g)]], mixed, [prefix_2], gain, out)
        else:
            pieces = [[(2, g)], [(0, g - 1), (1, g - 1)]]
            out = finish(pieces, mixed, [prefix_2, from_other[g - 1]], gain, out)
    return finish([[(0, g), (1, g)]], mixed, [from_other[g]], gain, out)


def solution(mesh):
    return jax.shard_map(
        on_device,
        mesh=mesh,
        in_specs=(
            P(("groups", "seq"), None),
            P(("groups", "seq"), None),
            P(("groups", "seq"), None),
            P(),
            P(),
            P(),
        ),
        out_specs=P(("groups", "seq"), None),
        check_vma=False,
    )
```

```python
import functools

import jax
import jax.numpy as jnp
from jax import lax
from jax.experimental import pallas as pl
from jax.experimental.pallas import tpu as pltpu
from jax.sharding import PartitionSpec as P

SPAN = 256
GROUPS = 2
BLOCK_HEADS = 6
RIM = 16
TILE = 8
VMEM_BYTES = 12 * 1024 * 1024
f32, bf16 = jnp.float32, jnp.bfloat16
IN_VMEM = pl.BlockSpec(memory_space=pltpu.VMEM)
IN_PLACE = pl.BlockSpec(memory_space=pl.ANY)
LIGHT = pl.CostEstimate(flops=1024, bytes_accessed=1024, transcendentals=0)


def in_hbm(array):
    return pltpu.with_memory_space_constraint(array, pltpu.HBM)


class Turn:
    last = ()


def kernel_call(body, name, in_specs, out_specs, out_shape, scratch=(), aliases=None):
    count = len(in_specs)

    def call(*operands):
        before = Turn.last

        def ordered(*refs):
            body(*refs[:count], *refs[count + len(before) :])

        results = pl.pallas_call(
            ordered,
            in_specs=[*in_specs, *[IN_PLACE] * len(before)],
            out_specs=out_specs,
            out_shape=out_shape,
            scratch_shapes=list(scratch),
            input_output_aliases=aliases or {},
            compiler_params=pltpu.CompilerParams(vmem_limit_bytes=VMEM_BYTES),
            cost_estimate=LIGHT,
            name=name,
        )(*operands, *before)
        Turn.last = (results[-1] if isinstance(results, (list, tuple)) else results,)
        return results

    return call


def shape(dims, kind):
    return jax.ShapeDtypeStruct(dims, kind)


def quarter_start(quarter, width):
    device = lax.axis_index("seq")
    core = (device & 1) ^ int(quarter < 2)
    pair = ((device >> 1) & 1) ^ int(quarter % 2 == 0)
    return (2 * core + pair) * (width // 4)


def columns(start, size):
    return pl.ds(pl.multiple_of(start, 128), size)


def block_heads(heads):
    return max(n for n in range(1, BLOCK_HEADS + 1) if heads % n == 0)


def pack_kernel(tap_count, head_dim, query_ref, key_ref, value_ref, rim_ref, tails, sems):
    back = tap_count - 1
    tok_count, width = query_ref.shape
    rows = pl.ds(tok_count - RIM, RIM)
    copies = [
        pltpu.make_async_copy(ref.at[rows], tails.at[i], sems.at[i])
        for i, ref in enumerate((key_ref, value_ref, query_ref))
    ]
    for copy in copies:
        copy.start()
    for copy in copies:
        copy.wait()
    key_tail, value_tail, query_tail = (tails[i].astype(f32)[-TILE:] for i in range(3))

    def paired(first, second):
        row = lax.broadcasted_iota(jnp.int32, first.shape, 0)
        return jnp.where(row < back, pltpu.roll(first, back, 0), pltpu.roll(second, 2 * back, 0))

    halves = []
    for start in (0, width // 2):
        tiles = [paired(key_tail[:, start : start + width // 2], value_tail[:, start : start + width // 2])]
        for at in range(start, start + width // 2, 2 * head_dim):
            heads = query_tail[:, at : at + 2 * head_dim]
            tiles.append(paired(heads[:, :head_dim], heads[:, head_dim:]))
        halves.append(jnp.concatenate(tiles, axis=1))
    rim_ref[...] = jnp.concatenate(halves, axis=0).astype(bf16)


def pack_rims(query_seq, key_seq, value_seq, tap_count, head_dim):
    width = query_seq.shape[1]
    return kernel_call(
        functools.partial(pack_kernel, tap_count, head_dim),
        "pack_rims",
        [IN_PLACE] * 3,
        IN_VMEM,
        shape((RIM, 3 * width // 4), bf16),
        [pltpu.VMEM((3, RIM, width), bf16), pltpu.SemaphoreType.DMA((3,))],
    )(in_hbm(query_seq), in_hbm(key_seq), in_hbm(value_seq))


def rim_tile(core_rim, chip_rim, quarter, start, size):
    device = lax.axis_index("seq")
    upper = ((device & 1) ^ int(quarter < 2)) != 0
    cols = columns(start, size)
    from_core, from_chip = (ref[:, cols].astype(f32) for ref in (core_rim, chip_rim))
    rim = jnp.where((device & 1) != 0, from_core, jnp.where(device > 0, from_chip, 0.0))
    return jnp.where(upper, rim[TILE:], rim[:TILE])


def state_rim(core_rim, chip_rim, quarter, width, start, size):
    pair = ((lax.axis_index("seq") >> 1) & 1) ^ int(quarter % 2 == 0)
    return rim_tile(core_rim, chip_rim, quarter, pair * (width // 4) + start, size)


def query_rim(core_rim, chip_rim, quarter, width, start, head_dim):
    pair = ((lax.axis_index("seq") >> 1) & 1) ^ int(quarter % 2 == 0)
    head = start // head_dim
    at = width // 2 + pair * (width // 8) + head // 2 * head_dim
    return rim_tile(core_rim, chip_rim, quarter, at, head_dim), head % 2 + 1


def convolved(scratch, rows, taps, rim=None, rim_end=0):
    length = rows.shape[0]
    if rim is None:
        scratch[:TILE] = jnp.zeros((TILE, rows.shape[1]), f32)
    else:
        scratch[:TILE] = pltpu.roll(rim, (-rim_end) % TILE, 0)
    scratch[TILE : TILE + length] = rows
    total = taps[0:1] * rows
    for offset in range(1, taps.shape[0]):
        total = total + taps[offset : offset + 1] * scratch[TILE - offset : TILE - offset + length]
    return total.astype(bf16)


def features(conv_rows, feature_map):
    projected = jnp.dot(conv_rows, feature_map, preferred_element_type=f32)
    return jnp.where(projected > 0, projected + 1.0, jnp.exp(projected)).astype(bf16)


def state_of(key_feat, value_conv):
    return lax.dot_general(
        key_feat, value_conv, (((0,), (0,)), ((), ())), preferred_element_type=f32
    )


def near_states_kernel(
    group, key_ref, value_ref, taps_ref, map_ref, feat_ref, conv_ref, state_ref, key_first, value_first, scratch
):
    head_dim = map_ref.shape[0]
    width = key_ref.shape[1]
    size = width // (4 * GROUPS)
    back = taps_ref.shape[1] - 1
    row = lax.broadcasted_iota(jnp.int32, (RIM, head_dim), 0)
    for quarter in range(4):
        for start in range(0, size, head_dim):
            natural = columns(quarter_start(quarter, width) + group * size + start, head_dim)
            at = quarter * size + start
            local = slice(at, at + head_dim)
            buffers = scratch.at[at // head_dim % scratch.shape[0]]
            key, value = key_ref[:, natural], value_ref[:, natural]
            key_first[:, local] = key[:RIM]
            value_first[:, local] = value[:RIM]
            key_conv = convolved(buffers.at[0], key.astype(f32), taps_ref[1, :, natural].astype(f32))
            key_feat = features(key_conv, map_ref[...])
            feat_ref[:, local] = key_feat
            value_conv = convolved(buffers.at[1], value.astype(f32), taps_ref[2, :, natural].astype(f32))
            conv_ref[:, local] = value_conv
            later = jnp.where(row < back, 0.0, key_feat[:RIM].astype(f32)).astype(bf16)
            key_feat = jnp.concatenate([later, key_feat[RIM:]], axis=0)
            state_ref[local] = state_of(key_feat, value_conv)


def near_states(group, key_seq, value_seq, conv_kernel, feature_map):
    tok_count, width = key_seq.shape
    head_dim = feature_map.shape[0]
    size = width // GROUPS
    rows, firsts = shape((tok_count, size), bf16), shape((RIM, size), bf16)
    return kernel_call(
        functools.partial(near_states_kernel, group),
        "near_states",
        [IN_VMEM] * 4,
        [IN_VMEM] * 5,
        [rows, rows, shape((size, head_dim), f32), firsts, firsts],
        [pltpu.VMEM((BLOCK_HEADS, 2, TILE + tok_count, head_dim), f32)],
    )(key_seq, value_seq, conv_kernel, feature_map)


def whole_states_kernel(
    group, key_ref, value_ref, taps_ref, map_ref, core_rim, chip_rim,
    feat_ref, conv_ref, other_ref, other_next, state_ref, scratch,
):
    head_dim = map_ref.shape[0]
    width = key_ref.shape[1]
    size = width // (4 * GROUPS)
    back = taps_ref.shape[1] - 1
    for quarter in range(4):
        for start in range(0, size, head_dim):
            natural = columns(quarter_start(quarter, width) + group * size + start, head_dim)
            at = quarter * size + start
            local = slice(at, at + head_dim)
            buffers = scratch.at[at // head_dim % scratch.shape[0]]
            taps = taps_ref[:, :, natural].astype(f32)
            rim = state_rim(core_rim, chip_rim, quarter, width, group * size + start, head_dim)
            key_conv = convolved(buffers.at[0], key_ref[:, natural].astype(f32), taps[1], rim, back)
            key_feat = features(key_conv, map_ref[...])
            feat_ref[:, local] = key_feat
            value_conv = convolved(buffers.at[1], value_ref[:, natural].astype(f32), taps[2], rim, 2 * back)
            conv_ref[:, local] = value_conv
            state = state_of(key_feat, value_conv)
            if quarter < 2:
                (other_ref, other_next)[quarter][start : start + head_dim] = state.astype(bf16)
            else:
                state_ref[at - 2 * size : at - 2 * size + head_dim] = state


def whole_states(group, key_seq, value_seq, conv_kernel, feature_map, rims):
    tok_count, width = key_seq.shape
    head_dim = feature_map.shape[0]
    size = width // GROUPS
    rows, other = shape((tok_count, size), bf16), shape((size // 4, head_dim), bf16)
    return kernel_call(
        functools.partial(whole_states_kernel, group),
        "whole_states",
        [IN_VMEM] * 6,
        [IN_VMEM] * 5,
        [rows, rows, other, other, shape((size // 2, head_dim), f32)],
        [pltpu.VMEM((BLOCK_HEADS, 2, TILE + tok_count, head_dim), f32)],
    )(key_seq, value_seq, conv_kernel, feature_map, *rims)


def first_rows_kernel(
    group, quarters, key_ref, value_ref, taps_ref, map_ref, core_rim, chip_rim, state_ref,
    feat_ref, conv_ref, sum_ref, scratch,
):
    head_dim = map_ref.shape[0]
    width = taps_ref.shape[2]
    back = taps_ref.shape[1] - 1
    row = lax.broadcasted_iota(jnp.int32, (RIM, head_dim), 0)
    size = width // (4 * GROUPS)
    for i, quarter in enumerate(quarters):
        there = slice(quarter * size, (quarter + 1) * size)
        natural = columns(quarter_start(quarter, width) + group * size, size)
        rim = state_rim(core_rim, chip_rim, quarter, width, group * size, size)
        conv = convolved(
            scratch.at[i, 0], key_ref[:, there].astype(f32), taps_ref[1, :, natural].astype(f32), rim, back
        )
        value_conv = convolved(
            scratch.at[i, 1], value_ref[:, there].astype(f32), taps_ref[2, :, natural].astype(f32), rim, 2 * back
        )
        conv_ref[:, i * size : (i + 1) * size] = value_conv
        parts = [slice(at, at + head_dim) for at in range(0, size, head_dim)]
        feats = [features(conv[:, part], map_ref[...]) for part in parts]
        feat_ref[:, i * size : (i + 1) * size] = jnp.concatenate(feats, axis=1)
        firsts = [jnp.where(row < back, feat.astype(f32), 0.0).astype(bf16) for feat in feats]
        for part, first in zip(parts, firsts):
            state = state_ref[there.start + part.start : there.start + part.stop]
            state = state + state_of(first, value_conv[:, part])
            sum_ref[i * size + part.start : i * size + part.stop] = state.astype(sum_ref.dtype)


def first_rows(group, quarters, state_type, key_first, value_first, conv_kernel, feature_map, rims, state):
    width = conv_kernel.shape[2]
    head_dim = feature_map.shape[0]
    size = width // (4 * GROUPS)
    rows = shape((RIM, len(quarters) * size), bf16)
    return kernel_call(
        functools.partial(first_rows_kernel, group, quarters),
        "first_rows",
        [IN_VMEM] * 7,
        [IN_VMEM] * 3,
        [rows, rows, shape((len(quarters) * size, head_dim), state_type)],
        [pltpu.VMEM((len(quarters), 2, TILE + RIM, size), f32)],
    )(key_first, value_first, conv_kernel, feature_map, *rims, state)


def within_kernel(
    quarter, group, query_ref, taps_ref, map_ref, core_rim, chip_rim, key_ref, value_ref, *rest
):
    (*firsts, feat_ref, mixed_ref, scratch) = rest
    head_dim = map_ref.shape[0]
    tok_count, width = query_ref.shape
    size = width // (4 * GROUPS)
    causal = lax.broadcasted_iota(jnp.int32, (tok_count, tok_count), 0) >= lax.broadcasted_iota(
        jnp.int32, (tok_count, tok_count), 1
    )
    for start in range(0, size, head_dim):
        natural = columns(quarter_start(quarter, width) + group * size + start, head_dim)
        local = slice(start, start + head_dim)
        at = slice(quarter * size + start, quarter * size + start + head_dim)
        first = quarter % 2 * size * int(quarter >= 2) + start
        first = slice(first, first + head_dim)
        key, value = key_ref[:, at], value_ref[:, at]
        if firsts:
            key = jnp.concatenate([firsts[0][:, first], key[RIM:]], axis=0)
            value = jnp.concatenate([firsts[1][:, first], value[RIM:]], axis=0)
        rim, end = query_rim(core_rim, chip_rim, quarter, width, group * size + start, head_dim)
        taps = taps_ref[0, :, natural].astype(f32)
        buffer = scratch.at[start // head_dim % scratch.shape[0]]
        conv = convolved(buffer, query_ref[:, natural].astype(f32), taps, rim, end * (taps_ref.shape[1] - 1))
        feat = features(conv, map_ref[...])
        feat_ref[:, local] = feat
        scores = lax.dot_general(feat, key, (((1,), (1,)), ((), ())), preferred_element_type=f32)
        weights = jnp.where(causal, scores, 0.0).astype(bf16)
        mixed_ref[:, local] = jnp.dot(weights, value, preferred_element_type=f32)


def within_block(quarter, group, query_seq, conv_kernel, feature_map, rims, feat, conv, firsts):
    tok_count, width = query_seq.shape
    head_dim = feature_map.shape[0]
    size = width // (4 * GROUPS)
    operands = (query_seq, conv_kernel, feature_map, *rims, feat, conv, *firsts)
    return kernel_call(
        functools.partial(within_kernel, quarter, group),
        "within_block",
        [IN_VMEM] * len(operands),
        [IN_VMEM] * 2,
        [shape((tok_count, size), bf16), shape((tok_count, size), f32)],
        [pltpu.VMEM((BLOCK_HEADS, TILE + tok_count, head_dim), f32)],
    )(*operands)


def finish_kernel(pieces, before, gain_ref, *rest):
    count = sum(len(part) for part in pieces)
    prefixes, rest = rest[: len(pieces)], rest[len(pieces) :]
    feats, mixes = rest[:count], rest[count : 2 * count]
    out_ref, *token, rows, sems = rest[2 * count + before :]
    for ref in token:
        ref[...] = jnp.zeros(ref.shape, f32)
    head_dim = prefixes[0].shape[1]
    tok_count, size = feats[0].shape
    copies = []
    for prefix_ref, part in zip(prefixes, pieces):
        for at, (quarter, group) in enumerate(part):
            i = len(copies)
            natural = quarter_start(quarter, out_ref.shape[1]) + group * size
            for start in range(0, size, head_dim):
                cols = slice(start, start + head_dim)
                prefix = prefix_ref[at * size + start : at * size + start + head_dim]
                mixed = mixes[i][:, cols] + jnp.dot(feats[i][:, cols], prefix, preferred_element_type=f32)
                inverse_rms = lax.rsqrt(jnp.mean(mixed * mixed, axis=-1, keepdims=True) + 1e-06)
                gain = gain_ref[:, columns(natural + start, head_dim)]
                rows[i, :, cols] = (mixed * inverse_rms * gain).astype(bf16)
            copies.append(pltpu.make_async_copy(rows.at[i], out_ref.at[:, columns(natural, size)], sems.at[i]))
            copies[-1].start()
    for copy in copies:
        copy.wait()


def finish(pieces, mixed, prefixes, norm_gain, before, last=False):
    width = norm_gain.shape[1]
    every = [piece for part in pieces for piece in part]
    count = len(every)
    tok_count, size = mixed[every[0]][0].shape
    operands = [norm_gain, *prefixes, *(mixed[p][0] for p in every), *(mixed[p][1] for p in every)]
    in_specs = [IN_VMEM] * len(operands)
    aliases = {}
    if before is not None:
        aliases = {len(operands): 0}
        operands.append(in_hbm(before))
        in_specs.append(IN_PLACE)
    return kernel_call(
        functools.partial(finish_kernel, pieces, len(aliases)),
        "finish",
        in_specs,
        [IN_PLACE, IN_VMEM][: 1 if last else 2],
        [pltpu.HBM((tok_count, width), bf16), shape((TILE, 128), f32)][: 1 if last else 2],
        [pltpu.VMEM((count, tok_count, size), bf16), pltpu.SemaphoreType.DMA((count,))],
        aliases,
    )(*operands)[0]


def swapped(block, distance):
    return lax.ppermute(block, "seq", [(i, i ^ distance) for i in range(lax.axis_size("seq"))])


def passed_on(block):
    count = lax.axis_size("seq")
    route = {i: i + 1 for i in range(1, count - 2, 2)}
    route |= {i: i - 1 for i in range(4, count - 3, 2)}
    route |= {0: 1, 2: 0, count - 2: count - 1, count - 1: count - 3}
    return lax.ppermute(block, "seq", sorted(route.items()))


def mapped(name, function, outputs, *arrays):
    def body(*refs):
        values = [ref[...] for ref in refs[: len(arrays)]]
        for ref, value in zip(refs[len(arrays) :], function(lax.axis_index("seq"), *values)):
            ref[...] = value.astype(ref.dtype)

    columns = arrays[0].shape[1]
    return kernel_call(
        body,
        name,
        [IN_VMEM] * len(arrays),
        [IN_VMEM] * len(outputs),
        [shape((rows, columns), kind) for rows, kind in outputs],
    )(*arrays)


def on_device(query_seq, key_seq, value_seq, conv_kernel, feature_map, norm_gain):
    tok_count, width = query_seq.shape
    tap_count = conv_kernel.shape[1]
    head_dim = feature_map.shape[0]
    device_count = lax.axis_size("seq")
    assert tok_count == SPAN and width % (4 * GROUPS * head_dim) == 0
    assert device_count >= 8 and device_count & (device_count - 1) == 0
    groups = range(GROUPS)
    rows = width // (4 * GROUPS)
    gain = norm_gain.reshape(1, width)

    def of_core(device):
        return (device & 1) != 0

    def of_pair(device):
        return (device & 2) != 0

    Turn.last = ()
    packed = pack_rims(query_seq, key_seq, value_seq, tap_count, head_dim)
    rims = (swapped(packed, 1), passed_on(packed))
    mixed = {}
    fill = [(q, g) for q in (3, 2, 1, 0) for g in groups]
    total = len(fill)

    def score(share):
        while fill and total - len(fill) < round(share * total):
            q, g = fill.pop(0)
            first = ()
            if firsts[g]:
                first = [part[q] for part in firsts[g][0]] if q < 2 else firsts[g][1]
            mixed[q, g] = within_block(q, g, query_seq, conv_kernel, feature_map, rims, *near[g], first)

    def chip_sums(device, state, paired, own):
        return state[:rows] + paired.astype(f32), state[rows:] + own.astype(f32)

    def pair_sums(device, own, arrived):
        total = own + arrived.astype(f32)
        return total, total

    def plane_sums(distance, device, total, *arrived):
        before, arrived = (0.0, arrived) if distance == 4 else (arrived[0], arrived[1:])
        upper = (device & distance) != 0
        if len(arrived) == 2:
            odd = (device & (distance // 2)) != 0
            mine, other = arrived
            arrived = (jnp.concatenate([jnp.where(odd, other, mine), jnp.where(odd, mine, other)], axis=0),)
        arrived = arrived[0].astype(f32)
        before = before + jnp.where(upper, arrived, 0.0)
        total = total + arrived
        give = total.astype(bf16)
        return total, before, jnp.where(upper, give[rows // 2 :], give[: rows // 2])

    def own_prefixes(distance, device, own, paired, cored, state, *step):
        before = plane_sums(distance, device, *step)[1] if step else jnp.zeros((rows, head_dim), f32)
        own_part = before + jnp.where(of_pair(device), paired.astype(f32), 0.0)
        others = before + jnp.where(of_pair(device), 0.0, own)
        return (
            others,
            own_part + jnp.where(of_core(device), cored.astype(f32), 0.0),
            own_part + jnp.where(of_core(device), 0.0, state[rows:]),
        )

    def paired_prefixes(device, arrived, cored, state, own):
        arrived = arrived.astype(f32)
        give = arrived + jnp.where(of_core(device), 0.0, state[:rows])
        return (
            arrived + jnp.where(of_core(device), cored.astype(f32), 0.0),
            jnp.concatenate([give.astype(bf16), own], axis=0),
        )

    near, firsts, state_b, from_core, chip, arriving = [], [], [], [], [], []
    running, earlier, from_pair = [None] * GROUPS, [None] * GROUPS, [None] * GROUPS
    distance = 4

    def pair_step(g):
        from_pair[g] = arriving[g]
        if distance < device_count:
            running[g], give = mapped("pair_sums", pair_sums, [(rows, f32), (rows, bf16)], chip[g], from_pair[g])
            arriving[g] = (swapped(give, distance),)

    for g in groups:
        if g == 0:
            *kept, partial, key_first, value_first = near_states(g, key_seq, value_seq, conv_kernel, feature_map)
            others, first_a = [], [[], []]
            for q in (0, 1):
                *first, other = first_rows(
                    g, (q,), bf16, key_first, value_first, conv_kernel, feature_map, rims, partial
                )
                others.append(swapped(other, 1))
                first_a[0].append(first[0])
                first_a[1].append(first[1])
            *first_b, state = first_rows(
                g, (2, 3), f32, key_first, value_first, conv_kernel, feature_map, rims, partial
            )
            firsts.append((first_a, first_b))
        else:
            *kept, other, other_next, state = whole_states(g, key_seq, value_seq, conv_kernel, feature_map, rims)
            others = [swapped(other, 1), swapped(other_next, 1)]
            firsts.append(None)
            pair_step(g - 1)
        near.append(kept)
        state_b.append(state)
        from_core.append(others)
        give, own = mapped("chip_sums", chip_sums, [(rows, bf16), (rows, f32)], state, *others)
        chip.append(own)
        arriving.append(swapped(give, 2))
    score(0.375)
    pair_step(GROUPS - 1)
    while 2 * distance < device_count:
        for g in groups:
            before = [] if distance == 4 else [earlier[g]]
            running[g], earlier[g], give = mapped(
                "plane_sums",
                functools.partial(plane_sums, distance),
                [(rows, f32), (rows, f32), (rows // 2, bf16)],
                running[g],
                *before,
                *arriving[g],
            )
            arriving[g] = swapped(give, 2 * distance)
            if g == 0:
                score(0.5)
        for g in groups:
            (mine,) = mapped("halves", lambda device, half: (half,), [(rows // 2, bf16)], arriving[g])
            arriving[g] = (mine, swapped(mine, distance))
            if g == 0:
                score(0.75)
        distance *= 2

    back, own_give = [None] * GROUPS, [None] * GROUPS
    owns = []
    for g in groups:
        step = ()
        if distance < device_count:
            step = (running[g], *([] if distance == 4 else [earlier[g]]), *arriving[g])
        others, own, own_give[g] = mapped(
            "own_prefixes",
            functools.partial(own_prefixes, distance),
            [(rows, bf16)] * 3,
            chip[g],
            from_pair[g],
            from_core[g][1],
            state_b[g],
            *step,
        )
        back[g] = swapped(others, 2)
        owns.append(own)
        score(0.75 + (1 - 0.75) * (g + 1) / GROUPS)
    out = finish([[(3, g)] for g in groups], mixed, owns, gain, None)
    from_other = [None] * GROUPS
    for g in groups:
        prefix_2, give = mapped(
            "paired_prefixes",
            paired_prefixes,
            [(rows, bf16), (2 * rows, bf16)],
            back[g],
            from_core[g][0],
            state_b[g],
            own_give[g],
        )
        from_other[g] = swapped(give, 1)
        if g == 0:
            out = finish([[(2, g)]], mixed, [prefix_2], gain, out)
        else:
            pieces = [[(2, g)], [(0, g - 1), (1, g - 1)]]
            out = finish(pieces, mixed, [prefix_2, from_other[g - 1]], gain, out)
    return finish([[(0, g), (1, g)]], mixed, [from_other[g]], gain, out, last=True)


def solution(mesh):
    return jax.shard_map(
        on_device,
        mesh=mesh,
        in_specs=(
            P(("groups", "seq"), None),
            P(("groups", "seq"), None),
            P(("groups", "seq"), None),
            P(),
            P(),
            P(),
        ),
        out_specs=P(("groups", "seq"), None),
        check_vma=False,
    )
```

```python
import functools

import jax
import jax.numpy as jnp
from jax import lax
from jax.experimental import pallas as pl
from jax.experimental.pallas import tpu as pltpu
from jax.sharding import PartitionSpec as P

SPAN = 256
GROUPS = 2
BLOCK_HEADS = 6
RIM = 16
TILE = 8
VMEM_BYTES = 12 * 1024 * 1024
f32, bf16 = jnp.float32, jnp.bfloat16
IN_VMEM = pl.BlockSpec(memory_space=pltpu.VMEM)
IN_PLACE = pl.BlockSpec(memory_space=pl.ANY)
LIGHT = pl.CostEstimate(flops=1024, bytes_accessed=1024, transcendentals=0)


def in_hbm(array):
    return pltpu.with_memory_space_constraint(array, pltpu.HBM)


class Turn:
    last = ()


def kernel_call(body, name, in_specs, out_specs, out_shape, scratch=(), aliases=None):
    count = len(in_specs)

    def call(*operands):
        before = Turn.last

        def ordered(*refs):
            body(*refs[:count], *refs[count + len(before) :])

        results = pl.pallas_call(
            ordered,
            in_specs=[*in_specs, *[IN_PLACE] * len(before)],
            out_specs=out_specs,
            out_shape=out_shape,
            scratch_shapes=list(scratch),
            input_output_aliases=aliases or {},
            compiler_params=pltpu.CompilerParams(vmem_limit_bytes=VMEM_BYTES),
            cost_estimate=LIGHT,
            name=name,
        )(*operands, *before)
        Turn.last = (results[-1] if isinstance(results, (list, tuple)) else results,)
        return results

    return call


def shape(dims, kind):
    return jax.ShapeDtypeStruct(dims, kind)


def quarter_start(quarter, width):
    device = lax.axis_index("seq")
    core = (device & 1) ^ int(quarter < 2)
    pair = ((device >> 1) & 1) ^ int(quarter % 2 == 0)
    return (2 * core + pair) * (width // 4)


def columns(start, size):
    return pl.ds(pl.multiple_of(start, 128), size)


def block_heads(heads):
    return max(n for n in range(1, BLOCK_HEADS + 1) if heads % n == 0)


def pack_kernel(tap_count, head_dim, query_ref, key_ref, value_ref, rim_ref, tails, sems):
    back = tap_count - 1
    tok_count, width = query_ref.shape
    rows = pl.ds(tok_count - RIM, RIM)
    copies = [
        pltpu.make_async_copy(ref.at[rows], tails.at[i], sems.at[i])
        for i, ref in enumerate((key_ref, value_ref, query_ref))
    ]
    for copy in copies:
        copy.start()
    for copy in copies:
        copy.wait()
    key_tail, value_tail, query_tail = (tails[i].astype(f32)[-TILE:] for i in range(3))

    def paired(first, second):
        row = lax.broadcasted_iota(jnp.int32, first.shape, 0)
        return jnp.where(row < back, pltpu.roll(first, back, 0), pltpu.roll(second, 2 * back, 0))

    halves = []
    for start in (0, width // 2):
        tiles = [paired(key_tail[:, start : start + width // 2], value_tail[:, start : start + width // 2])]
        for at in range(start, start + width // 2, 2 * head_dim):
            heads = query_tail[:, at : at + 2 * head_dim]
            tiles.append(paired(heads[:, :head_dim], heads[:, head_dim:]))
        halves.append(jnp.concatenate(tiles, axis=1))
    rim_ref[...] = jnp.concatenate(halves, axis=0).astype(bf16)


def pack_rims(query_seq, key_seq, value_seq, tap_count, head_dim):
    width = query_seq.shape[1]
    return kernel_call(
        functools.partial(pack_kernel, tap_count, head_dim),
        "pack_rims",
        [IN_PLACE] * 3,
        IN_VMEM,
        shape((RIM, 3 * width // 4), bf16),
        [pltpu.VMEM((3, RIM, width), bf16), pltpu.SemaphoreType.DMA((3,))],
    )(in_hbm(query_seq), in_hbm(key_seq), in_hbm(value_seq))


def rim_tile(core_rim, chip_rim, quarter, start, size):
    device = lax.axis_index("seq")
    upper = ((device & 1) ^ int(quarter < 2)) != 0
    cols = columns(start, size)
    from_core, from_chip = (ref[:, cols].astype(f32) for ref in (core_rim, chip_rim))
    rim = jnp.where((device & 1) != 0, from_core, jnp.where(device > 0, from_chip, 0.0))
    return jnp.where(upper, rim[TILE:], rim[:TILE])


def state_rim(core_rim, chip_rim, quarter, width, start, size):
    pair = ((lax.axis_index("seq") >> 1) & 1) ^ int(quarter % 2 == 0)
    return rim_tile(core_rim, chip_rim, quarter, pair * (width // 4) + start, size)


def query_rim(core_rim, chip_rim, quarter, width, start, head_dim):
    pair = ((lax.axis_index("seq") >> 1) & 1) ^ int(quarter % 2 == 0)
    head = start // head_dim
    at = width // 2 + pair * (width // 8) + head // 2 * head_dim
    return rim_tile(core_rim, chip_rim, quarter, at, head_dim), head % 2 + 1


def convolved(scratch, rows, taps, rim=None, rim_end=0):
    length = rows.shape[0]
    if rim is None:
        scratch[:TILE] = jnp.zeros((TILE, rows.shape[1]), f32)
    else:
        scratch[:TILE] = pltpu.roll(rim, (-rim_end) % TILE, 0)
    scratch[TILE : TILE + length] = rows
    total = taps[0:1] * rows
    for offset in range(1, taps.shape[0]):
        total = total + taps[offset : offset + 1] * scratch[TILE - offset : TILE - offset + length]
    return total.astype(bf16)


def features(conv_rows, feature_map):
    projected = jnp.dot(conv_rows, feature_map, preferred_element_type=f32)
    return jnp.where(projected > 0, projected + 1.0, jnp.exp(projected)).astype(bf16)


def state_of(key_feat, value_conv):
    return lax.dot_general(
        key_feat, value_conv, (((0,), (0,)), ((), ())), preferred_element_type=f32
    )


def near_states_kernel(
    group, key_ref, value_ref, taps_ref, map_ref, feat_ref, conv_ref, state_ref, key_first, value_first, scratch
):
    head_dim = map_ref.shape[0]
    width = key_ref.shape[1]
    size = width // (4 * GROUPS)
    back = taps_ref.shape[1] - 1
    row = lax.broadcasted_iota(jnp.int32, (RIM, head_dim), 0)
    for quarter in range(4):
        for start in range(0, size, head_dim):
            natural = columns(quarter_start(quarter, width) + group * size + start, head_dim)
            at = quarter * size + start
            local = slice(at, at + head_dim)
            buffers = scratch.at[at // head_dim % scratch.shape[0]]
            key, value = key_ref[:, natural], value_ref[:, natural]
            key_first[:, local] = key[:RIM]
            value_first[:, local] = value[:RIM]
            key_conv = convolved(buffers.at[0], key.astype(f32), taps_ref[1, :, natural].astype(f32))
            key_feat = features(key_conv, map_ref[...])
            feat_ref[:, local] = key_feat
            value_conv = convolved(buffers.at[1], value.astype(f32), taps_ref[2, :, natural].astype(f32))
            conv_ref[:, local] = value_conv
            later = jnp.where(row < back, 0.0, key_feat[:RIM].astype(f32)).astype(bf16)
            key_feat = jnp.concatenate([later, key_feat[RIM:]], axis=0)
            state_ref[local] = state_of(key_feat, value_conv)


def near_states(group, key_seq, value_seq, conv_kernel, feature_map):
    tok_count, width = key_seq.shape
    head_dim = feature_map.shape[0]
    size = width // GROUPS
    rows, firsts = shape((tok_count, size), bf16), shape((RIM, size), bf16)
    return kernel_call(
        functools.partial(near_states_kernel, group),
        "near_states",
        [IN_VMEM] * 4,
        [IN_VMEM] * 5,
        [rows, rows, shape((size, head_dim), f32), firsts, firsts],
        [pltpu.VMEM((BLOCK_HEADS, 2, TILE + tok_count, head_dim), f32)],
    )(key_seq, value_seq, conv_kernel, feature_map)


def whole_states_kernel(
    group, quarters, key_ref, value_ref, taps_ref, map_ref, core_rim, chip_rim, feat_ref, conv_ref, *rest
):
    (*states, scratch) = rest
    head_dim = map_ref.shape[0]
    width = key_ref.shape[1]
    size = width // (4 * GROUPS)
    back = taps_ref.shape[1] - 1
    for i, quarter in enumerate(quarters):
        for start in range(0, size, head_dim):
            natural = columns(quarter_start(quarter, width) + group * size + start, head_dim)
            at = i * size + start
            local = slice(at, at + head_dim)
            buffers = scratch.at[at // head_dim % scratch.shape[0]]
            taps = taps_ref[:, :, natural].astype(f32)
            rim = state_rim(core_rim, chip_rim, quarter, width, group * size + start, head_dim)
            key_conv = convolved(buffers.at[0], key_ref[:, natural].astype(f32), taps[1], rim, back)
            key_feat = features(key_conv, map_ref[...])
            feat_ref[:, local] = key_feat
            value_conv = convolved(buffers.at[1], value_ref[:, natural].astype(f32), taps[2], rim, 2 * back)
            conv_ref[:, local] = value_conv
            states[i][start : start + head_dim] = state_of(key_feat, value_conv).astype(states[i].dtype)


def whole_states(group, quarters, state_type, key_seq, value_seq, conv_kernel, feature_map, rims):
    tok_count, width = key_seq.shape
    head_dim = feature_map.shape[0]
    size = width // (4 * GROUPS)
    rows = shape((tok_count, len(quarters) * size), bf16)
    return kernel_call(
        functools.partial(whole_states_kernel, group, quarters),
        "whole_states",
        [IN_VMEM] * 6,
        [IN_VMEM] * (2 + len(quarters)),
        [rows, rows, *[shape((size, head_dim), state_type)] * len(quarters)],
        [pltpu.VMEM((BLOCK_HEADS, 2, TILE + tok_count, head_dim), f32)],
    )(key_seq, value_seq, conv_kernel, feature_map, *rims)


def first_rows_kernel(
    group, quarters, key_ref, value_ref, taps_ref, map_ref, core_rim, chip_rim, state_ref,
    feat_ref, conv_ref, *rest
):
    (*sums, scratch) = rest
    head_dim = map_ref.shape[0]
    width = taps_ref.shape[2]
    back = taps_ref.shape[1] - 1
    row = lax.broadcasted_iota(jnp.int32, (RIM, head_dim), 0)
    size = width // (4 * GROUPS)
    for i, quarter in enumerate(quarters):
        there = slice(quarter * size, (quarter + 1) * size)
        natural = columns(quarter_start(quarter, width) + group * size, size)
        rim = state_rim(core_rim, chip_rim, quarter, width, group * size, size)
        conv = convolved(
            scratch.at[i, 0], key_ref[:, there].astype(f32), taps_ref[1, :, natural].astype(f32), rim, back
        )
        value_conv = convolved(
            scratch.at[i, 1], value_ref[:, there].astype(f32), taps_ref[2, :, natural].astype(f32), rim, 2 * back
        )
        conv_ref[:, i * size : (i + 1) * size] = value_conv
        parts = [slice(at, at + head_dim) for at in range(0, size, head_dim)]
        feats = [features(conv[:, part], map_ref[...]) for part in parts]
        feat_ref[:, i * size : (i + 1) * size] = jnp.concatenate(feats, axis=1)
        firsts = [jnp.where(row < back, feat.astype(f32), 0.0).astype(bf16) for feat in feats]
        for part, first in zip(parts, firsts):
            state = state_ref[there.start + part.start : there.start + part.stop]
            state = state + state_of(first, value_conv[:, part])
            sums[i][part] = state.astype(sums[i].dtype)


def first_rows(group, quarters, state_type, key_first, value_first, conv_kernel, feature_map, rims, state):
    width = conv_kernel.shape[2]
    head_dim = feature_map.shape[0]
    size = width // (4 * GROUPS)
    rows = shape((RIM, len(quarters) * size), bf16)
    return kernel_call(
        functools.partial(first_rows_kernel, group, quarters),
        "first_rows",
        [IN_VMEM] * 7,
        [IN_VMEM] * (2 + len(quarters)),
        [rows, rows, *[shape((size, head_dim), state_type)] * len(quarters)],
        [pltpu.VMEM((len(quarters), 2, TILE + RIM, size), f32)],
    )(key_first, value_first, conv_kernel, feature_map, *rims, state)


def within_kernel(
    quarter, group, base, query_ref, taps_ref, map_ref, core_rim, chip_rim, key_ref, value_ref, *rest
):
    (*firsts, feat_ref, mixed_ref, scratch) = rest
    head_dim = map_ref.shape[0]
    tok_count, width = query_ref.shape
    size = width // (4 * GROUPS)
    causal = lax.broadcasted_iota(jnp.int32, (tok_count, tok_count), 0) >= lax.broadcasted_iota(
        jnp.int32, (tok_count, tok_count), 1
    )
    starts = range(0, size, head_dim)
    for start in starts:
        natural = columns(quarter_start(quarter, width) + group * size + start, head_dim)
        rim, end = query_rim(core_rim, chip_rim, quarter, width, group * size + start, head_dim)
        taps = taps_ref[0, :, natural].astype(f32)
        buffer = scratch.at[start // head_dim % scratch.shape[0]]
        conv = convolved(buffer, query_ref[:, natural].astype(f32), taps, rim, end * (taps_ref.shape[1] - 1))
        feat_ref[:, start : start + head_dim] = features(conv, map_ref[...])
    products = []
    for start in starts:
        local, at = slice(start, start + head_dim), slice(base + start, base + start + head_dim)
        first = quarter % 2 * size * int(quarter >= 2) + start
        first = slice(first, first + head_dim)
        key, value = key_ref[:, at], value_ref[:, at]
        if firsts:
            key = jnp.concatenate([firsts[0][:, first], key[RIM:]], axis=0)
            value = jnp.concatenate([firsts[1][:, first], value[RIM:]], axis=0)
        scores = lax.dot_general(feat_ref[:, local], key, (((1,), (1,)), ((), ())), preferred_element_type=f32)
        products.append((local, jnp.where(causal, scores, 0.0).astype(bf16), value))
    for local, weights, value in products:
        mixed_ref[:, local] = jnp.dot(weights, value, preferred_element_type=f32)


def within_block(quarter, group, query_seq, conv_kernel, feature_map, rims, feat, conv, base, firsts):
    tok_count, width = query_seq.shape
    head_dim = feature_map.shape[0]
    size = width // (4 * GROUPS)
    operands = (query_seq, conv_kernel, feature_map, *rims, feat, conv, *firsts)
    return kernel_call(
        functools.partial(within_kernel, quarter, group, base),
        "within_block",
        [IN_VMEM] * len(operands),
        [IN_VMEM] * 2,
        [shape((tok_count, size), bf16), shape((tok_count, size), f32)],
        [pltpu.VMEM((BLOCK_HEADS, TILE + tok_count, head_dim), f32)],
    )(*operands)


def finish_kernel(pieces, before, gain_ref, *rest):
    count = sum(len(part) for part in pieces)
    prefixes, rest = rest[: len(pieces)], rest[len(pieces) :]
    feats, mixes = rest[:count], rest[count : 2 * count]
    out_ref, *token, rows, sems = rest[2 * count + before :]
    for ref in token:
        ref[...] = jnp.zeros(ref.shape, f32)
    head_dim = prefixes[0].shape[1]
    tok_count, size = feats[0].shape
    copies = []
    for prefix_ref, part in zip(prefixes, pieces):
        for at, (quarter, group) in enumerate(part):
            i = len(copies)
            natural = quarter_start(quarter, out_ref.shape[1]) + group * size
            for start in range(0, size, head_dim):
                cols = slice(start, start + head_dim)
                prefix = prefix_ref[at * size + start : at * size + start + head_dim]
                mixed = mixes[i][:, cols] + jnp.dot(feats[i][:, cols], prefix, preferred_element_type=f32)
                inverse_rms = lax.rsqrt(jnp.mean(mixed * mixed, axis=-1, keepdims=True) + 1e-06)
                gain = gain_ref[:, columns(natural + start, head_dim)]
                rows[i, :, cols] = (mixed * inverse_rms * gain).astype(bf16)
            copies.append(pltpu.make_async_copy(rows.at[i], out_ref.at[:, columns(natural, size)], sems.at[i]))
            copies[-1].start()
    for copy in copies:
        copy.wait()


def finish(pieces, mixed, prefixes, norm_gain, before, last=False):
    width = norm_gain.shape[1]
    every = [piece for part in pieces for piece in part]
    count = len(every)
    tok_count, size = mixed[every[0]][0].shape
    operands = [norm_gain, *prefixes, *(mixed[p][0] for p in every), *(mixed[p][1] for p in every)]
    in_specs = [IN_VMEM] * len(operands)
    aliases = {}
    if before is not None:
        aliases = {len(operands): 0}
        operands.append(in_hbm(before))
        in_specs.append(IN_PLACE)
    return kernel_call(
        functools.partial(finish_kernel, pieces, len(aliases)),
        "finish",
        in_specs,
        [IN_PLACE, IN_VMEM][: 1 if last else 2],
        [pltpu.HBM((tok_count, width), bf16), shape((TILE, 128), f32)][: 1 if last else 2],
        [pltpu.VMEM((count, tok_count, size), bf16), pltpu.SemaphoreType.DMA((count,))],
        aliases,
    )(*operands)[0]


def swapped(block, distance):
    return lax.ppermute(block, "seq", [(i, i ^ distance) for i in range(lax.axis_size("seq"))])


def passed_on(block):
    count = lax.axis_size("seq")
    route = {i: i + 1 for i in range(1, count - 2, 2)}
    route |= {i: i - 1 for i in range(4, count - 3, 2)}
    route |= {0: 1, 2: 0, count - 2: count - 1, count - 1: count - 3}
    return lax.ppermute(block, "seq", sorted(route.items()))


def mapped(name, function, outputs, *arrays):
    def body(*refs):
        values = [ref[...] for ref in refs[: len(arrays)]]
        for ref, value in zip(refs[len(arrays) :], function(lax.axis_index("seq"), *values)):
            ref[...] = value.astype(ref.dtype)

    columns = arrays[0].shape[1]
    return kernel_call(
        body,
        name,
        [IN_VMEM] * len(arrays),
        [IN_VMEM] * len(outputs),
        [shape((rows, columns), kind) for rows, kind in outputs],
    )(*arrays)


def on_device(query_seq, key_seq, value_seq, conv_kernel, feature_map, norm_gain):
    tok_count, width = query_seq.shape
    tap_count = conv_kernel.shape[1]
    head_dim = feature_map.shape[0]
    device_count = lax.axis_size("seq")
    assert tok_count == SPAN and width % (4 * GROUPS * head_dim) == 0
    assert device_count >= 8 and device_count & (device_count - 1) == 0
    groups = range(GROUPS)
    rows = width // (4 * GROUPS)
    gain = norm_gain.reshape(1, width)

    def of_core(device):
        return (device & 1) != 0

    def of_pair(device):
        return (device & 2) != 0

    Turn.last = ()
    packed = pack_rims(query_seq, key_seq, value_seq, tap_count, head_dim)
    rims = (swapped(packed, 1), passed_on(packed))
    mixed = {}
    fill = [(q, g) for q in (3, 2, 1, 0) for g in groups]
    total = len(fill)

    def score(share):
        while fill and total - len(fill) < round(share * total):
            q, g = fill.pop(0)
            first = ()
            if firsts[g]:
                first = [part[q] for part in firsts[g][0]] if q < 2 else firsts[g][1]
            mixed[q, g] = within_block(q, g, query_seq, conv_kernel, feature_map, rims, *near[g][q], first)

    def chip_sums(device, paired, own, paired_arrived, own_arrived):
        return paired + paired_arrived.astype(f32), own + own_arrived.astype(f32)

    def pair_sums(device, own, arrived):
        total = own + arrived.astype(f32)
        return total, total

    def plane_sums(distance, device, total, *arrived):
        before, arrived = (0.0, arrived) if distance == 4 else (arrived[0], arrived[1:])
        upper = (device & distance) != 0
        if len(arrived) == 2:
            odd = (device & (distance // 2)) != 0
            mine, other = arrived
            arrived = (jnp.concatenate([jnp.where(odd, other, mine), jnp.where(odd, mine, other)], axis=0),)
        arrived = arrived[0].astype(f32)
        before = before + jnp.where(upper, arrived, 0.0)
        total = total + arrived
        give = total.astype(bf16)
        return total, before, jnp.where(upper, give[rows // 2 :], give[: rows // 2])

    def own_prefixes(distance, device, own, paired, cored, state, *step):
        before = plane_sums(distance, device, *step)[1] if step else jnp.zeros((rows, head_dim), f32)
        own_part = before + jnp.where(of_pair(device), paired.astype(f32), 0.0)
        others = before + jnp.where(of_pair(device), 0.0, own)
        return (
            others,
            own_part + jnp.where(of_core(device), cored.astype(f32), 0.0),
            own_part + jnp.where(of_core(device), 0.0, state),
        )

    def paired_prefixes(device, arrived, cored, state, own):
        arrived = arrived.astype(f32)
        give = arrived + jnp.where(of_core(device), 0.0, state)
        return (
            arrived + jnp.where(of_core(device), cored.astype(f32), 0.0),
            jnp.concatenate([give.astype(bf16), own], axis=0),
        )

    near, firsts, state_b, from_core, chip, arriving = [], [], [], [], [], []
    running, earlier, from_pair = [None] * GROUPS, [None] * GROUPS, [None] * GROUPS
    distance = 4

    def pair_step(g):
        from_pair[g] = arriving[g]
        if distance < device_count:
            running[g], give = mapped("pair_sums", pair_sums, [(rows, f32), (rows, bf16)], chip[g], from_pair[g])
            arriving[g] = (swapped(give, distance),)

    for g in groups:
        if g == 0:
            *kept, partial, key_first, value_first = near_states(g, key_seq, value_seq, conv_kernel, feature_map)
            near.append([(*kept, q * rows) for q in range(4)])
            others, first_a = [], [[], []]
            for q in (0, 1):
                *first, other = first_rows(
                    g, (q,), bf16, key_first, value_first, conv_kernel, feature_map, rims, partial
                )
                others.append(swapped(other, 1))
                first_a[0].append(first[0])
                first_a[1].append(first[1])
            *first_b, paired, single = first_rows(
                g, (2, 3), f32, key_first, value_first, conv_kernel, feature_map, rims, partial
            )
            firsts.append((first_a, first_b))
        else:
            *kept, other, other_next = whole_states(
                g, (0, 1), bf16, key_seq, value_seq, conv_kernel, feature_map, rims
            )
            others = [swapped(other, 1), swapped(other_next, 1)]
            near.append([(*kept, q * rows) for q in range(2)])
            *kept, paired, single = whole_states(
                g, (2, 3), f32, key_seq, value_seq, conv_kernel, feature_map, rims
            )
            near[g] += [(*kept, q * rows) for q in range(2)]
            firsts.append(None)
            pair_step(g - 1)
        state_b.append((paired, single))
        from_core.append(others)
        give, own = mapped("chip_sums", chip_sums, [(rows, bf16), (rows, f32)], paired, single, *others)
        chip.append(own)
        arriving.append(swapped(give, 2))
    score(0.375)
    pair_step(GROUPS - 1)
    while 2 * distance < device_count:
        for g in groups:
            before = [] if distance == 4 else [earlier[g]]
            running[g], earlier[g], give = mapped(
                "plane_sums",
                functools.partial(plane_sums, distance),
                [(rows, f32), (rows, f32), (rows // 2, bf16)],
                running[g],
                *before,
                *arriving[g],
            )
            arriving[g] = swapped(give, 2 * distance)
            if g == 0:
                score(0.5)
        for g in groups:
            (mine,) = mapped("halves", lambda device, half: (half,), [(rows // 2, bf16)], arriving[g])
            arriving[g] = (mine, swapped(mine, distance))
            if g == 0:
                score(0.75)
        distance *= 2

    back, own_give = [None] * GROUPS, [None] * GROUPS
    owns = []
    for g in groups:
        step = ()
        if distance < device_count:
            step = (running[g], *([] if distance == 4 else [earlier[g]]), *arriving[g])
        others, own, own_give[g] = mapped(
            "own_prefixes",
            functools.partial(own_prefixes, distance),
            [(rows, bf16)] * 3,
            chip[g],
            from_pair[g],
            from_core[g][1],
            state_b[g][1],
            *step,
        )
        back[g] = swapped(others, 2)
        owns.append(own)
        score(0.75 + (1 - 0.75) * (g + 1) / GROUPS)
    out = finish([[(3, g)] for g in groups], mixed, owns, gain, None)
    from_other = [None] * GROUPS
    for g in groups:
        prefix_2, give = mapped(
            "paired_prefixes",
            paired_prefixes,
            [(rows, bf16), (2 * rows, bf16)],
            back[g],
            from_core[g][0],
            state_b[g][0],
            own_give[g],
        )
        from_other[g] = swapped(give, 1)
        if g == 0:
            out = finish([[(2, g)]], mixed, [prefix_2], gain, out)
        else:
            pieces = [[(2, g)], [(0, g - 1), (1, g - 1)]]
            out = finish(pieces, mixed, [prefix_2, from_other[g - 1]], gain, out)
    return finish([[(0, g), (1, g)]], mixed, [from_other[g]], gain, out, last=True)


def solution(mesh):
    return jax.shard_map(
        on_device,
        mesh=mesh,
        in_specs=(
            P(("groups", "seq"), None),
            P(("groups", "seq"), None),
            P(("groups", "seq"), None),
            P(),
            P(),
            P(),
        ),
        out_specs=P(("groups", "seq"), None),
        check_vma=False,
    )
```

```python
import functools

import jax
import jax.numpy as jnp
from jax import lax
from jax.experimental import pallas as pl
from jax.experimental.pallas import tpu as pltpu
from jax.sharding import PartitionSpec as P

SPAN = 256
GROUPS = 2
BLOCK_HEADS = 6
RIM = 16
TILE = 8
VMEM_BYTES = 12 * 1024 * 1024
f32, bf16 = jnp.float32, jnp.bfloat16
IN_VMEM = pl.BlockSpec(memory_space=pltpu.VMEM)
IN_PLACE = pl.BlockSpec(memory_space=pl.ANY)
LIGHT = pl.CostEstimate(flops=1024, bytes_accessed=1024, transcendentals=0)


def in_hbm(array):
    return pltpu.with_memory_space_constraint(array, pltpu.HBM)


class Turn:
    last = ()


def kernel_call(body, name, in_specs, out_specs, out_shape, scratch=(), aliases=None):
    count = len(in_specs)

    def call(*operands):
        before = Turn.last

        def ordered(*refs):
            body(*refs[:count], *refs[count + len(before) :])

        results = pl.pallas_call(
            ordered,
            in_specs=[*in_specs, *[IN_PLACE] * len(before)],
            out_specs=out_specs,
            out_shape=out_shape,
            scratch_shapes=list(scratch),
            input_output_aliases=aliases or {},
            compiler_params=pltpu.CompilerParams(vmem_limit_bytes=VMEM_BYTES),
            cost_estimate=LIGHT,
            name=name,
        )(*operands, *before)
        Turn.last = (results[-1] if isinstance(results, (list, tuple)) else results,)
        return results

    return call


def shape(dims, kind):
    return jax.ShapeDtypeStruct(dims, kind)


def quarter_start(quarter, width):
    device = lax.axis_index("seq")
    core = (device & 1) ^ int(quarter < 2)
    pair = ((device >> 1) & 1) ^ int(quarter % 2 == 0)
    return (2 * core + pair) * (width // 4)


def columns(start, size):
    return pl.ds(pl.multiple_of(start, 128), size)


def block_heads(heads):
    return max(n for n in range(1, BLOCK_HEADS + 1) if heads % n == 0)


def pack_kernel(tap_count, head_dim, query_ref, key_ref, value_ref, rim_ref, tails, sems):
    back = tap_count - 1
    tok_count, width = query_ref.shape
    rows = pl.ds(tok_count - RIM, RIM)
    copies = [
        pltpu.make_async_copy(ref.at[rows], tails.at[i], sems.at[i])
        for i, ref in enumerate((key_ref, value_ref, query_ref))
    ]
    for copy in copies:
        copy.start()
    for copy in copies:
        copy.wait()
    key_tail, value_tail, query_tail = (tails[i].astype(f32)[-TILE:] for i in range(3))

    def paired(first, second):
        row = lax.broadcasted_iota(jnp.int32, first.shape, 0)
        return jnp.where(row < back, pltpu.roll(first, back, 0), pltpu.roll(second, 2 * back, 0))

    halves = []
    for start in (0, width // 2):
        tiles = [paired(key_tail[:, start : start + width // 2], value_tail[:, start : start + width // 2])]
        for at in range(start, start + width // 2, 2 * head_dim):
            heads = query_tail[:, at : at + 2 * head_dim]
            tiles.append(paired(heads[:, :head_dim], heads[:, head_dim:]))
        halves.append(jnp.concatenate(tiles, axis=1))
    rim_ref[...] = jnp.concatenate(halves, axis=0).astype(bf16)


def pack_rims(query_seq, key_seq, value_seq, tap_count, head_dim):
    width = query_seq.shape[1]
    return kernel_call(
        functools.partial(pack_kernel, tap_count, head_dim),
        "pack_rims",
        [IN_PLACE] * 3,
        IN_VMEM,
        shape((RIM, 3 * width // 4), bf16),
        [pltpu.VMEM((3, RIM, width), bf16), pltpu.SemaphoreType.DMA((3,))],
    )(in_hbm(query_seq), in_hbm(key_seq), in_hbm(value_seq))


def rim_tile(core_rim, chip_rim, quarter, start, size):
    device = lax.axis_index("seq")
    upper = ((device & 1) ^ int(quarter < 2)) != 0
    cols = columns(start, size)
    from_core, from_chip = (ref[:, cols].astype(f32) for ref in (core_rim, chip_rim))
    rim = jnp.where((device & 1) != 0, from_core, jnp.where(device > 0, from_chip, 0.0))
    return jnp.where(upper, rim[TILE:], rim[:TILE])


def state_rim(core_rim, chip_rim, quarter, width, start, size):
    pair = ((lax.axis_index("seq") >> 1) & 1) ^ int(quarter % 2 == 0)
    return rim_tile(core_rim, chip_rim, quarter, pair * (width // 4) + start, size)


def query_rim(core_rim, chip_rim, quarter, width, start, head_dim):
    pair = ((lax.axis_index("seq") >> 1) & 1) ^ int(quarter % 2 == 0)
    head = start // head_dim
    at = width // 2 + pair * (width // 8) + head // 2 * head_dim
    return rim_tile(core_rim, chip_rim, quarter, at, head_dim), head % 2 + 1


def convolved(scratch, rows, taps, rim=None, rim_end=0):
    length = rows.shape[0]
    if rim is None:
        scratch[:TILE] = jnp.zeros((TILE, rows.shape[1]), f32)
    else:
        scratch[:TILE] = pltpu.roll(rim, (-rim_end) % TILE, 0)
    scratch[TILE : TILE + length] = rows
    total = taps[0:1] * rows
    for offset in range(1, taps.shape[0]):
        total = total + taps[offset : offset + 1] * scratch[TILE - offset : TILE - offset + length]
    return total.astype(bf16)


def features(conv_rows, feature_map):
    projected = jnp.dot(conv_rows, feature_map, preferred_element_type=f32)
    return jnp.where(projected > 0, projected + 1.0, jnp.exp(projected)).astype(bf16)


def state_of(key_feat, value_conv):
    return lax.dot_general(
        key_feat, value_conv, (((0,), (0,)), ((), ())), preferred_element_type=f32
    )


def near_states_kernel(
    group, key_ref, value_ref, taps_ref, map_ref,
    feat_ref, conv_ref, other_ref, other_next, state_ref, key_first, value_first, scratch,
):
    head_dim = map_ref.shape[0]
    width = key_ref.shape[1]
    size = width // (4 * GROUPS)
    back = taps_ref.shape[1] - 1
    row = lax.broadcasted_iota(jnp.int32, (RIM, head_dim), 0)
    for quarter in range(4):
        for start in range(0, size, head_dim):
            natural = columns(quarter_start(quarter, width) + group * size + start, head_dim)
            at = quarter * size + start
            local = slice(at, at + head_dim)
            buffers = scratch.at[at // head_dim % scratch.shape[0]]
            key, value = key_ref[:, natural], value_ref[:, natural]
            key_first[:, local] = key[:RIM]
            value_first[:, local] = value[:RIM]
            key_conv = convolved(buffers.at[0], key.astype(f32), taps_ref[1, :, natural].astype(f32))
            key_feat = features(key_conv, map_ref[...])
            feat_ref[:, local] = key_feat
            value_conv = convolved(buffers.at[1], value.astype(f32), taps_ref[2, :, natural].astype(f32))
            conv_ref[:, local] = value_conv
            later = jnp.where(row < back, 0.0, key_feat[:RIM].astype(f32)).astype(bf16)
            key_feat = jnp.concatenate([later, key_feat[RIM:]], axis=0)
            state = state_of(key_feat, value_conv)
            if quarter < 2:
                (other_ref, other_next)[quarter][start : start + head_dim] = state.astype(bf16)
            else:
                state_ref[at - 2 * size : at - 2 * size + head_dim] = state


def near_states(group, key_seq, value_seq, conv_kernel, feature_map):
    tok_count, width = key_seq.shape
    head_dim = feature_map.shape[0]
    size = width // GROUPS
    rows, firsts = shape((tok_count, size), bf16), shape((RIM, size), bf16)
    other = shape((size // 4, head_dim), bf16)
    return kernel_call(
        functools.partial(near_states_kernel, group),
        "near_states",
        [IN_VMEM] * 4,
        [IN_VMEM] * 7,
        [rows, rows, other, other, shape((size // 2, head_dim), f32), firsts, firsts],
        [pltpu.VMEM((BLOCK_HEADS, 2, TILE + tok_count, head_dim), f32)],
    )(key_seq, value_seq, conv_kernel, feature_map)


def whole_states_kernel(
    group, quarters, key_ref, value_ref, taps_ref, map_ref, core_rim, chip_rim, feat_ref, conv_ref, *rest
):
    (*states, scratch) = rest
    head_dim = map_ref.shape[0]
    width = key_ref.shape[1]
    size = width // (4 * GROUPS)
    back = taps_ref.shape[1] - 1
    for i, quarter in enumerate(quarters):
        for start in range(0, size, head_dim):
            natural = columns(quarter_start(quarter, width) + group * size + start, head_dim)
            at = i * size + start
            local = slice(at, at + head_dim)
            buffers = scratch.at[at // head_dim % scratch.shape[0]]
            taps = taps_ref[:, :, natural].astype(f32)
            rim = state_rim(core_rim, chip_rim, quarter, width, group * size + start, head_dim)
            key_conv = convolved(buffers.at[0], key_ref[:, natural].astype(f32), taps[1], rim, back)
            key_feat = features(key_conv, map_ref[...])
            feat_ref[:, local] = key_feat
            value_conv = convolved(buffers.at[1], value_ref[:, natural].astype(f32), taps[2], rim, 2 * back)
            conv_ref[:, local] = value_conv
            states[i][start : start + head_dim] = state_of(key_feat, value_conv).astype(states[i].dtype)


def whole_states(group, quarters, state_type, key_seq, value_seq, conv_kernel, feature_map, rims):
    tok_count, width = key_seq.shape
    head_dim = feature_map.shape[0]
    size = width // (4 * GROUPS)
    rows = shape((tok_count, len(quarters) * size), bf16)
    return kernel_call(
        functools.partial(whole_states_kernel, group, quarters),
        "whole_states",
        [IN_VMEM] * 6,
        [IN_VMEM] * (2 + len(quarters)),
        [rows, rows, *[shape((size, head_dim), state_type)] * len(quarters)],
        [pltpu.VMEM((BLOCK_HEADS, 2, TILE + tok_count, head_dim), f32)],
    )(key_seq, value_seq, conv_kernel, feature_map, *rims)


def first_rows_kernel(
    group, quarters, key_ref, value_ref, taps_ref, map_ref, core_rim, chip_rim, *rest
):
    (*state_refs, feat_ref, conv_ref, scratch) = rest
    head_dim = map_ref.shape[0]
    width = taps_ref.shape[2]
    back = taps_ref.shape[1] - 1
    size = width // (4 * GROUPS)
    for i, quarter in enumerate(quarters):
        here, there = slice(i * size, (i + 1) * size), slice(quarter * size, (quarter + 1) * size)
        natural = columns(quarter_start(quarter, width) + group * size, size)
        rim = state_rim(core_rim, chip_rim, quarter, width, group * size, size)
        conv = convolved(
            scratch.at[i, 0], key_ref[:, there].astype(f32), taps_ref[1, :, natural].astype(f32), rim, back
        )
        value_conv = convolved(
            scratch.at[i, 1], value_ref[:, there].astype(f32), taps_ref[2, :, natural].astype(f32), rim, 2 * back
        )
        feats = [features(conv[:, at : at + head_dim], map_ref[...]) for at in range(0, size, head_dim)]
        feat = jnp.concatenate(feats, axis=1)
        feat_ref[:, here], conv_ref[:, here] = feat, value_conv
        if state_refs:
            old_ref, *new_refs = state_refs
            new_refs[i][...] = old_ref[here] + first_states(feat, value_conv, head_dim, back)


def first_states(feat, value_conv, head_dim, back):
    row = lax.broadcasted_iota(jnp.int32, (RIM, head_dim), 0)
    states = []
    for at in range(0, feat.shape[1], head_dim):
        first = jnp.where(row < back, feat[:, at : at + head_dim].astype(f32), 0.0).astype(bf16)
        states.append(state_of(first, value_conv[:, at : at + head_dim]))
    return jnp.concatenate(states, axis=0)


def first_rows(group, quarters, key_first, value_first, conv_kernel, feature_map, rims, state=None):
    width = conv_kernel.shape[2]
    head_dim = feature_map.shape[0]
    size = width // (4 * GROUPS)
    rows = shape((RIM, len(quarters) * size), bf16)
    states = [] if state is None else [shape((size, head_dim), f32)] * len(quarters)
    operands = [key_first, value_first, conv_kernel, feature_map, *rims, *([] if state is None else [state])]
    body = functools.partial(first_rows_kernel, group, quarters)

    def reordered(*refs):
        sources, (feat_ref, conv_ref, *sums, scratch) = refs[:6], refs[len(operands) :]
        body(*sources, *refs[6 : len(operands)], *sums, feat_ref, conv_ref, scratch)

    return kernel_call(
        reordered,
        "first_rows",
        [IN_VMEM] * len(operands),
        [IN_VMEM] * (2 + len(states)),
        [rows, rows, *states],
        [pltpu.VMEM((len(quarters), 2, TILE + RIM, size), f32)],
    )(*operands)


def within_kernel(
    quarter, group, base, query_ref, taps_ref, map_ref, core_rim, chip_rim, key_ref, value_ref, *rest
):
    (*firsts, feat_ref, mixed_ref, scratch) = rest
    head_dim = map_ref.shape[0]
    tok_count, width = query_ref.shape
    size = width // (4 * GROUPS)
    causal = lax.broadcasted_iota(jnp.int32, (tok_count, tok_count), 0) >= lax.broadcasted_iota(
        jnp.int32, (tok_count, tok_count), 1
    )
    starts = range(0, size, head_dim)
    for start in starts:
        natural = columns(quarter_start(quarter, width) + group * size + start, head_dim)
        rim, end = query_rim(core_rim, chip_rim, quarter, width, group * size + start, head_dim)
        taps = taps_ref[0, :, natural].astype(f32)
        buffer = scratch.at[start // head_dim % scratch.shape[0]]
        conv = convolved(buffer, query_ref[:, natural].astype(f32), taps, rim, end * (taps_ref.shape[1] - 1))
        feat_ref[:, start : start + head_dim] = features(conv, map_ref[...])
    products = []
    for start in starts:
        local, at = slice(start, start + head_dim), slice(base + start, base + start + head_dim)
        first = quarter % 2 * size + start
        first = slice(first, first + head_dim)
        key, value = key_ref[:, at], value_ref[:, at]
        if firsts:
            key = jnp.concatenate([firsts[0][:, first], key[RIM:]], axis=0)
            value = jnp.concatenate([firsts[1][:, first], value[RIM:]], axis=0)
        scores = lax.dot_general(feat_ref[:, local], key, (((1,), (1,)), ((), ())), preferred_element_type=f32)
        products.append((local, jnp.where(causal, scores, 0.0).astype(bf16), value))
    for local, weights, value in products:
        mixed_ref[:, local] = jnp.dot(weights, value, preferred_element_type=f32)


def within_block(quarter, group, query_seq, conv_kernel, feature_map, rims, feat, conv, base, firsts):
    tok_count, width = query_seq.shape
    head_dim = feature_map.shape[0]
    size = width // (4 * GROUPS)
    operands = (query_seq, conv_kernel, feature_map, *rims, feat, conv, *firsts)
    return kernel_call(
        functools.partial(within_kernel, quarter, group, base),
        "within_block",
        [IN_VMEM] * len(operands),
        [IN_VMEM] * 2,
        [shape((tok_count, size), bf16), shape((tok_count, size), f32)],
        [pltpu.VMEM((BLOCK_HEADS, TILE + tok_count, head_dim), f32)],
    )(*operands)


def finish_kernel(pieces, before, gain_ref, *rest):
    count = sum(len(part) for part in pieces)
    prefixes, rest = rest[: len(pieces)], rest[len(pieces) :]
    feats, mixes = rest[:count], rest[count : 2 * count]
    out_ref, *token, rows, sems = rest[2 * count + before :]
    for ref in token:
        ref[...] = jnp.zeros(ref.shape, f32)
    head_dim = prefixes[0].shape[1]
    tok_count, size = feats[0].shape
    copies = []
    for prefix_ref, part in zip(prefixes, pieces):
        for at, (quarter, group) in enumerate(part):
            i = len(copies)
            natural = quarter_start(quarter, out_ref.shape[1]) + group * size
            for start in range(0, size, head_dim):
                cols = slice(start, start + head_dim)
                prefix = prefix_ref[at * size + start : at * size + start + head_dim]
                mixed = mixes[i][:, cols] + jnp.dot(feats[i][:, cols], prefix, preferred_element_type=f32)
                inverse_rms = lax.rsqrt(jnp.mean(mixed * mixed, axis=-1, keepdims=True) + 1e-06)
                gain = gain_ref[:, columns(natural + start, head_dim)]
                rows[i, :, cols] = (mixed * inverse_rms * gain).astype(bf16)
            copies.append(pltpu.make_async_copy(rows.at[i], out_ref.at[:, columns(natural, size)], sems.at[i]))
            copies[-1].start()
    for copy in copies:
        copy.wait()


def finish(pieces, mixed, prefixes, norm_gain, before, last=False):
    width = norm_gain.shape[1]
    every = [piece for part in pieces for piece in part]
    count = len(every)
    tok_count, size = mixed[every[0]][0].shape
    operands = [norm_gain, *prefixes, *(mixed[p][0] for p in every), *(mixed[p][1] for p in every)]
    in_specs = [IN_VMEM] * len(operands)
    aliases = {}
    if before is not None:
        aliases = {len(operands): 0}
        operands.append(in_hbm(before))
        in_specs.append(IN_PLACE)
    return kernel_call(
        functools.partial(finish_kernel, pieces, len(aliases)),
        "finish",
        in_specs,
        [IN_PLACE, IN_VMEM][: 1 if last else 2],
        [pltpu.HBM((tok_count, width), bf16), shape((TILE, 128), f32)][: 1 if last else 2],
        [pltpu.VMEM((count, tok_count, size), bf16), pltpu.SemaphoreType.DMA((count,))],
        aliases,
    )(*operands)[0]


def swapped(block, distance):
    return lax.ppermute(block, "seq", [(i, i ^ distance) for i in range(lax.axis_size("seq"))])


def passed_on(block):
    count = lax.axis_size("seq")
    route = {i: i + 1 for i in range(1, count - 2, 2)}
    route |= {i: i - 1 for i in range(4, count - 3, 2)}
    route |= {0: 1, 2: 0, count - 2: count - 1, count - 1: count - 3}
    return lax.ppermute(block, "seq", sorted(route.items()))


def mapped(name, function, outputs, *arrays):
    def body(*refs):
        values = [ref[...] for ref in refs[: len(arrays)]]
        for ref, value in zip(refs[len(arrays) :], function(lax.axis_index("seq"), *values)):
            ref[...] = value.astype(ref.dtype)

    columns = arrays[0].shape[1]
    return kernel_call(
        body,
        name,
        [IN_VMEM] * len(arrays),
        [IN_VMEM] * len(outputs),
        [shape((rows, columns), kind) for rows, kind in outputs],
    )(*arrays)


def on_device(query_seq, key_seq, value_seq, conv_kernel, feature_map, norm_gain):
    tok_count, width = query_seq.shape
    tap_count = conv_kernel.shape[1]
    head_dim = feature_map.shape[0]
    device_count = lax.axis_size("seq")
    assert tok_count == SPAN and width % (4 * GROUPS * head_dim) == 0
    assert device_count >= 8 and device_count & (device_count - 1) == 0
    groups = range(GROUPS)
    rows = width // (4 * GROUPS)
    gain = norm_gain.reshape(1, width)

    def of_core(device):
        return (device & 1) != 0

    def of_pair(device):
        return (device & 2) != 0

    Turn.last = ()
    packed = pack_rims(query_seq, key_seq, value_seq, tap_count, head_dim)
    rims = (swapped(packed, 1), passed_on(packed))
    mixed = {}
    fill = [(q, g) for q in (3, 2, 1, 0) for g in groups]
    total = len(fill)

    def score(share):
        while fill and total - len(fill) < round(share * total):
            q, g = fill.pop(0)
            first = ()
            if firsts[g]:
                first = firsts[g][q // 2]
            mixed[q, g] = within_block(q, g, query_seq, conv_kernel, feature_map, rims, *near[g][q], first)

    def chip_sums(device, paired, own, *arrived):
        states, firsts = [part.astype(f32) for part in arrived[:2]], arrived[2:]
        for first in firsts:
            more = first_states(first[:RIM], first[RIM:], head_dim, tap_count - 1)
            states = [states[0] + more[:rows], states[1] + more[rows:]]
        return paired + states[0], own + states[1], *states

    def pair_sums(device, own, arrived):
        total = own + arrived.astype(f32)
        return total, total

    def plane_sums(distance, device, total, *arrived):
        before, arrived = (0.0, arrived) if distance == 4 else (arrived[0], arrived[1:])
        upper = (device & distance) != 0
        if len(arrived) == 2:
            odd = (device & (distance // 2)) != 0
            mine, other = arrived
            arrived = (jnp.concatenate([jnp.where(odd, other, mine), jnp.where(odd, mine, other)], axis=0),)
        arrived = arrived[0].astype(f32)
        before = before + jnp.where(upper, arrived, 0.0)
        total = total + arrived
        give = total.astype(bf16)
        return total, before, jnp.where(upper, give[rows // 2 :], give[: rows // 2])

    def own_prefixes(distance, device, own, paired, cored, state, *step):
        before = plane_sums(distance, device, *step)[1] if step else jnp.zeros((rows, head_dim), f32)
        own_part = before + jnp.where(of_pair(device), paired.astype(f32), 0.0)
        others = before + jnp.where(of_pair(device), 0.0, own)
        return (
            others,
            own_part + jnp.where(of_core(device), cored.astype(f32), 0.0),
            own_part + jnp.where(of_core(device), 0.0, state),
        )

    def paired_prefixes(device, arrived, cored, state, own):
        arrived = arrived.astype(f32)
        give = arrived + jnp.where(of_core(device), 0.0, state)
        return (
            arrived + jnp.where(of_core(device), cored.astype(f32), 0.0),
            jnp.concatenate([give.astype(bf16), own], axis=0),
        )

    near, firsts, state_b, from_core, chip, arriving = [], [], [], [], [], []
    running, earlier, from_pair = [None] * GROUPS, [None] * GROUPS, [None] * GROUPS
    distance = 4

    def pair_step(g):
        from_pair[g] = arriving[g]
        if distance < device_count:
            running[g], give = mapped("pair_sums", pair_sums, [(rows, f32), (rows, bf16)], chip[g], from_pair[g])
            arriving[g] = (swapped(give, distance),)

    for g in groups:
        if g == 0:
            *kept, other, other_next, partial, key_first, value_first = near_states(
                g, key_seq, value_seq, conv_kernel, feature_map
            )
            near.append([(*kept, q * rows) for q in range(4)])
            others = [swapped(other, 1), swapped(other_next, 1)]
            first_a = first_rows(g, (0, 1), key_first, value_first, conv_kernel, feature_map, rims)
            others.append(swapped(jnp.concatenate(first_a, axis=0), 1))
            *first_b, paired, single = first_rows(
                g, (2, 3), key_first, value_first, conv_kernel, feature_map, rims, partial
            )
            firsts.append((first_a, first_b))
        else:
            *kept, other, other_next = whole_states(
                g, (0, 1), bf16, key_seq, value_seq, conv_kernel, feature_map, rims
            )
            others = [swapped(other, 1), swapped(other_next, 1)]
            near.append([(*kept, q * rows) for q in range(2)])
            *kept, paired, single = whole_states(
                g, (2, 3), f32, key_seq, value_seq, conv_kernel, feature_map, rims
            )
            near[g] += [(*kept, q * rows) for q in range(2)]
            firsts.append(None)
            pair_step(g - 1)
        state_b.append((paired, single))
        give, own, *others = mapped(
            "chip_sums", chip_sums, [(rows, bf16), (rows, f32), (rows, f32), (rows, f32)], paired, single, *others
        )
        from_core.append(others)
        chip.append(own)
        arriving.append(swapped(give, 2))
    score(0.375)
    pair_step(GROUPS - 1)
    while 2 * distance < device_count:
        for g in groups:
            before = [] if distance == 4 else [earlier[g]]
            running[g], earlier[g], give = mapped(
                "plane_sums",
                functools.partial(plane_sums, distance),
                [(rows, f32), (rows, f32), (rows // 2, bf16)],
                running[g],
                *before,
                *arriving[g],
            )
            arriving[g] = swapped(give, 2 * distance)
            if g == 0:
                score(0.5)
        for g in groups:
            (mine,) = mapped("halves", lambda device, half: (half,), [(rows // 2, bf16)], arriving[g])
            arriving[g] = (mine, swapped(mine, distance))
            if g == 0:
                score(0.75)
        distance *= 2

    back, own_give = [None] * GROUPS, [None] * GROUPS
    owns = []
    for g in groups:
        step = ()
        if distance < device_count:
            step = (running[g], *([] if distance == 4 else [earlier[g]]), *arriving[g])
        others, own, own_give[g] = mapped(
            "own_prefixes",
            functools.partial(own_prefixes, distance),
            [(rows, bf16)] * 3,
            chip[g],
            from_pair[g],
            from_core[g][1],
            state_b[g][1],
            *step,
        )
        back[g] = swapped(others, 2)
        owns.append(own)
        score(0.75 + (1 - 0.75) * (g + 1) / GROUPS)
    out = finish([[(3, g)] for g in groups], mixed, owns, gain, None)
    from_other = [None] * GROUPS
    for g in groups:
        prefix_2, give = mapped(
            "paired_prefixes",
            paired_prefixes,
            [(rows, bf16), (2 * rows, bf16)],
            back[g],
            from_core[g][0],
            state_b[g][0],
            own_give[g],
        )
        from_other[g] = swapped(give, 1)
        if g == 0:
            out = finish([[(2, g)]], mixed, [prefix_2], gain, out)
        else:
            pieces = [[(2, g)], [(0, g - 1), (1, g - 1)]]
            out = finish(pieces, mixed, [prefix_2, from_other[g - 1]], gain, out)
    return finish([[(0, g), (1, g)]], mixed, [from_other[g]], gain, out, last=True)


def solution(mesh):
    return jax.shard_map(
        on_device,
        mesh=mesh,
        in_specs=(
            P(("groups", "seq"), None),
            P(("groups", "seq"), None),
            P(("groups", "seq"), None),
            P(),
            P(),
            P(),
        ),
        out_specs=P(("groups", "seq"), None),
        check_vma=False,
    )
```

```python
import functools

import jax
import jax.numpy as jnp
from jax import lax
from jax.experimental import pallas as pl
from jax.experimental.pallas import tpu as pltpu
from jax.sharding import PartitionSpec as P

SPAN = 256
GROUPS = 2
BLOCK_HEADS = 6
RIM = 16
TILE = 8
VMEM_BYTES = 12 * 1024 * 1024
f32, bf16 = jnp.float32, jnp.bfloat16
IN_VMEM = pl.BlockSpec(memory_space=pltpu.VMEM)
IN_PLACE = pl.BlockSpec(memory_space=pl.ANY)
LIGHT = pl.CostEstimate(flops=1024, bytes_accessed=1024, transcendentals=0)


def in_hbm(array):
    return pltpu.with_memory_space_constraint(array, pltpu.HBM)


class Turn:
    last = ()


def kernel_call(body, name, in_specs, out_specs, out_shape, scratch=(), aliases=None):
    count = len(in_specs)

    def call(*operands):
        before = Turn.last

        def ordered(*refs):
            body(*refs[:count], *refs[count + len(before) :])

        results = pl.pallas_call(
            ordered,
            in_specs=[*in_specs, *[IN_PLACE] * len(before)],
            out_specs=out_specs,
            out_shape=out_shape,
            scratch_shapes=list(scratch),
            input_output_aliases=aliases or {},
            compiler_params=pltpu.CompilerParams(vmem_limit_bytes=VMEM_BYTES),
            cost_estimate=LIGHT,
            name=name,
        )(*operands, *before)
        Turn.last = (results[-1] if isinstance(results, (list, tuple)) else results,)
        return results

    return call


def shape(dims, kind):
    return jax.ShapeDtypeStruct(dims, kind)


def quarter_start(quarter, width):
    device = lax.axis_index("seq")
    core = (device & 1) ^ int(quarter < 2)
    pair = ((device >> 1) & 1) ^ int(quarter % 2 == 0)
    return (2 * core + pair) * (width // 4)


def columns(start, size):
    return pl.ds(pl.multiple_of(start, 128), size)


def block_heads(heads):
    return max(n for n in range(1, BLOCK_HEADS + 1) if heads % n == 0)


def pack_kernel(tap_count, head_dim, query_ref, key_ref, value_ref, rim_ref, tails, sems):
    back = tap_count - 1
    tok_count, width = query_ref.shape
    rows = pl.ds(tok_count - RIM, RIM)
    copies = [
        pltpu.make_async_copy(ref.at[rows], tails.at[i], sems.at[i])
        for i, ref in enumerate((key_ref, value_ref, query_ref))
    ]
    for copy in copies:
        copy.start()
    for copy in copies:
        copy.wait()
    key_tail, value_tail, query_tail = (tails[i].astype(f32)[-TILE:] for i in range(3))

    def paired(first, second):
        row = lax.broadcasted_iota(jnp.int32, first.shape, 0)
        return jnp.where(row < back, pltpu.roll(first, back, 0), pltpu.roll(second, 2 * back, 0))

    halves = []
    for start in (0, width // 2):
        tiles = [paired(key_tail[:, start : start + width // 2], value_tail[:, start : start + width // 2])]
        for at in range(start, start + width // 2, 2 * head_dim):
            heads = query_tail[:, at : at + 2 * head_dim]
            tiles.append(paired(heads[:, :head_dim], heads[:, head_dim:]))
        halves.append(jnp.concatenate(tiles, axis=1))
    rim_ref[...] = jnp.concatenate(halves, axis=0).astype(bf16)


def pack_rims(query_seq, key_seq, value_seq, tap_count, head_dim):
    width = query_seq.shape[1]
    return kernel_call(
        functools.partial(pack_kernel, tap_count, head_dim),
        "pack_rims",
        [IN_PLACE] * 3,
        IN_VMEM,
        shape((RIM, 3 * width // 4), bf16),
        [pltpu.VMEM((3, RIM, width), bf16), pltpu.SemaphoreType.DMA((3,))],
    )(in_hbm(query_seq), in_hbm(key_seq), in_hbm(value_seq))


def rim_tile(core_rim, chip_rim, quarter, start, size):
    device = lax.axis_index("seq")
    upper = ((device & 1) ^ int(quarter < 2)) != 0
    cols = columns(start, size)
    from_core, from_chip = (ref[:, cols].astype(f32) for ref in (core_rim, chip_rim))
    rim = jnp.where((device & 1) != 0, from_core, jnp.where(device > 0, from_chip, 0.0))
    return jnp.where(upper, rim[TILE:], rim[:TILE])


def state_rim(core_rim, chip_rim, quarter, width, start, size):
    pair = ((lax.axis_index("seq") >> 1) & 1) ^ int(quarter % 2 == 0)
    return rim_tile(core_rim, chip_rim, quarter, pair * (width // 4) + start, size)


def query_rim(core_rim, chip_rim, quarter, width, start, head_dim):
    pair = ((lax.axis_index("seq") >> 1) & 1) ^ int(quarter % 2 == 0)
    head = start // head_dim
    at = width // 2 + pair * (width // 8) + head // 2 * head_dim
    return rim_tile(core_rim, chip_rim, quarter, at, head_dim), head % 2 + 1


def convolved(scratch, rows, taps, rim=None, rim_end=0):
    length = rows.shape[0]
    if rim is None:
        scratch[:TILE] = jnp.zeros((TILE, rows.shape[1]), f32)
    else:
        scratch[:TILE] = pltpu.roll(rim, (-rim_end) % TILE, 0)
    scratch[TILE : TILE + length] = rows
    total = taps[0:1] * rows
    for offset in range(1, taps.shape[0]):
        total = total + taps[offset : offset + 1] * scratch[TILE - offset : TILE - offset + length]
    return total.astype(bf16)


def features(conv_rows, feature_map):
    projected = jnp.dot(conv_rows, feature_map, preferred_element_type=f32)
    return jnp.where(projected > 0, projected + 1.0, jnp.exp(projected)).astype(bf16)


def state_of(key_feat, value_conv):
    return lax.dot_general(
        key_feat, value_conv, (((0,), (0,)), ((), ())), preferred_element_type=f32
    )


def near_states_kernel(
    group, quarters, key_ref, value_ref, taps_ref, map_ref, feat_ref, conv_ref, key_first, value_first, *rest
):
    (*states, scratch) = rest
    head_dim = map_ref.shape[0]
    width = key_ref.shape[1]
    size = width // (4 * GROUPS)
    back = taps_ref.shape[1] - 1
    row = lax.broadcasted_iota(jnp.int32, (RIM, head_dim), 0)
    for i, quarter in enumerate(quarters):
        for start in range(0, size, head_dim):
            natural = columns(quarter_start(quarter, width) + group * size + start, head_dim)
            at = i * size + start
            local = slice(at, at + head_dim)
            buffers = scratch.at[at // head_dim % scratch.shape[0]]
            key, value = key_ref[:, natural], value_ref[:, natural]
            key_first[:, local] = key[:RIM]
            value_first[:, local] = value[:RIM]
            key_conv = convolved(buffers.at[0], key.astype(f32), taps_ref[1, :, natural].astype(f32))
            key_feat = features(key_conv, map_ref[...])
            feat_ref[:, local] = key_feat
            value_conv = convolved(buffers.at[1], value.astype(f32), taps_ref[2, :, natural].astype(f32))
            conv_ref[:, local] = value_conv
            later = jnp.where(row < back, 0.0, key_feat[:RIM].astype(f32)).astype(bf16)
            key_feat = jnp.concatenate([later, key_feat[RIM:]], axis=0)
            state = state_of(key_feat, value_conv)
            states[i][start : start + head_dim] = state.astype(states[i].dtype)


def near_states(group, quarters, state_type, key_seq, value_seq, conv_kernel, feature_map):
    tok_count, width = key_seq.shape
    head_dim = feature_map.shape[0]
    size = width // (4 * GROUPS)
    count = len(quarters)
    rows, firsts = shape((tok_count, count * size), bf16), shape((RIM, count * size), bf16)
    return kernel_call(
        functools.partial(near_states_kernel, group, quarters),
        "near_states",
        [IN_VMEM] * 4,
        [IN_VMEM] * (4 + count),
        [rows, rows, firsts, firsts, *[shape((size, head_dim), state_type)] * count],
        [pltpu.VMEM((BLOCK_HEADS, 2, TILE + tok_count, head_dim), f32)],
    )(key_seq, value_seq, conv_kernel, feature_map)


def whole_states_kernel(
    group, quarters, key_ref, value_ref, taps_ref, map_ref, core_rim, chip_rim, feat_ref, conv_ref, *rest
):
    (*states, scratch) = rest
    head_dim = map_ref.shape[0]
    width = key_ref.shape[1]
    size = width // (4 * GROUPS)
    back = taps_ref.shape[1] - 1
    for i, quarter in enumerate(quarters):
        for start in range(0, size, head_dim):
            natural = columns(quarter_start(quarter, width) + group * size + start, head_dim)
            at = i * size + start
            local = slice(at, at + head_dim)
            buffers = scratch.at[at // head_dim % scratch.shape[0]]
            taps = taps_ref[:, :, natural].astype(f32)
            rim = state_rim(core_rim, chip_rim, quarter, width, group * size + start, head_dim)
            key_conv = convolved(buffers.at[0], key_ref[:, natural].astype(f32), taps[1], rim, back)
            key_feat = features(key_conv, map_ref[...])
            feat_ref[:, local] = key_feat
            value_conv = convolved(buffers.at[1], value_ref[:, natural].astype(f32), taps[2], rim, 2 * back)
            conv_ref[:, local] = value_conv
            states[i][start : start + head_dim] = state_of(key_feat, value_conv).astype(states[i].dtype)


def whole_states(group, quarters, state_type, key_seq, value_seq, conv_kernel, feature_map, rims):
    tok_count, width = key_seq.shape
    head_dim = feature_map.shape[0]
    size = width // (4 * GROUPS)
    rows = shape((tok_count, len(quarters) * size), bf16)
    return kernel_call(
        functools.partial(whole_states_kernel, group, quarters),
        "whole_states",
        [IN_VMEM] * 6,
        [IN_VMEM] * (2 + len(quarters)),
        [rows, rows, *[shape((size, head_dim), state_type)] * len(quarters)],
        [pltpu.VMEM((BLOCK_HEADS, 2, TILE + tok_count, head_dim), f32)],
    )(key_seq, value_seq, conv_kernel, feature_map, *rims)


def first_rows_kernel(
    group, quarters, key_ref, value_ref, taps_ref, map_ref, core_rim, chip_rim, *rest
):
    (*state_refs, feat_ref, conv_ref, scratch) = rest
    head_dim = map_ref.shape[0]
    width = taps_ref.shape[2]
    back = taps_ref.shape[1] - 1
    size = width // (4 * GROUPS)
    for i, quarter in enumerate(quarters):
        here = there = slice(i * size, (i + 1) * size)
        natural = columns(quarter_start(quarter, width) + group * size, size)
        rim = state_rim(core_rim, chip_rim, quarter, width, group * size, size)
        conv = convolved(
            scratch.at[i, 0], key_ref[:, there].astype(f32), taps_ref[1, :, natural].astype(f32), rim, back
        )
        value_conv = convolved(
            scratch.at[i, 1], value_ref[:, there].astype(f32), taps_ref[2, :, natural].astype(f32), rim, 2 * back
        )
        feats = [features(conv[:, at : at + head_dim], map_ref[...]) for at in range(0, size, head_dim)]
        feat = jnp.concatenate(feats, axis=1)
        feat_ref[:, here], conv_ref[:, here] = feat, value_conv
        if state_refs:
            old_refs, new_refs = state_refs[: len(quarters)], state_refs[len(quarters) :]
            new_refs[i][...] = old_refs[i][...] + first_states(feat, value_conv, head_dim, back)


def first_states(feat, value_conv, head_dim, back):
    row = lax.broadcasted_iota(jnp.int32, (RIM, head_dim), 0)
    states = []
    for at in range(0, feat.shape[1], head_dim):
        first = jnp.where(row < back, feat[:, at : at + head_dim].astype(f32), 0.0).astype(bf16)
        states.append(state_of(first, value_conv[:, at : at + head_dim]))
    return jnp.concatenate(states, axis=0)


def first_rows(group, quarters, key_first, value_first, conv_kernel, feature_map, rims, before=()):
    width = conv_kernel.shape[2]
    head_dim = feature_map.shape[0]
    size = width // (4 * GROUPS)
    rows = shape((RIM, len(quarters) * size), bf16)
    more = [shape((size, head_dim), f32)] * len(before) if before else [rows]
    operands = [key_first, value_first, conv_kernel, feature_map, *rims, *before]
    body = functools.partial(first_rows_kernel, group, quarters)

    def reordered(*refs):
        sources, (feat_ref, conv_ref, *more, scratch) = refs[:6], refs[len(operands) :]
        if before:
            body(*sources, *refs[6 : len(operands)], *more, feat_ref, conv_ref, scratch)
        else:
            body(*sources, feat_ref, conv_ref, scratch)
            tiles = [ref[...].astype(f32)[:TILE] for ref in (feat_ref, conv_ref)]
            more[0][...] = jnp.concatenate(tiles, axis=0).astype(bf16)

    return kernel_call(
        reordered,
        "first_rows",
        [IN_VMEM] * len(operands),
        [IN_VMEM] * (2 + len(more)),
        [rows, rows, *more],
        [pltpu.VMEM((len(quarters), 2, TILE + RIM, size), f32)],
    )(*operands)


def within_kernel(
    quarter, group, base, query_ref, taps_ref, map_ref, core_rim, chip_rim, key_ref, value_ref, *rest
):
    (*firsts, feat_ref, mixed_ref, scratch) = rest
    head_dim = map_ref.shape[0]
    tok_count, width = query_ref.shape
    size = width // (4 * GROUPS)
    causal = lax.broadcasted_iota(jnp.int32, (tok_count, tok_count), 0) >= lax.broadcasted_iota(
        jnp.int32, (tok_count, tok_count), 1
    )
    starts = range(0, size, head_dim)
    for start in starts:
        natural = columns(quarter_start(quarter, width) + group * size + start, head_dim)
        rim, end = query_rim(core_rim, chip_rim, quarter, width, group * size + start, head_dim)
        taps = taps_ref[0, :, natural].astype(f32)
        buffer = scratch.at[start // head_dim % scratch.shape[0]]
        conv = convolved(buffer, query_ref[:, natural].astype(f32), taps, rim, end * (taps_ref.shape[1] - 1))
        feat_ref[:, start : start + head_dim] = features(conv, map_ref[...])
    products = []
    for start in starts:
        local, at = slice(start, start + head_dim), slice(base + start, base + start + head_dim)
        first = quarter % 2 * size + start
        first = slice(first, first + head_dim)
        key, value = key_ref[:, at], value_ref[:, at]
        if firsts:
            key = jnp.concatenate([firsts[0][:, first], key[RIM:]], axis=0)
            value = jnp.concatenate([firsts[1][:, first], value[RIM:]], axis=0)
        scores = lax.dot_general(feat_ref[:, local], key, (((1,), (1,)), ((), ())), preferred_element_type=f32)
        products.append((local, jnp.where(causal, scores, 0.0).astype(bf16), value))
    for local, weights, value in products:
        mixed_ref[:, local] = jnp.dot(weights, value, preferred_element_type=f32)


def within_block(quarter, group, query_seq, conv_kernel, feature_map, rims, feat, conv, base, firsts):
    tok_count, width = query_seq.shape
    head_dim = feature_map.shape[0]
    size = width // (4 * GROUPS)
    operands = (query_seq, conv_kernel, feature_map, *rims, feat, conv, *firsts)
    return kernel_call(
        functools.partial(within_kernel, quarter, group, base),
        "within_block",
        [IN_VMEM] * len(operands),
        [IN_VMEM] * 2,
        [shape((tok_count, size), bf16), shape((tok_count, size), f32)],
        [pltpu.VMEM((BLOCK_HEADS, TILE + tok_count, head_dim), f32)],
    )(*operands)


def finish_kernel(pieces, before, gain_ref, *rest):
    count = sum(len(part) for part in pieces)
    prefixes, rest = rest[: len(pieces)], rest[len(pieces) :]
    feats, mixes = rest[:count], rest[count : 2 * count]
    out_ref, *token, rows, sems = rest[2 * count + before :]
    for ref in token:
        ref[...] = jnp.zeros(ref.shape, f32)
    head_dim = prefixes[0].shape[1]
    tok_count, size = feats[0].shape
    copies = []
    for prefix_ref, part in zip(prefixes, pieces):
        for at, (quarter, group) in enumerate(part):
            i = len(copies)
            natural = quarter_start(quarter, out_ref.shape[1]) + group * size
            for start in range(0, size, head_dim):
                cols = slice(start, start + head_dim)
                prefix = prefix_ref[at * size + start : at * size + start + head_dim]
                mixed = mixes[i][:, cols] + jnp.dot(feats[i][:, cols], prefix, preferred_element_type=f32)
                inverse_rms = lax.rsqrt(jnp.mean(mixed * mixed, axis=-1, keepdims=True) + 1e-06)
                gain = gain_ref[:, columns(natural + start, head_dim)]
                rows[i, :, cols] = (mixed * inverse_rms * gain).astype(bf16)
            copies.append(pltpu.make_async_copy(rows.at[i], out_ref.at[:, columns(natural, size)], sems.at[i]))
            copies[-1].start()
    for copy in copies:
        copy.wait()


def finish(pieces, mixed, prefixes, norm_gain, before, last=False):
    width = norm_gain.shape[1]
    every = [piece for part in pieces for piece in part]
    count = len(every)
    tok_count, size = mixed[every[0]][0].shape
    operands = [norm_gain, *prefixes, *(mixed[p][0] for p in every), *(mixed[p][1] for p in every)]
    in_specs = [IN_VMEM] * len(operands)
    aliases = {}
    if before is not None:
        aliases = {len(operands): 0}
        operands.append(in_hbm(before))
        in_specs.append(IN_PLACE)
    return kernel_call(
        functools.partial(finish_kernel, pieces, len(aliases)),
        "finish",
        in_specs,
        [IN_PLACE, IN_VMEM][: 1 if last else 2],
        [pltpu.HBM((tok_count, width), bf16), shape((TILE, 128), f32)][: 1 if last else 2],
        [pltpu.VMEM((count, tok_count, size), bf16), pltpu.SemaphoreType.DMA((count,))],
        aliases,
    )(*operands)[0]


def swapped(block, distance):
    return lax.ppermute(block, "seq", [(i, i ^ distance) for i in range(lax.axis_size("seq"))])


def passed_on(block):
    count = lax.axis_size("seq")
    route = {i: i + 1 for i in range(1, count - 2, 2)}
    route |= {i: i - 1 for i in range(4, count - 3, 2)}
    route |= {0: 1, 2: 0, count - 2: count - 1, count - 1: count - 3}
    return lax.ppermute(block, "seq", sorted(route.items()))


def mapped(name, function, outputs, *arrays):
    def body(*refs):
        values = [ref[...] for ref in refs[: len(arrays)]]
        for ref, value in zip(refs[len(arrays) :], function(lax.axis_index("seq"), *values)):
            ref[...] = value.astype(ref.dtype)

    columns = arrays[0].shape[1]
    return kernel_call(
        body,
        name,
        [IN_VMEM] * len(arrays),
        [IN_VMEM] * len(outputs),
        [shape((rows, columns), kind) for rows, kind in outputs],
    )(*arrays)


def on_device(query_seq, key_seq, value_seq, conv_kernel, feature_map, norm_gain):
    tok_count, width = query_seq.shape
    tap_count = conv_kernel.shape[1]
    head_dim = feature_map.shape[0]
    device_count = lax.axis_size("seq")
    assert tok_count == SPAN and width % (4 * GROUPS * head_dim) == 0
    assert device_count >= 8 and device_count & (device_count - 1) == 0
    groups = range(GROUPS)
    rows = width // (4 * GROUPS)
    gain = norm_gain.reshape(1, width)

    def of_core(device):
        return (device & 1) != 0

    def of_pair(device):
        return (device & 2) != 0

    Turn.last = ()
    packed = pack_rims(query_seq, key_seq, value_seq, tap_count, head_dim)
    rims = (swapped(packed, 1), passed_on(packed))
    mixed = {}
    fill = [(q, g) for q in (3, 2, 1, 0) for g in groups]
    total = len(fill)

    def score(share):
        while fill and total - len(fill) < round(share * total):
            q, g = fill.pop(0)
            first = ()
            if firsts[g]:
                first = firsts[g][q // 2]
            mixed[q, g] = within_block(q, g, query_seq, conv_kernel, feature_map, rims, *near[g][q], first)

    def chip_sums(device, paired, own, *arrived):
        states, firsts = [part.astype(f32) for part in arrived[:2]], arrived[2:]
        for first in firsts:
            first = first.astype(f32)
            blank = jnp.zeros((TILE, first.shape[1]), f32)
            first = [jnp.concatenate([part, blank], axis=0).astype(bf16) for part in (first[:TILE], first[TILE:])]
            more = first_states(*first, head_dim, tap_count - 1)
            states = [states[0] + more[:rows], states[1] + more[rows:]]
        return paired + states[0], own + states[1], *states

    def pair_sums(device, own, arrived):
        total = own + arrived.astype(f32)
        return total, total

    def plane_sums(distance, device, total, *arrived):
        before, arrived = (0.0, arrived) if distance == 4 else (arrived[0], arrived[1:])
        upper = (device & distance) != 0
        if len(arrived) == 2:
            odd = (device & (distance // 2)) != 0
            mine, other = arrived
            arrived = (jnp.concatenate([jnp.where(odd, other, mine), jnp.where(odd, mine, other)], axis=0),)
        arrived = arrived[0].astype(f32)
        before = before + jnp.where(upper, arrived, 0.0)
        total = total + arrived
        give = total.astype(bf16)
        return total, before, jnp.where(upper, give[rows // 2 :], give[: rows // 2])

    def back_prefixes(distance, device, own, *step):
        before = plane_sums(distance, device, *step)[1] if step else jnp.zeros((rows, head_dim), f32)
        return before, before + jnp.where(of_pair(device), 0.0, own)

    def own_prefixes(device, before, paired, cored, state):
        before = before + jnp.where(of_pair(device), paired.astype(f32), 0.0)
        return (
            before + jnp.where(of_core(device), cored.astype(f32), 0.0),
            before + jnp.where(of_core(device), 0.0, state),
        )

    def paired_prefixes(device, arrived, cored, state, own):
        arrived = arrived.astype(f32)
        give = arrived + jnp.where(of_core(device), 0.0, state)
        return (
            arrived + jnp.where(of_core(device), cored.astype(f32), 0.0),
            jnp.concatenate([give.astype(bf16), own], axis=0),
        )

    near, firsts, state_b, from_core, chip, arriving = [], [], [], [], [], []
    running, earlier, from_pair = [None] * GROUPS, [None] * GROUPS, [None] * GROUPS
    distance = 4

    def pair_step(g):
        from_pair[g] = arriving[g]
        if distance < device_count:
            running[g], give = mapped("pair_sums", pair_sums, [(rows, f32), (rows, bf16)], chip[g], from_pair[g])
            arriving[g] = (swapped(give, distance),)

    for g in groups:
        if g == 0:
            near.append([])
            *kept, key_first, value_first, other, other_next = near_states(
                g, (0, 1), bf16, key_seq, value_seq, conv_kernel, feature_map
            )
            near[g] += [(*kept, q * rows) for q in range(2)]
            others = [swapped(other, 1), swapped(other_next, 1)]
            *kept, key_next, value_next, paired, single = near_states(
                g, (2, 3), f32, key_seq, value_seq, conv_kernel, feature_map
            )
            near[g] += [(*kept, q * rows) for q in range(2)]
            *first_a, first_tiles = first_rows(g, (0, 1), key_first, value_first, conv_kernel, feature_map, rims)
            others.append(swapped(first_tiles, 1))
            *first_b, paired, single = first_rows(
                g, (2, 3), key_next, value_next, conv_kernel, feature_map, rims, (paired, single)
            )
            firsts.append((first_a, first_b))
        else:
            *kept, other, other_next = whole_states(
                g, (0, 1), bf16, key_seq, value_seq, conv_kernel, feature_map, rims
            )
            others = [swapped(other, 1), swapped(other_next, 1)]
            near.append([(*kept, q * rows) for q in range(2)])
            *kept, paired, single = whole_states(
                g, (2, 3), f32, key_seq, value_seq, conv_kernel, feature_map, rims
            )
            near[g] += [(*kept, q * rows) for q in range(2)]
            firsts.append(None)
            pair_step(g - 1)
        state_b.append((paired, single))
        give, own, *others = mapped(
            "chip_sums", chip_sums, [(rows, bf16), (rows, f32), (rows, f32), (rows, f32)], paired, single, *others
        )
        from_core.append(others)
        chip.append(own)
        arriving.append(swapped(give, 2))
    score(0.375)
    pair_step(GROUPS - 1)
    while 2 * distance < device_count:
        for g in groups:
            before = [] if distance == 4 else [earlier[g]]
            running[g], earlier[g], give = mapped(
                "plane_sums",
                functools.partial(plane_sums, distance),
                [(rows, f32), (rows, f32), (rows // 2, bf16)],
                running[g],
                *before,
                *arriving[g],
            )
            arriving[g] = swapped(give, 2 * distance)
            if g == 0:
                score(0.5)
        for g in groups:
            (mine,) = mapped("halves", lambda device, half: (half,), [(rows // 2, bf16)], arriving[g])
            arriving[g] = (mine, swapped(mine, distance))
            if g == 0:
                score(0.75)
        distance *= 2

    back, own_give = [None] * GROUPS, [None] * GROUPS
    owns = []
    for g in groups:
        step = ()
        if distance < device_count:
            step = (running[g], *([] if distance == 4 else [earlier[g]]), *arriving[g])
        before, give = mapped(
            "back_prefixes",
            functools.partial(back_prefixes, distance),
            [(rows, f32), (rows, bf16)],
            chip[g],
            *step,
        )
        back[g] = swapped(give, 2)
        own, own_give[g] = mapped(
            "own_prefixes",
            own_prefixes,
            [(rows, bf16)] * 2,
            before,
            from_pair[g],
            from_core[g][1],
            state_b[g][1],
        )
        owns.append(own)
        score(0.75 + (1 - 0.75) * (g + 1) / GROUPS)
    out = finish([[(3, g)] for g in groups], mixed, owns, gain, None)
    from_other = [None] * GROUPS
    for g in groups:
        prefix_2, give = mapped(
            "paired_prefixes",
            paired_prefixes,
            [(rows, bf16), (2 * rows, bf16)],
            back[g],
            from_core[g][0],
            state_b[g][0],
            own_give[g],
        )
        from_other[g] = swapped(give, 1)
        if g == 0:
            out = finish([[(2, g)]], mixed, [prefix_2], gain, out)
        else:
            pieces = [[(2, g)], [(0, g - 1), (1, g - 1)]]
            out = finish(pieces, mixed, [prefix_2, from_other[g - 1]], gain, out)
    return finish([[(0, g), (1, g)]], mixed, [from_other[g]], gain, out, last=True)


def solution(mesh):
    return jax.shard_map(
        on_device,
        mesh=mesh,
        in_specs=(
            P(("groups", "seq"), None),
            P(("groups", "seq"), None),
            P(("groups", "seq"), None),
            P(),
            P(),
            P(),
        ),
        out_specs=P(("groups", "seq"), None),
        check_vma=False,
    )
```

```python
import functools

import jax
import jax.numpy as jnp
from jax import lax
from jax.experimental import pallas as pl
from jax.experimental.pallas import tpu as pltpu
from jax.sharding import PartitionSpec as P

SPAN = 256
GROUPS = 2
BLOCK_HEADS = 6
RIM = 16
TILE = 8
VMEM_BYTES = 12 * 1024 * 1024
f32, bf16 = jnp.float32, jnp.bfloat16
IN_VMEM = pl.BlockSpec(memory_space=pltpu.VMEM)
IN_PLACE = pl.BlockSpec(memory_space=pl.ANY)
LIGHT = pl.CostEstimate(flops=1024, bytes_accessed=1024, transcendentals=0)


def in_hbm(array):
    return pltpu.with_memory_space_constraint(array, pltpu.HBM)


class Turn:
    last = ()


def kernel_call(body, name, in_specs, out_specs, out_shape, scratch=(), aliases=None):
    count = len(in_specs)

    def call(*operands):
        before = Turn.last

        def ordered(*refs):
            body(*refs[:count], *refs[count + len(before) :])

        results = pl.pallas_call(
            ordered,
            in_specs=[*in_specs, *[IN_PLACE] * len(before)],
            out_specs=out_specs,
            out_shape=out_shape,
            scratch_shapes=list(scratch),
            input_output_aliases=aliases or {},
            compiler_params=pltpu.CompilerParams(vmem_limit_bytes=VMEM_BYTES),
            cost_estimate=LIGHT,
            name=name,
        )(*operands, *before)
        Turn.last = (results[-1] if isinstance(results, (list, tuple)) else results,)
        return results

    return call


def shape(dims, kind):
    return jax.ShapeDtypeStruct(dims, kind)


def quarter_start(quarter, width):
    device = lax.axis_index("seq")
    core = (device & 1) ^ int(quarter < 2)
    pair = ((device >> 1) & 1) ^ int(quarter % 2 == 0)
    return (2 * core + pair) * (width // 4)


def columns(start, size):
    return pl.ds(pl.multiple_of(start, 128), size)


def block_heads(heads):
    return max(n for n in range(1, BLOCK_HEADS + 1) if heads % n == 0)


def pack_kernel(tap_count, head_dim, query_ref, key_ref, value_ref, rim_ref, tails, sems):
    back = tap_count - 1
    tok_count, width = query_ref.shape
    rows = pl.ds(tok_count - RIM, RIM)
    copies = [
        pltpu.make_async_copy(ref.at[rows], tails.at[i], sems.at[i])
        for i, ref in enumerate((key_ref, value_ref, query_ref))
    ]
    for copy in copies:
        copy.start()
    for copy in copies:
        copy.wait()
    key_tail, value_tail, query_tail = (tails[i].astype(f32)[-TILE:] for i in range(3))

    def paired(first, second):
        row = lax.broadcasted_iota(jnp.int32, first.shape, 0)
        return jnp.where(row < back, pltpu.roll(first, back, 0), pltpu.roll(second, 2 * back, 0))

    halves = []
    for start in (0, width // 2):
        tiles = [paired(key_tail[:, start : start + width // 2], value_tail[:, start : start + width // 2])]
        for at in range(start, start + width // 2, 2 * head_dim):
            heads = query_tail[:, at : at + 2 * head_dim]
            tiles.append(paired(heads[:, :head_dim], heads[:, head_dim:]))
        halves.append(jnp.concatenate(tiles, axis=1))
    rim_ref[...] = jnp.concatenate(halves, axis=0).astype(bf16)


def pack_rims(query_seq, key_seq, value_seq, tap_count, head_dim):
    width = query_seq.shape[1]
    return kernel_call(
        functools.partial(pack_kernel, tap_count, head_dim),
        "pack_rims",
        [IN_PLACE] * 3,
        IN_VMEM,
        shape((RIM, 3 * width // 4), bf16),
        [pltpu.VMEM((3, RIM, width), bf16), pltpu.SemaphoreType.DMA((3,))],
    )(in_hbm(query_seq), in_hbm(key_seq), in_hbm(value_seq))


def rim_tile(core_rim, chip_rim, quarter, start, size):
    device = lax.axis_index("seq")
    upper = ((device & 1) ^ int(quarter < 2)) != 0
    cols = columns(start, size)
    from_core, from_chip = (ref[:, cols].astype(f32) for ref in (core_rim, chip_rim))
    rim = jnp.where((device & 1) != 0, from_core, jnp.where(device > 0, from_chip, 0.0))
    return jnp.where(upper, rim[TILE:], rim[:TILE])


def state_rim(core_rim, chip_rim, quarter, width, start, size):
    pair = ((lax.axis_index("seq") >> 1) & 1) ^ int(quarter % 2 == 0)
    return rim_tile(core_rim, chip_rim, quarter, pair * (width // 4) + start, size)


def query_rim(core_rim, chip_rim, quarter, width, start, head_dim):
    pair = ((lax.axis_index("seq") >> 1) & 1) ^ int(quarter % 2 == 0)
    head = start // head_dim
    at = width // 2 + pair * (width // 8) + head // 2 * head_dim
    return rim_tile(core_rim, chip_rim, quarter, at, head_dim), head % 2 + 1


def convolved(scratch, rows, taps, rim=None, rim_end=0):
    length = rows.shape[0]
    if rim is None:
        scratch[:TILE] = jnp.zeros((TILE, rows.shape[1]), f32)
    else:
        scratch[:TILE] = pltpu.roll(rim, (-rim_end) % TILE, 0)
    scratch[TILE : TILE + length] = rows
    total = taps[0:1] * rows
    for offset in range(1, taps.shape[0]):
        total = total + taps[offset : offset + 1] * scratch[TILE - offset : TILE - offset + length]
    return total.astype(bf16)


def features(conv_rows, feature_map):
    projected = jnp.dot(conv_rows, feature_map, preferred_element_type=f32)
    return jnp.where(projected > 0, projected + 1.0, jnp.exp(projected)).astype(bf16)


def state_of(key_feat, value_conv):
    return lax.dot_general(
        key_feat, value_conv, (((0,), (0,)), ((), ())), preferred_element_type=f32
    )


def near_states_kernel(
    group, quarters, key_ref, value_ref, taps_ref, map_ref, feat_ref, conv_ref, key_first, value_first, *rest
):
    (*states, scratch) = rest
    head_dim = map_ref.shape[0]
    width = key_ref.shape[1]
    size = width // (4 * GROUPS)
    back = taps_ref.shape[1] - 1
    row = lax.broadcasted_iota(jnp.int32, (RIM, head_dim), 0)
    for i, quarter in enumerate(quarters):
        for start in range(0, size, head_dim):
            natural = columns(quarter_start(quarter, width) + group * size + start, head_dim)
            at = i * size + start
            local = slice(at, at + head_dim)
            buffers = scratch.at[at // head_dim % scratch.shape[0]]
            key, value = key_ref[:, natural], value_ref[:, natural]
            key_first[:, local] = key[:RIM]
            value_first[:, local] = value[:RIM]
            key_conv = convolved(buffers.at[0], key.astype(f32), taps_ref[1, :, natural].astype(f32))
            key_feat = features(key_conv, map_ref[...])
            feat_ref[:, local] = key_feat
            value_conv = convolved(buffers.at[1], value.astype(f32), taps_ref[2, :, natural].astype(f32))
            conv_ref[:, local] = value_conv
            later = jnp.where(row < back, 0.0, key_feat[:RIM].astype(f32)).astype(bf16)
            key_feat = jnp.concatenate([later, key_feat[RIM:]], axis=0)
            state = state_of(key_feat, value_conv)
            states[i][start : start + head_dim] = state.astype(states[i].dtype)


def near_states(group, quarters, state_type, key_seq, value_seq, conv_kernel, feature_map):
    tok_count, width = key_seq.shape
    head_dim = feature_map.shape[0]
    size = width // (4 * GROUPS)
    count = len(quarters)
    rows, firsts = shape((tok_count, count * size), bf16), shape((RIM, count * size), bf16)
    return kernel_call(
        functools.partial(near_states_kernel, group, quarters),
        "near_states",
        [IN_VMEM] * 4,
        [IN_VMEM] * (4 + count),
        [rows, rows, firsts, firsts, *[shape((size, head_dim), state_type)] * count],
        [pltpu.VMEM((BLOCK_HEADS, 2, TILE + tok_count, head_dim), f32)],
    )(key_seq, value_seq, conv_kernel, feature_map)


def whole_states_kernel(
    group, quarters, key_ref, value_ref, taps_ref, map_ref, core_rim, chip_rim, feat_ref, conv_ref, *rest
):
    (*states, scratch) = rest
    head_dim = map_ref.shape[0]
    width = key_ref.shape[1]
    size = width // (4 * GROUPS)
    back = taps_ref.shape[1] - 1
    for i, quarter in enumerate(quarters):
        for start in range(0, size, head_dim):
            natural = columns(quarter_start(quarter, width) + group * size + start, head_dim)
            at = i * size + start
            local = slice(at, at + head_dim)
            buffers = scratch.at[at // head_dim % scratch.shape[0]]
            taps = taps_ref[:, :, natural].astype(f32)
            rim = state_rim(core_rim, chip_rim, quarter, width, group * size + start, head_dim)
            key_conv = convolved(buffers.at[0], key_ref[:, natural].astype(f32), taps[1], rim, back)
            key_feat = features(key_conv, map_ref[...])
            feat_ref[:, local] = key_feat
            value_conv = convolved(buffers.at[1], value_ref[:, natural].astype(f32), taps[2], rim, 2 * back)
            conv_ref[:, local] = value_conv
            states[i][start : start + head_dim] = state_of(key_feat, value_conv).astype(states[i].dtype)


def whole_states(group, quarters, state_type, key_seq, value_seq, conv_kernel, feature_map, rims):
    tok_count, width = key_seq.shape
    head_dim = feature_map.shape[0]
    size = width // (4 * GROUPS)
    rows = shape((tok_count, len(quarters) * size), bf16)
    return kernel_call(
        functools.partial(whole_states_kernel, group, quarters),
        "whole_states",
        [IN_VMEM] * 6,
        [IN_VMEM] * (2 + len(quarters)),
        [rows, rows, *[shape((size, head_dim), state_type)] * len(quarters)],
        [pltpu.VMEM((BLOCK_HEADS, 2, TILE + tok_count, head_dim), f32)],
    )(key_seq, value_seq, conv_kernel, feature_map, *rims)


def first_rows_kernel(
    group, quarters, key_ref, value_ref, taps_ref, map_ref, core_rim, chip_rim, *rest
):
    (*state_refs, feat_ref, conv_ref, scratch) = rest
    head_dim = map_ref.shape[0]
    width = taps_ref.shape[2]
    back = taps_ref.shape[1] - 1
    size = width // (4 * GROUPS)
    for i, quarter in enumerate(quarters):
        here = there = slice(i * size, (i + 1) * size)
        natural = columns(quarter_start(quarter, width) + group * size, size)
        rim = state_rim(core_rim, chip_rim, quarter, width, group * size, size)
        conv = convolved(
            scratch.at[i, 0], key_ref[:, there].astype(f32), taps_ref[1, :, natural].astype(f32), rim, back
        )
        value_conv = convolved(
            scratch.at[i, 1], value_ref[:, there].astype(f32), taps_ref[2, :, natural].astype(f32), rim, 2 * back
        )
        feats = [features(conv[:, at : at + head_dim], map_ref[...]) for at in range(0, size, head_dim)]
        feat = jnp.concatenate(feats, axis=1)
        feat_ref[:, here], conv_ref[:, here] = feat, value_conv
        if state_refs:
            old_refs, new_refs = state_refs[: len(quarters)], state_refs[len(quarters) :]
            new_refs[i][...] = old_refs[i][...] + first_states(feat, value_conv, head_dim, back)


def first_states(feat, value_conv, head_dim, back):
    row = lax.broadcasted_iota(jnp.int32, (RIM, head_dim), 0)
    states = []
    for at in range(0, feat.shape[1], head_dim):
        first = jnp.where(row < back, feat[:, at : at + head_dim].astype(f32), 0.0).astype(bf16)
        states.append(state_of(first, value_conv[:, at : at + head_dim]))
    return jnp.concatenate(states, axis=0)


def first_rows(group, quarters, key_first, value_first, conv_kernel, feature_map, rims, before=()):
    width = conv_kernel.shape[2]
    head_dim = feature_map.shape[0]
    size = width // (4 * GROUPS)
    rows = shape((RIM, len(quarters) * size), bf16)
    more = [shape((size, head_dim), f32)] * len(before) if before else [rows]
    operands = [key_first, value_first, conv_kernel, feature_map, *rims, *before]
    body = functools.partial(first_rows_kernel, group, quarters)

    def reordered(*refs):
        sources, (feat_ref, conv_ref, *more, scratch) = refs[:6], refs[len(operands) :]
        if before:
            body(*sources, *refs[6 : len(operands)], *more, feat_ref, conv_ref, scratch)
        else:
            body(*sources, feat_ref, conv_ref, scratch)
            tiles = [ref[...].astype(f32)[:TILE] for ref in (feat_ref, conv_ref)]
            more[0][...] = jnp.concatenate(tiles, axis=0).astype(bf16)

    return kernel_call(
        reordered,
        "first_rows",
        [IN_VMEM] * len(operands),
        [IN_VMEM] * (2 + len(more)),
        [rows, rows, *more],
        [pltpu.VMEM((len(quarters), 2, TILE + RIM, size), f32)],
    )(*operands)


def within_kernel(
    quarter, group, base, query_ref, taps_ref, map_ref, core_rim, chip_rim, key_ref, value_ref, *rest
):
    (*firsts, feat_ref, mixed_ref, scratch) = rest
    head_dim = map_ref.shape[0]
    tok_count, width = query_ref.shape
    size = width // (4 * GROUPS)
    causal = lax.broadcasted_iota(jnp.int32, (tok_count, tok_count), 0) >= lax.broadcasted_iota(
        jnp.int32, (tok_count, tok_count), 1
    )
    starts = range(0, size, head_dim)
    for start in starts:
        natural = columns(quarter_start(quarter, width) + group * size + start, head_dim)
        rim, end = query_rim(core_rim, chip_rim, quarter, width, group * size + start, head_dim)
        taps = taps_ref[0, :, natural].astype(f32)
        buffer = scratch.at[start // head_dim % scratch.shape[0]]
        conv = convolved(buffer, query_ref[:, natural].astype(f32), taps, rim, end * (taps_ref.shape[1] - 1))
        feat_ref[:, start : start + head_dim] = features(conv, map_ref[...])
    products = []
    for start in starts:
        local, at = slice(start, start + head_dim), slice(base + start, base + start + head_dim)
        first = quarter % 2 * size + start
        first = slice(first, first + head_dim)
        key, value = key_ref[:, at], value_ref[:, at]
        if firsts:
            key = jnp.concatenate([firsts[0][:, first], key[RIM:]], axis=0)
            value = jnp.concatenate([firsts[1][:, first], value[RIM:]], axis=0)
        scores = lax.dot_general(feat_ref[:, local], key, (((1,), (1,)), ((), ())), preferred_element_type=f32)
        products.append((local, jnp.where(causal, scores, 0.0).astype(bf16), value))
    for local, weights, value in products:
        mixed_ref[:, local] = jnp.dot(weights, value, preferred_element_type=f32)


def within_block(quarter, group, query_seq, conv_kernel, feature_map, rims, feat, conv, base, firsts):
    tok_count, width = query_seq.shape
    head_dim = feature_map.shape[0]
    size = width // (4 * GROUPS)
    operands = (query_seq, conv_kernel, feature_map, *rims, feat, conv, *firsts)
    return kernel_call(
        functools.partial(within_kernel, quarter, group, base),
        "within_block",
        [IN_VMEM] * len(operands),
        [IN_VMEM] * 2,
        [shape((tok_count, size), bf16), shape((tok_count, size), f32)],
        [pltpu.VMEM((BLOCK_HEADS, TILE + tok_count, head_dim), f32)],
    )(*operands)


def finish_kernel(pieces, before, gain_ref, *rest):
    count = sum(len(part) for part in pieces)
    prefixes, rest = rest[: len(pieces)], rest[len(pieces) :]
    feats, mixes = rest[:count], rest[count : 2 * count]
    out_ref, *token, rows, sems = rest[2 * count + before :]
    for ref in token:
        ref[...] = jnp.zeros(ref.shape, f32)
    head_dim = prefixes[0].shape[1]
    tok_count, size = feats[0].shape
    step = size // 2 if size % (2 * head_dim) == 0 else size
    i, copies = 0, []
    for prefix_ref, part in zip(prefixes, pieces):
        for at, (quarter, group) in enumerate(part):
            natural = quarter_start(quarter, out_ref.shape[1]) + group * size
            for start in range(0, size, head_dim):
                cols = slice(start, start + head_dim)
                prefix = prefix_ref[at * size + start : at * size + start + head_dim]
                mixed = mixes[i][:, cols] + jnp.dot(feats[i][:, cols], prefix, preferred_element_type=f32)
                inverse_rms = lax.rsqrt(jnp.mean(mixed * mixed, axis=-1, keepdims=True) + 1e-06)
                gain = gain_ref[:, columns(natural + start, head_dim)]
                rows[i, :, cols] = (mixed * inverse_rms * gain).astype(bf16)
                if (start + head_dim) % step == 0:
                    part_cols = pl.ds(start + head_dim - step, step)
                    there = columns(natural + start + head_dim - step, step)
                    copies.append(
                        pltpu.make_async_copy(rows.at[i, :, part_cols], out_ref.at[:, there], sems.at[len(copies)])
                    )
                    copies[-1].start()
            i += 1
    for copy in copies:
        copy.wait()


def finish(pieces, mixed, prefixes, norm_gain, before, last=False):
    width = norm_gain.shape[1]
    every = [piece for part in pieces for piece in part]
    count = len(every)
    tok_count, size = mixed[every[0]][0].shape
    operands = [norm_gain, *prefixes, *(mixed[p][0] for p in every), *(mixed[p][1] for p in every)]
    in_specs = [IN_VMEM] * len(operands)
    aliases = {}
    if before is not None:
        aliases = {len(operands): 0}
        operands.append(in_hbm(before))
        in_specs.append(IN_PLACE)
    return kernel_call(
        functools.partial(finish_kernel, pieces, len(aliases)),
        "finish",
        in_specs,
        [IN_PLACE, IN_VMEM][: 1 if last else 2],
        [pltpu.HBM((tok_count, width), bf16), shape((TILE, 128), f32)][: 1 if last else 2],
        [pltpu.VMEM((count, tok_count, size), bf16), pltpu.SemaphoreType.DMA((2 * count,))],
        aliases,
    )(*operands)[0]


def swapped(block, distance):
    return lax.ppermute(block, "seq", [(i, i ^ distance) for i in range(lax.axis_size("seq"))])


def passed_on(block):
    count = lax.axis_size("seq")
    route = {i: i + 1 for i in range(1, count - 2, 2)}
    route |= {i: i - 1 for i in range(4, count - 3, 2)}
    route |= {0: 1, 2: 0, count - 2: count - 1, count - 1: count - 3}
    return lax.ppermute(block, "seq", sorted(route.items()))


def mapped(name, function, outputs, *arrays):
    def body(*refs):
        values = [ref[...] for ref in refs[: len(arrays)]]
        for ref, value in zip(refs[len(arrays) :], function(lax.axis_index("seq"), *values)):
            ref[...] = value.astype(ref.dtype)

    columns = arrays[0].shape[1]
    return kernel_call(
        body,
        name,
        [IN_VMEM] * len(arrays),
        [IN_VMEM] * len(outputs),
        [shape((rows, columns), kind) for rows, kind in outputs],
    )(*arrays)


def on_device(query_seq, key_seq, value_seq, conv_kernel, feature_map, norm_gain):
    tok_count, width = query_seq.shape
    tap_count = conv_kernel.shape[1]
    head_dim = feature_map.shape[0]
    device_count = lax.axis_size("seq")
    assert tok_count == SPAN and width % (4 * GROUPS * head_dim) == 0
    assert device_count >= 8 and device_count & (device_count - 1) == 0
    groups = range(GROUPS)
    rows = width // (4 * GROUPS)
    gain = norm_gain.reshape(1, width)

    def of_core(device):
        return (device & 1) != 0

    def of_pair(device):
        return (device & 2) != 0

    Turn.last = ()
    packed = pack_rims(query_seq, key_seq, value_seq, tap_count, head_dim)
    rims = (swapped(packed, 1), passed_on(packed))
    mixed = {}
    fill = [(q, g) for q in (3, 2, 1, 0) for g in groups]
    total = len(fill)

    def score(share):
        while fill and total - len(fill) < round(share * total):
            q, g = fill.pop(0)
            first = ()
            if firsts[g]:
                first = firsts[g][q // 2]
            mixed[q, g] = within_block(q, g, query_seq, conv_kernel, feature_map, rims, *near[g][q], first)

    def chip_sums(device, paired, own, *arrived):
        states, firsts = [part.astype(f32) for part in arrived[:2]], arrived[2:]
        for first in firsts:
            first = first.astype(f32)
            blank = jnp.zeros((TILE, first.shape[1]), f32)
            first = [jnp.concatenate([part, blank], axis=0).astype(bf16) for part in (first[:TILE], first[TILE:])]
            more = first_states(*first, head_dim, tap_count - 1)
            states = [states[0] + more[:rows], states[1] + more[rows:]]
        return paired + states[0], own + states[1], *states

    def pair_sums(device, own, arrived):
        total = own + arrived.astype(f32)
        return total, total

    def plane_sums(distance, device, total, *arrived):
        before, arrived = (0.0, arrived) if distance == 4 else (arrived[0], arrived[1:])
        upper = (device & distance) != 0
        if len(arrived) == 2:
            odd = (device & (distance // 2)) != 0
            mine, other = arrived
            arrived = (jnp.concatenate([jnp.where(odd, other, mine), jnp.where(odd, mine, other)], axis=0),)
        arrived = arrived[0].astype(f32)
        before = before + jnp.where(upper, arrived, 0.0)
        total = total + arrived
        give = total.astype(bf16)
        return total, before, jnp.where(upper, give[rows // 2 :], give[: rows // 2])

    def back_prefixes(distance, device, own, *step):
        before = plane_sums(distance, device, *step)[1] if step else jnp.zeros((rows, head_dim), f32)
        return before, before + jnp.where(of_pair(device), 0.0, own)

    def own_prefixes(device, before, paired, cored, state):
        before = before + jnp.where(of_pair(device), paired.astype(f32), 0.0)
        return (
            before + jnp.where(of_core(device), cored.astype(f32), 0.0),
            before + jnp.where(of_core(device), 0.0, state),
        )

    def paired_prefixes(device, arrived, cored, state, own):
        arrived = arrived.astype(f32)
        give = arrived + jnp.where(of_core(device), 0.0, state)
        return (
            arrived + jnp.where(of_core(device), cored.astype(f32), 0.0),
            jnp.concatenate([give.astype(bf16), own], axis=0),
        )

    near, firsts, state_b, from_core, chip, arriving = [], [], [], [], [], []
    running, earlier, from_pair = [None] * GROUPS, [None] * GROUPS, [None] * GROUPS
    distance = 4

    def pair_step(g):
        from_pair[g] = arriving[g]
        if distance < device_count:
            running[g], give = mapped("pair_sums", pair_sums, [(rows, f32), (rows, bf16)], chip[g], from_pair[g])
            arriving[g] = (swapped(give, distance),)

    for g in groups:
        if g == 0:
            near.append([])
            *kept, key_first, value_first, other, other_next = near_states(
                g, (0, 1), bf16, key_seq, value_seq, conv_kernel, feature_map
            )
            near[g] += [(*kept, q * rows) for q in range(2)]
            others = [swapped(other, 1), swapped(other_next, 1)]
            *kept, key_next, value_next, paired, single = near_states(
                g, (2, 3), f32, key_seq, value_seq, conv_kernel, feature_map
            )
            near[g] += [(*kept, q * rows) for q in range(2)]
            *first_a, first_tiles = first_rows(g, (0, 1), key_first, value_first, conv_kernel, feature_map, rims)
            others.append(swapped(first_tiles, 1))
            *first_b, paired, single = first_rows(
                g, (2, 3), key_next, value_next, conv_kernel, feature_map, rims, (paired, single)
            )
            firsts.append((first_a, first_b))
        else:
            *kept, other, other_next = whole_states(
                g, (0, 1), bf16, key_seq, value_seq, conv_kernel, feature_map, rims
            )
            others = [swapped(other, 1), swapped(other_next, 1)]
            near.append([(*kept, q * rows) for q in range(2)])
            *kept, paired, single = whole_states(
                g, (2, 3), f32, key_seq, value_seq, conv_kernel, feature_map, rims
            )
            near[g] += [(*kept, q * rows) for q in range(2)]
            firsts.append(None)
            pair_step(g - 1)
        state_b.append((paired, single))
        give, own, *others = mapped(
            "chip_sums", chip_sums, [(rows, bf16), (rows, f32), (rows, f32), (rows, f32)], paired, single, *others
        )
        from_core.append(others)
        chip.append(own)
        arriving.append(swapped(give, 2))
    score(0.375)
    pair_step(GROUPS - 1)
    while 2 * distance < device_count:
        for g in groups:
            before = [] if distance == 4 else [earlier[g]]
            running[g], earlier[g], give = mapped(
                "plane_sums",
                functools.partial(plane_sums, distance),
                [(rows, f32), (rows, f32), (rows // 2, bf16)],
                running[g],
                *before,
                *arriving[g],
            )
            arriving[g] = swapped(give, 2 * distance)
            if g == 0:
                score(0.5)
        for g in groups:
            (mine,) = mapped("halves", lambda device, half: (half,), [(rows // 2, bf16)], arriving[g])
            arriving[g] = (mine, swapped(mine, distance))
            if g == 0:
                score(0.75)
        distance *= 2

    back, own_give = [None] * GROUPS, [None] * GROUPS
    owns = []
    for g in groups:
        step = ()
        if distance < device_count:
            step = (running[g], *([] if distance == 4 else [earlier[g]]), *arriving[g])
        before, give = mapped(
            "back_prefixes",
            functools.partial(back_prefixes, distance),
            [(rows, f32), (rows, bf16)],
            chip[g],
            *step,
        )
        back[g] = swapped(give, 2)
        own, own_give[g] = mapped(
            "own_prefixes",
            own_prefixes,
            [(rows, bf16)] * 2,
            before,
            from_pair[g],
            from_core[g][1],
            state_b[g][1],
        )
        owns.append(own)
        score(0.75 + (1 - 0.75) * (g + 1) / GROUPS)
    out = finish([[(3, g)] for g in groups], mixed, owns, gain, None)
    from_other = [None] * GROUPS
    for g in groups:
        prefix_2, give = mapped(
            "paired_prefixes",
            paired_prefixes,
            [(rows, bf16), (2 * rows, bf16)],
            back[g],
            from_core[g][0],
            state_b[g][0],
            own_give[g],
        )
        from_other[g] = swapped(give, 1)
        if g == 0:
            out = finish([[(2, g)]], mixed, [prefix_2], gain, out)
        else:
            pieces = [[(2, g)], [(0, g - 1), (1, g - 1)]]
            out = finish(pieces, mixed, [prefix_2, from_other[g - 1]], gain, out)
    return finish([[(0, g), (1, g)]], mixed, [from_other[g]], gain, out, last=True)


def solution(mesh):
    return jax.shard_map(
        on_device,
        mesh=mesh,
        in_specs=(
            P(("groups", "seq"), None),
            P(("groups", "seq"), None),
            P(("groups", "seq"), None),
            P(),
            P(),
            P(),
        ),
        out_specs=P(("groups", "seq"), None),
        check_vma=False,
    )
```
